32 devices in a mesh: fsdp: 8 (over y, x, core), tp: 4 (over z).
Axes of the slice: x: 2, y: 2, z: 4, core: 2. Of those that a mesh axis runs over, the one named last changes fastest.
Arguments:
- activations: bfloat16 [16384, 5120], P(('fsdp', 'tp')), may hold values from -6 to 6
- grad_out: bfloat16 [16384, 1024], P(('fsdp', 'tp')), may hold values from -6 to 6
- master_w: float32 [5120, 1024], P(('fsdp', 'tp')), may hold values from -0.078125 to 0.078125
- embed_table: bfloat16 [151936, 5120], P(('fsdp', 'tp')), may hold values from -6 to 6
- token_ids: int32 [64], replicated, may hold values from 0 to 151935
- queries: bfloat16 [64, 8192], P('fsdp', 'tp'), may hold values from -30 to 30
- cache_keys: bfloat16 [64, 512, 1024], P('fsdp', None, 'tp'), may hold values from -6 to 6
- cache_values: bfloat16 [64, 512, 1024], P('fsdp', None, 'tp'), may hold values from -6 to 6
- new_key: bfloat16 [64, 1024], P('fsdp', 'tp'), may hold values from -6 to 6
- first_value: bfloat16 [64, 1024], P('fsdp', 'tp'), may hold values from -6 to 6
- residual_mix: float32 [8], P('tp'), may hold values from 0.2 to 0.8
- lengths: int32 [64], P('fsdp'), may hold values from 1 to 512, 16384 in all
Outputs:
- w_next: float32 [5120, 1024], P(('fsdp', 'tp'))
- new_value: bfloat16 [64, 1024], P('fsdp', 'tp')
- attended: bfloat16 [64, 8192], P('fsdp', 'tp')
The draws below stay inside these ranges and needn't reach their ends.
Inputs may be any that keep to these rules, and one draw needn't show every extreme that they name: `lengths`: some row holds exactly 512 positions.
All inputs are finite; a program needn't handle non-finite values. No bound on the sum of `lengths` on one device may be relied on, other than what follows from the above.
Results may differ from the reference program's by a relative error of at most 0.006.
Values may be sent and summed in bfloat16 or wider, within the bound.
No kernel may reach another device: no remote copies, remote signals or barrier semaphores. Data moves between devices by JAX's collectives and lax.ppermute only.
A program may use at most 128 MiB of HBM per device.

```python
import math
import jax
import jax.numpy as jnp
import numpy as np
from jax import lax

D = 5120
HEADS = 64
KV = 8
HD = 128
VOCAB = 151936
TOK_DEV = 512
CTX = 512
KVD = 1024
TOKENS = 16384
ROWS_ALL = 64
DEVICES = 32


def draw_queries(key, part):
    key = jax.random.fold_in(key, 1)
    group = HEADS // KV
    values = jnp.clip(jax.random.normal(key, (ROWS_ALL, KV, group, HD), jnp.float32), -6.0, 6.0)
    return values.reshape(ROWS_ALL, HEADS * HD).astype(jnp.bfloat16)


def draw_cache_keys(key, part):
    key = jax.random.fold_in(key, 2)
    values = jnp.clip(jax.random.normal(key, (ROWS_ALL, CTX, KV, HD), jnp.float32), -6.0, 6.0)
    return values.reshape(ROWS_ALL, CTX, KVD).astype(jnp.bfloat16)


def draw_token_ids(key, part):
    key = jax.random.fold_in(key, 3)
    per_device = ROWS_ALL // DEVICES
    slice_len = VOCAB // DEVICES
    positions = jnp.arange(ROWS_ALL, dtype=jnp.int32)
    home = positions // per_device
    kinds = jax.random.randint(jax.random.fold_in(key, 21), (ROWS_ALL,), 0, 3)
    anywhere = jax.random.randint(jax.random.fold_in(key, 22), (ROWS_ALL,), 0, DEVICES)
    offset = jnp.where(kinds == 0, 1, jnp.where(kinds == 1, DEVICES // 2, anywhere))
    offset = jnp.where(positions % per_device == 0, offset, anywhere)
    owner = (home + offset) % DEVICES
    inside = jax.random.randint(jax.random.fold_in(key, 23), (ROWS_ALL,), 0, slice_len)
    return (owner * slice_len + inside).astype(jnp.int32)


def with_spikes(entries, rng, source, target, shards_of, factor):
    def block_of(dim):
        return (jnp.arange(entries.shape[dim]) // (entries.shape[dim] // shards_of)).reshape((-1,) + (1,) * (entries.ndim - 1 - dim))

    first = jax.random.permutation(rng, shards_of)[block_of(target)]
    far = (block_of(target) + shards_of // 2) % shards_of
    return jnp.where((block_of(source) == first) | (block_of(source) == far), factor * entries, entries)


def level_of(stream_key, shape, split, low, high):
    def one(position, blocks):
        heights = jax.random.uniform(jax.random.fold_in(jax.random.fold_in(stream_key, 6), position), (blocks,), jnp.float32, low / len(split), high / len(split))
        return jnp.repeat(jnp.exp(heights), shape[position] // blocks).reshape((-1,) + (1,) * (len(shape) - position - 1))

    level = one(*split[0])
    for cut in split[1:]:
        level = level * one(*cut)
    return level


def length_profile(count, total, most, lean):
    portions = [(1 << 20) // math.isqrt(grade ** lean) + 1 for grade in range(2, count + 1)]
    surplus, holding = total - most - (count - 1), [1] * (count - 1)
    while surplus > 0:
        free = [i for i in range(count - 1) if holding[i] < most]
        mass, remaining = sum([portions[i] for i in free]), surplus
        for i in free:
            extra = min(most - holding[i], max(1, remaining * portions[i] // mass), surplus)
            holding[i] = holding[i] + extra
            surplus = surplus - extra
    return np.array([most] + holding)


def uneven(own_key, amount, total, bound, lean):
    if amount == 2:
        one = jax.random.randint(own_key, (), max(1, total - bound), min(bound, total - 1) + 1)
        return jnp.stack([one, total - one])
    sizes = jnp.asarray(length_profile(amount, total, bound, lean), jnp.int32)
    couples = (amount - 1) // 2
    giver, sink = sizes[1:1 + 2 * couples:2], sizes[2:2 + 2 * couples:2]
    margin = jnp.minimum(giver - 1, bound - sink)
    shifted = jax.random.randint(jax.random.fold_in(own_key, 1), (couples,), 0, 1 << 20) % (margin + 1)
    sizes = sizes.at[1:1 + 2 * couples:2].set(giver - shifted).at[2:2 + 2 * couples:2].set(sink + shifted)
    return sizes[jax.random.permutation(jax.random.fold_in(own_key, 2), amount)]


def centred(key, extent, deviation, bound, split=(), kind=jnp.bfloat16):
    array = jax.random.normal(key, extent, jnp.float32) * deviation
    if len(split) > 0:
        array = level_of(key, extent, split, -0.22, 0.18) * array
    return jnp.clip(array, min=-bound, max=bound).astype(kind)


def gaussian_with(stream_key, extent, width, reach, cuts, heavy, held_as=jnp.bfloat16):
    values = width * jax.random.normal(stream_key, extent, jnp.float32)
    if cuts:
        values = values * level_of(stream_key, extent, cuts, -0.22, 0.18)
    return jnp.clip(with_spikes(values, jax.random.fold_in(stream_key, 3), *heavy), -reach, reach).astype(held_as)


def setup_inputs(seed: int = 0) -> dict:
    streams_of = jax.random.split(jax.random.key(seed), 13)
    return {
        "activations": gaussian_with(streams_of[0], (TOKENS, D), 1.0, 6.0, ((0, 32),), (0, 1, 32, 2.75)),
        "grad_out": centred(streams_of[1], (TOKENS, KVD), 1.0, 6.0, ((0, 32),)),
        "master_w": centred(streams_of[2], (D, KVD), D ** -0.5, 0.078125, ((0, 32),), jnp.float32),
        "embed_table": centred(streams_of[3], (VOCAB, D), 1.0, 6.0, ((0, 32),)),
        "token_ids": draw_token_ids(jax.random.fold_in(streams_of[12], 71), 0),
        "queries": draw_queries(jax.random.fold_in(streams_of[12], 71), 0),
        "cache_keys": draw_cache_keys(jax.random.fold_in(streams_of[12], 71), 0),
        "cache_values": centred(streams_of[7], (ROWS_ALL, CTX, KVD), 1.0, 6.0, ((0, 8), (2, 4))),
        "new_key": centred(streams_of[8], (ROWS_ALL, KVD), 1.0, 6.0, ((0, 8), (1, 4))),
        "first_value": centred(streams_of[9], (ROWS_ALL, KVD), 1.0, 6.0, ((0, 8), (1, 4))),
        "residual_mix": jnp.clip(0.2 + 0.6 * jax.random.uniform(streams_of[10], (KV,), jnp.float32) ** level_of(streams_of[10], (KV,), ((0, 4),), -0.2, 0.2), 0.2, 0.8),
        "lengths": uneven(streams_of[11], ROWS_ALL, ROWS_ALL * CTX // 2, CTX, 0).astype(jnp.int32),
    }


def reference(activations, grad_out, master_w, embed_table, token_ids, queries, cache_keys, cache_values, new_key, first_value, residual_mix, lengths):
    blocks_a = activations.reshape(DEVICES, TOK_DEV, D)
    blocks_g = grad_out.reshape(DEVICES, TOK_DEV, KVD)

    def accumulate(total, pair):
        left = pair[0].astype(jnp.float32)
        right = pair[1].astype(jnp.float32)
        return (total + jnp.dot(left.T, right), None)
    grad_w, _ = lax.scan(accumulate, jnp.zeros((D, KVD), jnp.float32), (blocks_a, blocks_g))
    coef = 1.0 / math.sqrt(TOKENS * D)
    w_next = master_w - coef * grad_w
    w_roll = w_next.astype(jnp.bfloat16)
    embedded = embed_table[token_ids]
    own_value = jnp.dot(embedded, w_roll, preferred_element_type=jnp.float32)
    share = jnp.repeat(residual_mix, HD)[None, :]
    new_value = (share * own_value + (1.0 - share) * first_value.astype(jnp.float32)).astype(jnp.bfloat16)
    group = HEADS // KV
    scale = 1.0 / math.sqrt(HD)
    query_f = queries.astype(jnp.float32).reshape(ROWS_ALL, KV, group, HD)
    keys_f = cache_keys.astype(jnp.float32).reshape(ROWS_ALL, CTX, KV, HD)
    vals_f = cache_values.astype(jnp.float32).reshape(ROWS_ALL, CTX, KV, HD)
    newk_f = new_key.astype(jnp.float32).reshape(ROWS_ALL, KV, HD)
    newv_f = new_value.astype(jnp.float32).reshape(ROWS_ALL, KV, HD)
    scores = jnp.einsum('rkgd,rckd->rkgc', query_f, keys_f) * scale
    fresh = jnp.einsum('rkgd,rkd->rkg', query_f, newk_f) * scale
    valid = jnp.arange(CTX, dtype=jnp.int32)[None, :] < lengths[:, None]
    scores = jnp.where(valid[:, None, None, :], scores, -1e+30)
    peak = jnp.maximum(lax.optimization_barrier(jnp.max(scores, axis=-1)), fresh)
    expo = jnp.exp(scores - peak[..., None])
    expo_new = jnp.exp(fresh - peak)
    total = lax.optimization_barrier(jnp.sum(expo, axis=-1)) + expo_new
    probs = (expo / total[..., None]).astype(jnp.bfloat16)
    probs_new = (expo_new / total).astype(jnp.bfloat16)
    mixed = jnp.einsum('rkgc,rckd->rkgd', probs.astype(jnp.float32), vals_f)
    mixed = mixed + probs_new.astype(jnp.float32)[..., None] * newv_f[:, :, None, :]
    attended = mixed.reshape(ROWS_ALL, HEADS * HD).astype(jnp.bfloat16)
    return (w_next, new_value, attended)
```

```python
import math

import jax
import jax.numpy as jnp
from jax import lax
from jax.experimental import pallas as pl
from jax.experimental.pallas import tpu as pltpu
from jax.sharding import PartitionSpec as P

HEADS = 64
KV = 8
HD = 128
LANES = 128
SLAB = 16


def exchange(value, axis, mask):
    return lax.ppermute(value, axis, [(i, i ^ mask) for i in range(lax.axis_size(axis))])


def transpose_block(order, block, out):
    out[...] = block[...].T


def pack(activations, order, width):
    tokens = activations.shape[0]
    count = len(order)
    if width % LANES:
        flipped = activations.T
        return jnp.concatenate(
            [lax.dynamic_slice_in_dim(flipped, place * width, width, 0) for place in order]
        )
    return pl.pallas_call(
        transpose_block,
        grid_spec=pltpu.PrefetchScalarGridSpec(
            num_scalar_prefetch=1,
            grid=(count,),
            in_specs=[pl.BlockSpec((tokens, width), lambda j, order: (0, order[j]))],
            out_specs=pl.BlockSpec((width, tokens), lambda j, order: (j, 0)),
        ),
        out_shape=jax.ShapeDtypeStruct((count * width, tokens), activations.dtype),
        compiler_params=pltpu.CompilerParams(vmem_limit_bytes=32 << 20),
        cost_estimate=pl.CostEstimate(
            flops=0, bytes_accessed=4 * count * width * tokens, transcendentals=0
        ),
    )(jnp.stack(order).astype(jnp.int32), activations)


def pick_rows(place, *refs):
    slabs, out, held = refs[:SLAB], refs[SLAB], refs[SLAB + 1]
    held[...] = jnp.zeros_like(held)
    for k in range(SLAB):
        inside = place[pl.program_id(0) * SLAB + k]

        @pl.when(inside >= 0)
        def _():
            rows = slabs[k][...].astype(jnp.float32)
            at = lax.broadcasted_iota(jnp.int32, rows.shape, 0)
            chosen = jnp.where(at == lax.rem(inside, SLAB), rows, 0.0)
            held[k : k + 1, :] = jnp.sum(chosen, axis=0, keepdims=True)

    out[...] = held[...].astype(out.dtype)


def lookup(embed_table, token_ids, start):
    here, width = embed_table.shape
    count = token_ids.shape[0]
    inside = token_ids - start
    place = jnp.where((inside >= 0) & (inside < here), inside, -1)

    def slab_of(k):
        return lambda i, place: (jnp.maximum(place[i * SLAB + k], 0) // SLAB, 0)

    return pl.pallas_call(
        pick_rows,
        grid_spec=pltpu.PrefetchScalarGridSpec(
            num_scalar_prefetch=1,
            grid=(count // SLAB,),
            in_specs=[pl.BlockSpec((SLAB, width), slab_of(k)) for k in range(SLAB)],
            out_specs=pl.BlockSpec((SLAB, width), lambda i, place: (i, 0)),
            scratch_shapes=[pltpu.VMEM((SLAB, width), jnp.float32)],
        ),
        out_shape=jax.ShapeDtypeStruct((count, width), embed_table.dtype),
        compiler_params=pltpu.CompilerParams(vmem_limit_bytes=32 << 20),
        cost_estimate=pl.CostEstimate(
            flops=0, bytes_accessed=2 * count * SLAB * width, transcendentals=0
        ),
    )(place.astype(jnp.int32), *([embed_table] * SLAB))


def dot32(left, right):
    return jnp.dot(left, right, preferred_element_type=jnp.float32)


def per_device(
    activations,
    grad_out,
    master_w,
    embed_table,
    token_ids,
    queries,
    cache_keys,
    cache_values,
    new_key,
    first_value,
    residual_mix,
    lengths,
):
    count_fsdp = lax.axis_size("fsdp")
    count_tp = lax.axis_size("tp")
    devices_all = count_fsdp * count_tp
    width = activations.shape[1]
    tokens_total = activations.shape[0] * devices_all
    coef = 1.0 / math.sqrt(tokens_total * width)
    f = lax.axis_index("fsdp")
    t = lax.axis_index("tp")
    core = f & 1
    upper = f >> 1
    upper_bits = count_fsdp.bit_length() - 2
    uppers = 1 << upper_bits

    block = width // count_fsdp
    arranged = [r ^ (r >> 1) for r in range(uppers)][::-1]
    grads = [grad_out, exchange(grad_out, "fsdp", 1)]
    outgoing = pack(activations, [((r ^ upper) << 1) | (1 - core) for r in arranged], block)
    incoming = exchange(outgoing, "fsdp", 1)
    staying = pack(activations, [((r ^ upper) << 1) | core for r in arranged], block)
    lefts = [staying, incoming]

    def partial(wanted, first, last):
        places = [arranged.index(r) for r in wanted]
        runs = []
        for place in places:
            if runs and runs[-1][1] == place:
                runs[-1][1] = place + 1
            else:
                runs.append([place, place + 1])
        return [
            sum(
                dot32(left[low * block : high * block], grad[:, first:last])
                for left, grad in zip(lefts, grads)
            )
            for low, high in runs
        ]

    columns = master_w.shape[1]
    rows = master_w.shape[0]
    quarter = columns // 4
    eighth = columns // 8
    sizes = [quarter, quarter, eighth, eighth, eighth, eighth]
    chunks = []
    first = 0
    for index, size in enumerate(sizes):
        order = list(range(upper_bits))
        chunks.append((first, first + size, order if index % 2 == 0 else order[::-1]))
        first += size

    def reduce_chunk(first, last, order):
        arrived = {r: [] for r in range(uppers)}
        remaining = list(arranged)
        for bit in order:
            sent = [r for r in remaining if (r >> bit) & 1]
            remaining = [r for r in remaining if not (r >> bit) & 1]
            value = jnp.concatenate(partial(sent, first, last))
            for step in range(len(arrived[sent[0]])):
                value = value + jnp.concatenate([arrived[r][step] for r in sent]).astype(
                    jnp.float32
                )
            got = exchange(value.astype(jnp.bfloat16), "fsdp", 2 << bit)
            for at, r in enumerate(sent):
                arrived[r ^ (1 << bit)].append(got[at * block : (at + 1) * block])
        total = jnp.concatenate(partial([0], first, last))
        for piece in arrived[0]:
            total = total + piece.astype(jnp.float32)
        grad = lax.dynamic_slice_in_dim(total, t * rows, rows, 0)
        for step in range(1, count_tp):
            away = lax.dynamic_slice_in_dim(total, (t ^ step) * rows, rows, 0)
            grad = grad + exchange(away.astype(jnp.bfloat16), "tp", step).astype(jnp.float32)
        return master_w[:, first:last] - coef * grad

    w_next = jnp.concatenate([reduce_chunk(*chunk) for chunk in chunks], axis=1)

    tokens_new = token_ids.shape[0]
    half = tokens_new // 2
    piece = half // count_tp
    flat = f * count_tp + t
    found = lookup(embed_table, token_ids, flat * embed_table.shape[0])
    held = lax.dynamic_slice_in_dim(found, core * half, half, 0) + exchange(
        lax.dynamic_slice_in_dim(found, (1 - core) * half, half, 0), "fsdp", 1
    )
    mine = lax.dynamic_slice_in_dim(held, t * piece, piece, 0)
    for step in range(1, count_tp):
        mine = mine + exchange(
            lax.dynamic_slice_in_dim(held, (t ^ step) * piece, piece, 0), "tp", step
        )
    for bit in range(1, upper_bits + 1):
        mine = mine + exchange(mine, "fsdp", 1 << bit)
    near = jnp.concatenate([mine] + [exchange(mine, "tp", step) for step in range(1, count_tp)])
    embedded = jnp.concatenate([near, exchange(near, "fsdp", 1)])

    through = lax.dot_general(
        embedded, activations, (((1,), (1,)), ((), ())), preferred_element_type=jnp.float32
    )
    high = through.astype(jnp.bfloat16)
    low = (through - high.astype(jnp.float32)).astype(jnp.bfloat16)
    own_columns = lax.dynamic_slice_in_dim(embedded, flat * rows, rows, 1).astype(jnp.float32)
    share_own = jnp.dot(
        own_columns,
        master_w,
        preferred_element_type=jnp.float32,
        precision=lax.Precision.HIGHEST,
    ) - coef * (dot32(high, grad_out) + dot32(low, grad_out))
    rows_f = tokens_new // count_fsdp

    def rows_of(j):
        start = (f ^ j) * rows_f
        at = start // piece
        placed = ((at // count_tp) ^ core) * count_tp + ((at % count_tp) ^ t)
        return lax.dynamic_slice_in_dim(share_own, placed * piece + start % piece, rows_f, 0)

    parts = {j: rows_of(j) for j in range(count_fsdp)}
    for bit in range(upper_bits + 1):
        sent = [j for j in parts if (j >> bit) & 1]
        got = exchange(jnp.concatenate([parts[j] for j in sent]), "fsdp", 1 << bit)
        parts = {
            j ^ (1 << bit): parts[j ^ (1 << bit)] + got[at * rows_f : (at + 1) * rows_f]
            for at, j in enumerate(sent)
        }
    col_width = columns // count_tp
    own_value = lax.dynamic_slice_in_dim(parts[0], t * col_width, col_width, 1)
    for step in range(1, count_tp):
        own_value = own_value + exchange(
            lax.dynamic_slice_in_dim(parts[0], (t ^ step) * col_width, col_width, 1), "tp", step
        )

    share = jnp.repeat(residual_mix, HD)[None, :]
    new_value = (share * own_value + (1.0 - share) * first_value.astype(jnp.float32)).astype(
        jnp.bfloat16
    )
    rows = queries.shape[0]
    heads_kv = residual_mix.shape[0]
    group = HEADS // KV
    context = cache_keys.shape[1]
    scale = 1.0 / math.sqrt(HD)
    query_b = queries.reshape(rows, heads_kv, group, HD)
    keys_b = cache_keys.reshape(rows, context, heads_kv, HD)
    vals_b = cache_values.reshape(rows, context, heads_kv, HD)
    newk_b = new_key.reshape(rows, heads_kv, HD)
    newv_b = new_value.reshape(rows, heads_kv, HD)
    scores = (
        jnp.einsum("rkgd,rckd->rkgc", query_b, keys_b, preferred_element_type=jnp.float32) * scale
    )
    fresh = jnp.einsum("rkgd,rkd->rkg", query_b, newk_b, preferred_element_type=jnp.float32) * scale
    valid = jnp.arange(context, dtype=jnp.int32)[None, :] < lengths[:, None]
    scores = jnp.where(valid[:, None, None, :], scores, -1e30)
    peak = jnp.maximum(jnp.max(scores, axis=-1), fresh)
    expo = jnp.exp(scores - peak[..., None])
    expo_new = jnp.exp(fresh - peak)
    total = jnp.sum(expo, axis=-1) + expo_new
    probs = (expo / total[..., None]).astype(jnp.bfloat16)
    probs_new = (expo_new / total).astype(jnp.bfloat16)
    mixed = jnp.einsum("rkgc,rckd->rkgd", probs, vals_b, preferred_element_type=jnp.float32)
    mixed = (
        mixed + probs_new.astype(jnp.float32)[..., None] * newv_b.astype(jnp.float32)[:, :, None, :]
    )
    attended = mixed.reshape(rows, group * heads_kv * HD).astype(jnp.bfloat16)
    return (w_next, new_value, attended)


def solution(mesh):
    return jax.shard_map(
        per_device,
        mesh=mesh,
        in_specs=(
            P(("fsdp", "tp"), None),
            P(("fsdp", "tp"), None),
            P(("fsdp", "tp"), None),
            P(("fsdp", "tp"), None),
            P(),
            P("fsdp", "tp"),
            P("fsdp", None, "tp"),
            P("fsdp", None, "tp"),
            P("fsdp", "tp"),
            P("fsdp", "tp"),
            P("tp"),
            P("fsdp"),
        ),
        out_specs=(P(("fsdp", "tp"), None), P("fsdp", "tp"), P("fsdp", "tp")),
        check_vma=False,
    )
```

```python
import functools
import math

import jax
import jax.numpy as jnp
from jax import lax
from jax.experimental import pallas as pl
from jax.experimental.pallas import tpu as pltpu
from jax.sharding import PartitionSpec as P

HEADS = 64
KV = 8
HD = 128
LANES = 128
SLAB = 16
VMEM = 56 << 20


def exchange(value, axis, mask):
    return lax.ppermute(value, axis, [(i, i ^ mask) for i in range(lax.axis_size(axis))])


def transpose_block(units, order, block, out):
    flipped = block[...].T
    rows = flipped.shape[0] // units
    for unit in range(units):
        place = pl.multiple_of(order[pl.num_programs(0) + unit] * rows, rows)
        out[pl.ds(place, rows), :] = flipped[unit * rows : (unit + 1) * rows]


def pack(activations, blocks, units, width):
    tokens = activations.shape[0]
    count = len(blocks)
    rows = width // len(units)
    if width % LANES or rows % 32:
        flipped = activations.T
        return jnp.concatenate(
            [
                lax.dynamic_slice_in_dim(flipped, block * width + unit * rows, rows, 0)
                for block in blocks
                for unit in units
            ]
        )
    return pl.pallas_call(
        functools.partial(transpose_block, len(units)),
        grid_spec=pltpu.PrefetchScalarGridSpec(
            num_scalar_prefetch=1,
            grid=(count,),
            in_specs=[pl.BlockSpec((tokens, width), lambda j, order: (0, order[j]))],
            out_specs=pl.BlockSpec((width, tokens), lambda j, order: (j, 0)),
        ),
        out_shape=jax.ShapeDtypeStruct((count * width, tokens), activations.dtype),
        compiler_params=pltpu.CompilerParams(vmem_limit_bytes=VMEM),
        cost_estimate=pl.CostEstimate(
            flops=0, bytes_accessed=4 * count * width * tokens, transcendentals=0
        ),
    )(jnp.stack(list(blocks) + list(units)).astype(jnp.int32), activations)


def runs_of(units):
    runs = []
    for unit in units:
        if runs and runs[-1][1] == unit:
            runs[-1][1] = unit + 1
        else:
            runs.append([unit, unit + 1])
    return runs


def multiply(wanted, rows, blocks, *refs):
    count = len(wanted)
    sources = refs[:4]
    outs = refs[4 : 4 + count]
    near, far, near_grad, far_grad, sems = refs[4 + count :]
    per_block = near.shape[0] // blocks
    copies = {}
    for at, (source, target) in enumerate(((sources[2], near_grad), (sources[3], far_grad))):
        copies["grad", at] = pltpu.make_async_copy(source, target, sems.at[at])
    for block in range(blocks):
        span = pl.ds(block * per_block, per_block)
        for at, (source, target) in enumerate(((sources[0], near), (sources[1], far))):
            copies[block, at] = pltpu.make_async_copy(
                source.at[span], target.at[span], sems.at[2 + 2 * block + at]
            )
    for copy in copies.values():
        copy.start()
    for at in range(2):
        copies["grad", at].wait()
    units_block = per_block // rows
    for block in range(blocks):
        for at in range(2):
            copies[block, at].wait()
        for (units, first, last, _), out in zip(wanted, outs):
            here = [unit for unit in units if unit // units_block == block]
            for low, high in runs_of(here):
                span = slice(low * rows, high * rows)
                place = units.index(low) * rows
                product = dot32(near[span, :], near_grad[:, first:last])
                product += dot32(far[span, :], far_grad[:, first:last])
                out[place : place + (high - low) * rows, :] = product.astype(out.dtype)


def products(lefts, grads, wanted, rows, blocks):
    total, tokens = lefts[0].shape
    columns = grads[0].shape[1]
    if rows % 32 or any((first | last) % LANES for _, first, last, _ in wanted):
        return [
            jnp.concatenate(
                [
                    sum(
                        dot32(left[low * rows : high * rows], grad[:, first:last])
                        for left, grad in zip(lefts, grads)
                    )
                    for low, high in runs_of(units)
                ]
            ).astype(kind)
            for units, first, last, kind in wanted
        ]
    shapes = [
        jax.ShapeDtypeStruct((len(units) * rows, last - first), kind)
        for units, first, last, kind in wanted
    ]
    work = sum(shape.size for shape in shapes)
    return pl.pallas_call(
        functools.partial(multiply, wanted, rows, blocks),
        out_shape=shapes,
        in_specs=[pl.BlockSpec(memory_space=pl.ANY)] * 4,
        out_specs=[pl.BlockSpec(memory_space=pltpu.VMEM)] * len(shapes),
        scratch_shapes=[pltpu.VMEM((total, tokens), lefts[0].dtype)] * 2
        + [pltpu.VMEM((tokens, columns), grads[0].dtype)] * 2
        + [pltpu.SemaphoreType.DMA((2 + 2 * blocks,))],
        compiler_params=pltpu.CompilerParams(vmem_limit_bytes=VMEM),
        cost_estimate=pl.CostEstimate(
            flops=4 * work * tokens,
            bytes_accessed=4 * tokens * (total + columns) + 4 * work,
            transcendentals=0,
        ),
    )(*lefts, *grads)


def pick_rows(place, *refs):
    slabs, out, held = refs[:SLAB], refs[SLAB], refs[SLAB + 1]
    held[...] = jnp.zeros_like(held)
    for k in range(SLAB):
        inside = place[pl.program_id(0) * SLAB + k]

        @pl.when(inside >= 0)
        def _():
            rows = slabs[k][...].astype(jnp.float32)
            at = lax.broadcasted_iota(jnp.int32, rows.shape, 0)
            chosen = jnp.where(at == lax.rem(inside, SLAB), rows, 0.0)
            held[k : k + 1, :] = jnp.sum(chosen, axis=0, keepdims=True)

    out[...] = held[...].astype(out.dtype)


def lookup(embed_table, token_ids, start):
    here, width = embed_table.shape
    count = token_ids.shape[0]
    inside = token_ids - start
    place = jnp.where((inside >= 0) & (inside < here), inside, -1)

    def slab_of(k):
        return lambda i, place: (jnp.maximum(place[i * SLAB + k], 0) // SLAB, 0)

    return pl.pallas_call(
        pick_rows,
        grid_spec=pltpu.PrefetchScalarGridSpec(
            num_scalar_prefetch=1,
            grid=(count // SLAB,),
            in_specs=[pl.BlockSpec((SLAB, width), slab_of(k)) for k in range(SLAB)],
            out_specs=pl.BlockSpec((SLAB, width), lambda i, place: (i, 0)),
            scratch_shapes=[pltpu.VMEM((SLAB, width), jnp.float32)],
        ),
        out_shape=jax.ShapeDtypeStruct((count, width), embed_table.dtype),
        compiler_params=pltpu.CompilerParams(vmem_limit_bytes=32 << 20),
        cost_estimate=pl.CostEstimate(
            flops=0, bytes_accessed=2 * count * SLAB * width, transcendentals=0
        ),
    )(place.astype(jnp.int32), *([embed_table] * SLAB))


def dot32(left, right):
    return jnp.dot(left, right, preferred_element_type=jnp.float32)


def per_device(
    activations,
    grad_out,
    master_w,
    embed_table,
    token_ids,
    queries,
    cache_keys,
    cache_values,
    new_key,
    first_value,
    residual_mix,
    lengths,
):
    count_fsdp = lax.axis_size("fsdp")
    count_tp = lax.axis_size("tp")
    devices_all = count_fsdp * count_tp
    width = activations.shape[1]
    tokens_total = activations.shape[0] * devices_all
    coef = 1.0 / math.sqrt(tokens_total * width)
    f = lax.axis_index("fsdp")
    t = lax.axis_index("tp")
    core = f & 1
    upper = f >> 1
    upper_bits = count_fsdp.bit_length() - 2
    uppers = 1 << upper_bits

    block = width // count_fsdp
    rows = master_w.shape[0]
    columns = master_w.shape[1]
    arranged = [r ^ (r >> 1) for r in range(uppers)][::-1]
    units_tp = [t ^ unit for unit in range(count_tp)]
    grads = [grad_out, exchange(grad_out, "fsdp", 1)]
    outgoing = pack(
        activations, [((r ^ upper) << 1) | (1 - core) for r in arranged], units_tp, block
    )
    incoming = exchange(outgoing, "fsdp", 1)
    staying = pack(activations, [((r ^ upper) << 1) | core for r in arranged], units_tp, block)
    lefts = [staying, incoming]

    places = [(r, unit) for r in arranged for unit in range(count_tp)]
    steps_upper = [("fsdp", bit) for bit in range(upper_bits)]
    steps_tp = [("tp", bit) for bit in range(count_tp.bit_length() - 1)]
    wide = columns * 3 // 8
    orders = [
        (0, wide, steps_upper + steps_tp),
        (wide, 2 * wide, steps_upper[::-1] + steps_tp),
        (2 * wide, columns, steps_tp[:1] + steps_upper + steps_tp[1:]),
    ]

    def has(place, step):
        return (place[step[0] == "tp"] >> step[1]) & 1

    def flip(place, step):
        mask = 1 << step[1]
        return (place[0], place[1] ^ mask) if step[0] == "tp" else (place[0] ^ mask, place[1])

    def split(held, step):
        return [p for p in held if has(p, step)], [p for p in held if not has(p, step)]

    wanted_sent, wanted_kept, kept = [], [], []
    for first, last, steps in orders:
        go, stay = split(places, steps[0])
        kept.append(stay)
        wanted_sent.append(([places.index(p) for p in go], first, last, jnp.bfloat16))
        wanted_kept.append(([places.index(p) for p in stay], first, last, jnp.float32))
    sending = products(lefts, grads, wanted_sent, rows, uppers)

    def take(value, held, chosen):
        runs = runs_of([held.index(p) for p in chosen])
        return jnp.concatenate([value[low * rows : high * rows] for low, high in runs])

    def send(value, step):
        mask = 1 << step[1]
        return exchange(value, step[0], 2 * mask if step[0] == "fsdp" else mask)

    first_got = [send(value, order[2][0]) for value, order in zip(sending, orders)]
    values = products(lefts, grads, wanted_kept, rows, uppers)
    finished = []
    for value, got, held, (first, last, steps) in zip(values, first_got, kept, orders):
        for at, step in enumerate(steps):
            if at:
                go, held = split(held, step)
                got = send(take(value, whole, go).astype(jnp.bfloat16), step)
                value = take(value, whole, held)
            else:
                go = split(places, step)[0]
            whole = held
            value = value + take(got, [flip(p, step) for p in go], held).astype(jnp.float32)
        finished.append(value)
    w_next = jnp.concatenate(
        [master_w[:, o[0] : o[1]] - coef * value for o, value in zip(orders, finished)], axis=1
    )

    flat = f * count_tp + t
    embedded = lax.psum(
        lookup(embed_table, token_ids, flat * embed_table.shape[0]), ("fsdp", "tp")
    )

    through = lax.dot_general(
        embedded, activations, (((1,), (1,)), ((), ())), preferred_element_type=jnp.float32
    )
    high = through.astype(jnp.bfloat16)
    low = (through - high.astype(jnp.float32)).astype(jnp.bfloat16)
    own_columns = lax.dynamic_slice_in_dim(embedded, flat * rows, rows, 1).astype(jnp.float32)
    share_own = jnp.dot(
        own_columns,
        master_w,
        preferred_element_type=jnp.float32,
        precision=lax.Precision.HIGHEST,
    ) - coef * (dot32(high, grad_out) + dot32(low, grad_out))
    rows_f = token_ids.shape[0] // count_fsdp
    col_width = columns // count_tp
    own_value = lax.psum_scatter(
        share_own.reshape(count_fsdp, rows_f, count_tp, col_width)
        .transpose(0, 2, 1, 3)
        .reshape(devices_all * rows_f, col_width),
        ("fsdp", "tp"),
        scatter_dimension=0,
        tiled=True,
    )

    share = jnp.repeat(residual_mix, HD)[None, :]
    new_value = (share * own_value + (1.0 - share) * first_value.astype(jnp.float32)).astype(
        jnp.bfloat16
    )
    rows = queries.shape[0]
    heads_kv = residual_mix.shape[0]
    group = HEADS // KV
    context = cache_keys.shape[1]
    scale = 1.0 / math.sqrt(HD)
    query_b = queries.reshape(rows, heads_kv, group, HD)
    keys_b = cache_keys.reshape(rows, context, heads_kv, HD)
    vals_b = cache_values.reshape(rows, context, heads_kv, HD)
    newk_b = new_key.reshape(rows, heads_kv, HD)
    newv_b = new_value.reshape(rows, heads_kv, HD)
    scores = (
        jnp.einsum("rkgd,rckd->rkgc", query_b, keys_b, preferred_element_type=jnp.float32) * scale
    )
    fresh = jnp.einsum("rkgd,rkd->rkg", query_b, newk_b, preferred_element_type=jnp.float32) * scale
    valid = jnp.arange(context, dtype=jnp.int32)[None, :] < lengths[:, None]
    scores = jnp.where(valid[:, None, None, :], scores, -1e30)
    peak = jnp.maximum(jnp.max(scores, axis=-1), fresh)
    expo = jnp.exp(scores - peak[..., None])
    expo_new = jnp.exp(fresh - peak)
    total = jnp.sum(expo, axis=-1) + expo_new
    probs = (expo / total[..., None]).astype(jnp.bfloat16)
    probs_new = (expo_new / total).astype(jnp.bfloat16)
    mixed = jnp.einsum("rkgc,rckd->rkgd", probs, vals_b, preferred_element_type=jnp.float32)
    mixed = (
        mixed + probs_new.astype(jnp.float32)[..., None] * newv_b.astype(jnp.float32)[:, :, None, :]
    )
    attended = mixed.reshape(rows, group * heads_kv * HD).astype(jnp.bfloat16)
    return (w_next, new_value, attended)


def solution(mesh):
    return jax.shard_map(
        per_device,
        mesh=mesh,
        in_specs=(
            P(("fsdp", "tp"), None),
            P(("fsdp", "tp"), None),
            P(("fsdp", "tp"), None),
            P(("fsdp", "tp"), None),
            P(),
            P("fsdp", "tp"),
            P("fsdp", None, "tp"),
            P("fsdp", None, "tp"),
            P("fsdp", "tp"),
            P("fsdp", "tp"),
            P("tp"),
            P("fsdp"),
        ),
        out_specs=(P(("fsdp", "tp"), None), P("fsdp", "tp"), P("fsdp", "tp")),
        check_vma=False,
    )
```

```python
import functools
import math

import jax
import jax.numpy as jnp
from jax import lax
from jax.experimental import pallas as pl
from jax.experimental.pallas import tpu as pltpu
from jax.sharding import PartitionSpec as P

HEADS = 64
KV = 8
HD = 128
LANES = 128
SLAB = 16
VMEM = 56 << 20


def exchange(value, axis, mask):
    return lax.ppermute(value, axis, [(i, i ^ mask) for i in range(lax.axis_size(axis))])


def transpose_block(units, order, block, out):
    width = block.shape[1]
    rows = width // units
    for low in range(0, width, LANES):
        flipped = block[:, low : low + LANES].T
        edge = low
        while edge < low + LANES:
            unit = edge // rows
            end = min(low + LANES, (unit + 1) * rows)
            place = order[pl.num_programs(0) + unit] * rows + (edge - unit * rows)
            place = pl.multiple_of(place, 32)
            out[pl.ds(place, end - edge), :] = flipped[edge - low : end - low]
            edge = end


def pack(activations, blocks, units, width):
    tokens = activations.shape[0]
    count = len(blocks)
    rows = width // len(units)
    if width % LANES or rows % 32:
        flipped = activations.T
        return jnp.concatenate(
            [
                lax.dynamic_slice_in_dim(flipped, block * width + unit * rows, rows, 0)
                for block in blocks
                for unit in units
            ]
        )
    return pl.pallas_call(
        functools.partial(transpose_block, len(units)),
        grid_spec=pltpu.PrefetchScalarGridSpec(
            num_scalar_prefetch=1,
            grid=(count,),
            in_specs=[pl.BlockSpec((tokens, width), lambda j, order: (0, order[j]))],
            out_specs=pl.BlockSpec((width, tokens), lambda j, order: (j, 0)),
        ),
        out_shape=jax.ShapeDtypeStruct((count * width, tokens), activations.dtype),
        compiler_params=pltpu.CompilerParams(vmem_limit_bytes=VMEM),
        cost_estimate=pl.CostEstimate(
            flops=0, bytes_accessed=4 * count * width * tokens, transcendentals=0
        ),
    )(jnp.stack(list(blocks) + list(units)).astype(jnp.int32), activations)


def runs_of(units):
    runs = []
    for unit in units:
        if runs and runs[-1][1] == unit:
            runs[-1][1] = unit + 1
        else:
            runs.append([unit, unit + 1])
    return runs


def multiply(wanted, rows, blocks, base, *refs):
    count = len(wanted)
    sources = refs[:4]
    outs = refs[4 : 4 + count]
    near, far, near_grad, far_grad, sems = refs[4 + count :]
    per_block = near.shape[0] // blocks
    units_block = per_block // rows
    needed = [
        block
        for block in range(blocks)
        if any(unit // units_block == block for item in wanted for unit in item[0])
    ]
    columns = pl.ds(base, near_grad.shape[1])
    copies = {}
    for at, (source, target) in enumerate(((sources[2], near_grad), (sources[3], far_grad))):
        copies["grad", at] = pltpu.make_async_copy(source.at[:, columns], target, sems.at[at])
    for block in needed:
        span = pl.ds(block * per_block, per_block)
        for at, (source, target) in enumerate(((sources[0], near), (sources[1], far))):
            copies[block, at] = pltpu.make_async_copy(
                source.at[span], target.at[span], sems.at[2 + 2 * block + at]
            )
    for copy in copies.values():
        copy.start()
    for at in range(2):
        copies["grad", at].wait()
    for block in needed:
        for at in range(2):
            copies[block, at].wait()
        for (units, first, last, _), out in zip(wanted, outs):
            here = [unit for unit in units if unit // units_block == block]
            for low, high in runs_of(here):
                span = slice(low * rows, high * rows)
                place = units.index(low) * rows
                cut = slice(first - base, last - base)
                product = dot32(near[span, :], near_grad[:, cut])
                product += dot32(far[span, :], far_grad[:, cut])
                out[place : place + (high - low) * rows, :] = product.astype(out.dtype)


def products(lefts, grads, wanted, rows, blocks):
    total, tokens = lefts[0].shape
    base = min(first for _, first, _, _ in wanted)
    columns = max(last for _, _, last, _ in wanted) - base
    if rows % 32 or any((first | last) % LANES for _, first, last, _ in wanted):
        return [
            jnp.concatenate(
                [
                    sum(
                        dot32(left[low * rows : high * rows], grad[:, first:last])
                        for left, grad in zip(lefts, grads)
                    )
                    for low, high in runs_of(units)
                ]
            ).astype(kind)
            for units, first, last, kind in wanted
        ]
    shapes = [
        jax.ShapeDtypeStruct((len(units) * rows, last - first), kind)
        for units, first, last, kind in wanted
    ]
    work = sum(shape.size for shape in shapes)
    return pl.pallas_call(
        functools.partial(multiply, wanted, rows, blocks, base),
        out_shape=shapes,
        in_specs=[pl.BlockSpec(memory_space=pl.ANY)] * 4,
        out_specs=[pl.BlockSpec(memory_space=pltpu.VMEM)] * len(shapes),
        scratch_shapes=[pltpu.VMEM((total, tokens), lefts[0].dtype)] * 2
        + [pltpu.VMEM((tokens, columns), grads[0].dtype)] * 2
        + [pltpu.SemaphoreType.DMA((2 + 2 * blocks,))],
        compiler_params=pltpu.CompilerParams(vmem_limit_bytes=VMEM),
        cost_estimate=pl.CostEstimate(
            flops=4 * work * tokens,
            bytes_accessed=4 * tokens * (total + columns) + 4 * work,
            transcendentals=0,
        ),
    )(*lefts, *grads)


def pick_rows(place, *refs):
    slabs, out, held = refs[:SLAB], refs[SLAB], refs[SLAB + 1]
    held[...] = jnp.zeros_like(held)
    for k in range(SLAB):
        inside = place[pl.program_id(0) * SLAB + k]

        @pl.when(inside >= 0)
        def _():
            rows = slabs[k][...].astype(jnp.float32)
            at = lax.broadcasted_iota(jnp.int32, rows.shape, 0)
            chosen = jnp.where(at == lax.rem(inside, SLAB), rows, 0.0)
            held[k : k + 1, :] = jnp.sum(chosen, axis=0, keepdims=True)

    out[...] = held[...].astype(out.dtype)


def lookup(embed_table, token_ids, start):
    here, width = embed_table.shape
    count = token_ids.shape[0]
    inside = token_ids - start
    place = jnp.where((inside >= 0) & (inside < here), inside, -1)

    def slab_of(k):
        return lambda i, place: (jnp.maximum(place[i * SLAB + k], 0) // SLAB, 0)

    return pl.pallas_call(
        pick_rows,
        grid_spec=pltpu.PrefetchScalarGridSpec(
            num_scalar_prefetch=1,
            grid=(count // SLAB,),
            in_specs=[pl.BlockSpec((SLAB, width), slab_of(k)) for k in range(SLAB)],
            out_specs=pl.BlockSpec((SLAB, width), lambda i, place: (i, 0)),
            scratch_shapes=[pltpu.VMEM((SLAB, width), jnp.float32)],
        ),
        out_shape=jax.ShapeDtypeStruct((count, width), embed_table.dtype),
        compiler_params=pltpu.CompilerParams(vmem_limit_bytes=32 << 20),
        cost_estimate=pl.CostEstimate(
            flops=0, bytes_accessed=2 * count * SLAB * width, transcendentals=0
        ),
    )(place.astype(jnp.int32), *([embed_table] * SLAB))


def spread(blocks, units, folds, order, found, out, flipped):
    width = flipped.shape[0]
    rows = width // units
    lines = rows // folds
    for block in range(blocks):
        start = pl.multiple_of(order[block] * width, LANES)
        flipped[...] = found[:, pl.ds(start, width)].astype(jnp.float32).T
        for unit in range(units):
            from_row = order[blocks + unit] * rows
            pieces = [
                flipped[pl.ds(pl.multiple_of(from_row + fold * lines, 8), lines), :]
                for fold in range(folds)
            ]
            place = (block * units + unit) * lines
            out[place : place + lines, :] = jnp.concatenate(pieces, axis=1)


def arrange(found, blocks, units, width, lanes):
    tokens = found.shape[0]
    rows = width // len(units)
    folds = lanes // tokens
    lines = rows // folds
    if width % LANES or lines % 8:
        flipped = found.T
        parts = [
            lax.dynamic_slice_in_dim(flipped, block * width + unit * rows, rows, 0)
            for block in blocks
            for unit in units
        ]
        return jnp.concatenate(
            [
                jnp.concatenate(
                    [part[fold * lines : (fold + 1) * lines] for fold in range(folds)], axis=1
                )
                for part in parts
            ]
        )
    shape = jax.ShapeDtypeStruct((len(blocks) * len(units) * lines, lanes), jnp.float32)
    return pl.pallas_call(
        functools.partial(spread, len(blocks), len(units), folds),
        in_specs=[
            pl.BlockSpec(memory_space=pltpu.SMEM),
            pl.BlockSpec(memory_space=pltpu.VMEM),
        ],
        out_specs=pl.BlockSpec(memory_space=pltpu.VMEM),
        out_shape=shape,
        scratch_shapes=[pltpu.VMEM((width, tokens), jnp.float32)],
        compiler_params=pltpu.CompilerParams(vmem_limit_bytes=32 << 20),
        cost_estimate=pl.CostEstimate(
            flops=0, bytes_accessed=2 * found.size + 4 * shape.size, transcendentals=0
        ),
    )(jnp.stack(list(blocks) + list(units)).astype(jnp.int32), found).astype(found.dtype)


def dot32(left, right):
    return jnp.dot(left, right, preferred_element_type=jnp.float32)


def per_device(
    activations,
    grad_out,
    master_w,
    embed_table,
    token_ids,
    queries,
    cache_keys,
    cache_values,
    new_key,
    first_value,
    residual_mix,
    lengths,
):
    count_fsdp = lax.axis_size("fsdp")
    count_tp = lax.axis_size("tp")
    devices_all = count_fsdp * count_tp
    width = activations.shape[1]
    tokens_total = activations.shape[0] * devices_all
    coef = 1.0 / math.sqrt(tokens_total * width)
    f = lax.axis_index("fsdp")
    t = lax.axis_index("tp")
    core = f & 1
    upper = f >> 1
    upper_bits = count_fsdp.bit_length() - 2
    uppers = 1 << upper_bits

    block = width // count_fsdp
    rows = master_w.shape[0]
    columns = master_w.shape[1]
    arranged = [r ^ (r >> 1) for r in range(uppers)][::-1]
    units_tp = [t ^ unit for unit in range(count_tp)]
    grads = [grad_out, exchange(grad_out, "fsdp", 1)]
    outgoing = pack(
        activations, [((r ^ upper) << 1) | (1 - core) for r in arranged], units_tp, block
    )
    incoming = exchange(outgoing, "fsdp", 1)
    staying = pack(activations, [((r ^ upper) << 1) | core for r in arranged], units_tp, block)
    lefts = [staying, incoming]

    tokens_new = token_ids.shape[0]
    flat = f * count_tp + t
    quarter = columns // 4
    eighth = columns // 8
    folds = quarter // tokens_new
    found = lookup(embed_table, token_ids, flat * embed_table.shape[0])
    theirs = arrange(found, [((r ^ upper) << 1) | (1 - core) for r in arranged], units_tp, block, quarter)
    ours = arrange(found, [((r ^ upper) << 1) | core for r in arranged], units_tp, block, quarter)
    asked = ours + exchange(theirs, "fsdp", 1)
    lines = rows // folds

    places = [(r, unit) for r in arranged for unit in range(count_tp)]
    steps_upper = [("fsdp", bit) for bit in range(upper_bits)]
    steps_tp = [("tp", bit) for bit in range(count_tp.bit_length() - 1)]
    one, two, three = (
        steps_upper + steps_tp,
        steps_upper[::-1] + steps_tp,
        steps_tp + steps_upper,
    )
    edges = [0, quarter, 2 * quarter, 3 * quarter, 3 * quarter + eighth, columns]
    spans = list(zip(edges[:-1], edges[1:]))
    orders = [one, two, three, one, two]

    def has(place, step):
        return (place[step[0] == "tp"] >> step[1]) & 1

    def flip(place, step):
        mask = 1 << step[1]
        return (place[0], place[1] ^ mask) if step[0] == "tp" else (place[0] ^ mask, place[1])

    def split(held, step):
        return [p for p in held if has(p, step)], [p for p in held if not has(p, step)]

    def take(value, held, chosen, size):
        runs = runs_of([held.index(p) for p in chosen])
        return jnp.concatenate([value[low * size : high * size] for low, high in runs])

    def send(value, step):
        mask = 1 << step[1]
        return exchange(value, step[0], 2 * mask if step[0] == "fsdp" else mask)

    def compute(which, sent):
        wanted = []
        for index in which:
            chosen = split(places, orders[index][0])[0 if sent else 1]
            units = [places.index(p) for p in chosen]
            kind = jnp.bfloat16 if sent else jnp.float32
            wanted.append((units, *spans[index], kind))
        return dict(zip(which, products(lefts, grads, wanted, rows, uppers)))

    going = compute([0, 1], True)
    going |= compute([2, 3, 4], True)
    go, stay = split(places, three[0])
    going[2] = jnp.concatenate([going[2], take(asked, places, go, lines)])
    got = {index: send(value, orders[index][0]) for index, value in going.items()}
    values = {index: [value] for index, value in compute(list(range(5)), False).items()}
    values[2].append(take(asked, places, stay, lines).astype(jnp.float32))
    sizes = {index: [rows] for index in range(5)}
    sizes[2].append(lines)
    held = {index: places for index in range(5)}
    token = going[4]

    def receive(index, step):
        gone, kept = split(held[index], step)
        landed = [flip(p, step) for p in gone]
        start = 0
        added = []
        for value, size in zip(values[index], sizes[index]):
            piece = got[index][start : start + len(gone) * size]
            start += len(gone) * size
            added.append(value + take(piece, landed, kept, size).astype(jnp.float32))
        values[index], held[index] = added, kept

    for at in range(len(one)):
        for group in ((0, 1), (2,), (3, 4)) if at == 0 else ((0, 1), (3, 4), (2,)):
            tied = lax.optimization_barrier([got[index] for index in group] + [token])
            for index, arrived in zip(group, tied):
                got[index] = arrived
                receive(index, orders[index][at])
            if at + 1 == len(one):
                continue
            outgoing = []
            for index in group:
                gone, kept = split(held[index], orders[index][at + 1])
                pieces = [
                    take(value, held[index], gone, size).astype(jnp.bfloat16)
                    for value, size in zip(values[index], sizes[index])
                ]
                values[index] = [
                    take(value, held[index], kept, size)
                    for value, size in zip(values[index], sizes[index])
                ]
                outgoing.append(jnp.concatenate(pieces))
            outgoing = lax.optimization_barrier(outgoing)
            token = outgoing[-1]
            for index, value in zip(group, outgoing):
                got[index] = send(value, orders[index][at + 1])
    w_next = jnp.concatenate(
        [master_w[:, low:high] - coef * values[at][0] for at, (low, high) in enumerate(spans)],
        axis=1,
    )

    flat_rows = values[2][1].astype(jnp.bfloat16)
    columns_own = jnp.concatenate(
        [flat_rows[:, fold * tokens_new : (fold + 1) * tokens_new] for fold in range(folds)]
    )
    share_own = lax.dot_general(
        columns_own,
        w_next.astype(jnp.bfloat16),
        (((0,), (0,)), ((), ())),
        preferred_element_type=jnp.float32,
    )
    rows_f = tokens_new // count_fsdp
    col_width = columns // count_tp
    blocks_own = (
        share_own.reshape(count_fsdp, rows_f, count_tp, col_width)
        .transpose(0, 2, 1, 3)
        .reshape(devices_all, rows_f, col_width)
    )
    own_value = jnp.sum(
        lax.all_to_all(blocks_own, ("fsdp", "tp"), split_axis=0, concat_axis=0), axis=0
    )

    share = jnp.repeat(residual_mix, HD)[None, :]
    new_value = (share * own_value + (1.0 - share) * first_value.astype(jnp.float32)).astype(
        jnp.bfloat16
    )
    rows = queries.shape[0]
    heads_kv = residual_mix.shape[0]
    group = HEADS // KV
    context = cache_keys.shape[1]
    scale = 1.0 / math.sqrt(HD)
    query_b = queries.reshape(rows, heads_kv, group, HD)
    keys_b = cache_keys.reshape(rows, context, heads_kv, HD)
    vals_b = cache_values.reshape(rows, context, heads_kv, HD)
    newk_b = new_key.reshape(rows, heads_kv, HD)
    newv_b = new_value.reshape(rows, heads_kv, HD)
    scores = (
        jnp.einsum("rkgd,rckd->rkgc", query_b, keys_b, preferred_element_type=jnp.float32) * scale
    )
    fresh = jnp.einsum("rkgd,rkd->rkg", query_b, newk_b, preferred_element_type=jnp.float32) * scale
    valid = jnp.arange(context, dtype=jnp.int32)[None, :] < lengths[:, None]
    scores = jnp.where(valid[:, None, None, :], scores, -1e30)
    peak = jnp.maximum(jnp.max(scores, axis=-1), fresh)
    expo = jnp.exp(scores - peak[..., None])
    expo_new = jnp.exp(fresh - peak)
    total = jnp.sum(expo, axis=-1) + expo_new
    probs = (expo / total[..., None]).astype(jnp.bfloat16)
    probs_new = (expo_new / total).astype(jnp.bfloat16)
    mixed = jnp.einsum("rkgc,rckd->rkgd", probs, vals_b, preferred_element_type=jnp.float32)
    mixed = (
        mixed + probs_new.astype(jnp.float32)[..., None] * newv_b.astype(jnp.float32)[:, :, None, :]
    )
    attended = mixed.reshape(rows, group * heads_kv * HD).astype(jnp.bfloat16)
    return (w_next, new_value, attended)


def solution(mesh):
    return jax.shard_map(
        per_device,
        mesh=mesh,
        in_specs=(
            P(("fsdp", "tp"), None),
            P(("fsdp", "tp"), None),
            P(("fsdp", "tp"), None),
            P(("fsdp", "tp"), None),
            P(),
            P("fsdp", "tp"),
            P("fsdp", None, "tp"),
            P("fsdp", None, "tp"),
            P("fsdp", "tp"),
            P("fsdp", "tp"),
            P("tp"),
            P("fsdp"),
        ),
        out_specs=(P(("fsdp", "tp"), None), P("fsdp", "tp"), P("fsdp", "tp")),
        check_vma=False,
    )
```

```python
import functools
import math

import jax
import jax.numpy as jnp
from jax import lax
from jax.experimental import pallas as pl
from jax.experimental.pallas import tpu as pltpu
from jax.sharding import PartitionSpec as P

HEADS = 64
KV = 8
HD = 128
LANES = 128
SLAB = 16
VMEM = 56 << 20


def exchange(value, axis, mask):
    return lax.ppermute(value, axis, [(i, i ^ mask) for i in range(lax.axis_size(axis))])


def own_place():
    f = lax.axis_index("fsdp")
    return f & 1, f >> 1, lax.axis_index("tp")


def transpose_blocks(arranged, mine, units, source, out, wide, tall, arrived, left):
    core, upper, t = own_place()
    width = wide.shape[2]
    rows = width // units
    side = core if mine else 1 - core
    taken, given = [], []
    for j, r in enumerate(arranged):
        start = pl.multiple_of((((r ^ upper) << 1) | side) * width, LANES)
        copy = pltpu.make_async_copy(source.at[:, pl.ds(start, width)], wide.at[j], arrived.at[j])
        copy.start()
        taken.append(copy)
    for j in range(len(arranged)):
        taken[j].wait()
        for low in range(0, width, LANES):
            tall[j, low : low + LANES, :] = wide[j, :, low : low + LANES].T
        for unit in range(units):
            place = pl.multiple_of(j * width + (unit ^ t) * rows, 32)
            copy = pltpu.make_async_copy(
                tall.at[j, pl.ds(unit * rows, rows)],
                out.at[pl.ds(place, rows)],
                left.at[j * units + unit],
            )
            copy.start()
            given.append(copy)
    for copy in given:
        copy.wait()


def pack(activations, arranged, mine, units, width):
    tokens = activations.shape[0]
    count = len(arranged)
    rows = width // units
    if width % LANES or rows % 32:
        core, upper, t = own_place()
        side = core if mine else 1 - core
        flipped = activations.T
        return jnp.concatenate(
            [
                lax.dynamic_slice_in_dim(
                    flipped, (((r ^ upper) << 1) | side) * width + (unit ^ t) * rows, rows, 0
                )
                for r in arranged
                for unit in range(units)
            ]
        )
    kind = activations.dtype
    return pl.pallas_call(
        functools.partial(transpose_blocks, arranged, mine, units),
        in_specs=[pl.BlockSpec(memory_space=pl.ANY)],
        out_specs=pl.BlockSpec(memory_space=pl.ANY),
        out_shape=jax.ShapeDtypeStruct((count * width, tokens), kind),
        scratch_shapes=[
            pltpu.VMEM((count, tokens, width), kind),
            pltpu.VMEM((count, width, tokens), kind),
            pltpu.SemaphoreType.DMA((count,)),
            pltpu.SemaphoreType.DMA((count * units,)),
        ],
        compiler_params=pltpu.CompilerParams(vmem_limit_bytes=VMEM),
        cost_estimate=pl.CostEstimate(
            flops=0, bytes_accessed=4 * count * width * tokens, transcendentals=0
        ),
    )(activations)


def runs_of(units):
    runs = []
    for unit in units:
        if runs and runs[-1][1] == unit:
            runs[-1][1] = unit + 1
        else:
            runs.append([unit, unit + 1])
    return runs


def multiply(wanted, rows, blocks, base, *refs):
    count = len(wanted)
    sources = refs[:4]
    outs = refs[4 : 4 + count]
    left, right, sems = refs[4 + count :]
    tokens = left.shape[1] // 2
    per_block = left.shape[0] // blocks
    units_block = per_block // rows
    needed = [
        block
        for block in range(blocks)
        if any(unit // units_block == block for item in wanted for unit in item[0])
    ]
    columns = pl.ds(base, right.shape[1])
    halves = [pl.ds(0, tokens), pl.ds(tokens, tokens)]
    grads, lefts = [], {}
    for at, half in enumerate(halves):
        grads.append(
            pltpu.make_async_copy(sources[2 + at].at[:, columns], right.at[half], sems.at[at])
        )
        grads[at].start()
    for block in needed:
        span = pl.ds(block * per_block, per_block)
        for at, half in enumerate(halves):
            lefts[block, at] = pltpu.make_async_copy(
                sources[at].at[span], left.at[span, half], sems.at[2 + 2 * block + at]
            )
            lefts[block, at].start()
    for copy in grads:
        copy.wait()
    for block in needed:
        for at in range(2):
            lefts[block, at].wait()
        for (units, first, last, _), out in zip(wanted, outs):
            here = [unit for unit in units if unit // units_block == block]
            for low, high in runs_of(here):
                place = units.index(low) * rows
                product = dot32(
                    left[low * rows : high * rows, :], right[:, first - base : last - base]
                )
                out[place : place + (high - low) * rows, :] = product.astype(out.dtype)


def products(lefts, grads, wanted, rows, blocks):
    total, tokens = lefts[0].shape
    base = min(first for _, first, _, _ in wanted)
    columns = max(last for _, _, last, _ in wanted) - base
    if rows % 32 or any((first | last) % LANES for _, first, last, _ in wanted):
        return [
            jnp.concatenate(
                [
                    sum(
                        dot32(left[low * rows : high * rows], grad[:, first:last])
                        for left, grad in zip(lefts, grads)
                    )
                    for low, high in runs_of(units)
                ]
            ).astype(kind)
            for units, first, last, kind in wanted
        ]
    shapes = [
        jax.ShapeDtypeStruct((len(units) * rows, last - first), kind)
        for units, first, last, kind in wanted
    ]
    return pl.pallas_call(
        functools.partial(multiply, wanted, rows, blocks, base),
        out_shape=shapes,
        in_specs=[pl.BlockSpec(memory_space=pl.ANY)] * 4,
        out_specs=[pl.BlockSpec(memory_space=pltpu.VMEM)] * len(shapes),
        scratch_shapes=[
            pltpu.VMEM((total, 2 * tokens), lefts[0].dtype),
            pltpu.VMEM((2 * tokens, columns), grads[0].dtype),
            pltpu.SemaphoreType.DMA((2 + 2 * blocks,)),
        ],
        compiler_params=pltpu.CompilerParams(vmem_limit_bytes=VMEM // 2),
        cost_estimate=pl.CostEstimate(flops=1, bytes_accessed=1, transcendentals=0),
    )(*lefts, *grads)


def pick_rows(arranged, units, place, table, tail, *refs):
    outs, (slabs, found, flipped, sems) = refs[:2], refs[2:]
    here = table.shape[0]
    whole = here // SLAB * SLAB
    tokens, width_all = found.shape
    width = flipped.shape[0]
    rows = width // units
    lanes = outs[0].shape[1]
    folds = lanes // tokens
    lines = rows // folds

    def slab_copy(source, k):
        return pltpu.make_async_copy(source, slabs.at[k], sems.at[k])

    for k in range(tokens):
        inside = place[k]

        @pl.when((inside >= 0) & (inside < whole))
        def _():
            start = pl.multiple_of(lax.div(inside, SLAB) * SLAB, SLAB)
            slab_copy(table.at[pl.ds(start, SLAB)], k).start()

        @pl.when(inside >= whole)
        def _():
            slab_copy(tail, k).start()

    found[...] = jnp.zeros_like(found)
    for k in range(tokens):
        inside = place[k]

        @pl.when(inside >= 0)
        def _():
            slab_copy(tail, k).wait()
            line = jnp.where(inside < whole, lax.rem(inside, SLAB), inside - (here - SLAB))
            held = slabs[k].astype(jnp.float32)
            at = lax.broadcasted_iota(jnp.int32, held.shape, 0)
            found[k : k + 1, :] = jnp.sum(
                jnp.where(at == line, held, 0.0), axis=0, keepdims=True
            )

    core, upper, t = own_place()
    for side, out in zip((1 - core, core), outs):
        for j, r in enumerate(arranged):
            start = pl.multiple_of((((r ^ upper) << 1) | side) * width, LANES)
            flipped[...] = found[:, pl.ds(start, width)].T
            for unit in range(units):
                from_row = (unit ^ t) * rows
                pieces = [
                    flipped[pl.ds(pl.multiple_of(from_row + fold * lines, 8), lines), :]
                    for fold in range(folds)
                ]
                put = (j * units + unit) * lines
                out[put : put + lines, :] = jnp.concatenate(pieces, axis=1).astype(out.dtype)


def fold_unit(part, lanes):
    rows, tokens = part.shape
    if tokens >= lanes:
        return jnp.concatenate([part[:, at : at + lanes] for at in range(0, tokens, lanes)])
    lines = rows * tokens // lanes
    return jnp.concatenate([part[at : at + lines] for at in range(0, rows, lines)], axis=1)


def unfold_unit(folded, rows):
    lines, lanes = folded.shape
    tokens = lines * lanes // rows
    if tokens >= lanes:
        return jnp.concatenate([folded[at : at + rows] for at in range(0, lines, rows)], axis=1)
    return jnp.concatenate([folded[:, at : at + tokens] for at in range(0, lanes, tokens)])


def lookup(embed_table, token_ids, arranged, units, width, lanes):
    here, width_all = embed_table.shape
    tokens = token_ids.shape[0]
    rows = width // units
    core, upper, t = own_place()
    inside = token_ids - (lax.axis_index("fsdp") * units + t) * here
    place = jnp.where((inside >= 0) & (inside < here), inside, -1).astype(jnp.int32)
    kind = embed_table.dtype
    if width % LANES or lanes % tokens or (rows * tokens // lanes) % 16:
        found = jnp.where(
            (place >= 0)[:, None], embed_table[jnp.maximum(place, 0)], jnp.zeros((), kind)
        )
        flipped = found.T
        return [
            jnp.concatenate(
                [
                    fold_unit(
                        lax.dynamic_slice_in_dim(
                            flipped,
                            (((r ^ upper) << 1) | side) * width + (unit ^ t) * rows,
                            rows,
                            0,
                        ),
                        lanes,
                    )
                    for r in arranged
                    for unit in range(units)
                ]
            )
            for side in (1 - core, core)
        ]
    shape = jax.ShapeDtypeStruct((len(arranged) * width * tokens // lanes, lanes), kind)
    return pl.pallas_call(
        functools.partial(pick_rows, arranged, units),
        in_specs=[
            pl.BlockSpec(memory_space=pltpu.SMEM),
            pl.BlockSpec(memory_space=pl.ANY),
            pl.BlockSpec(memory_space=pl.ANY),
        ],
        out_specs=[pl.BlockSpec(memory_space=pltpu.VMEM)] * 2,
        out_shape=[shape, shape],
        scratch_shapes=[
            pltpu.VMEM((tokens, SLAB, width_all), kind),
            pltpu.VMEM((tokens, width_all), jnp.float32),
            pltpu.VMEM((width, tokens), jnp.float32),
            pltpu.SemaphoreType.DMA((tokens,)),
        ],
        compiler_params=pltpu.CompilerParams(vmem_limit_bytes=VMEM // 2),
        cost_estimate=pl.CostEstimate(flops=1, bytes_accessed=1, transcendentals=0),
    )(place, embed_table, embed_table[here - SLAB :])


def dot32(left, right):
    return jnp.dot(left, right, preferred_element_type=jnp.float32)


def per_device(
    activations,
    grad_out,
    master_w,
    embed_table,
    token_ids,
    queries,
    cache_keys,
    cache_values,
    new_key,
    first_value,
    residual_mix,
    lengths,
):
    count_fsdp = lax.axis_size("fsdp")
    count_tp = lax.axis_size("tp")
    devices_all = count_fsdp * count_tp
    width = activations.shape[1]
    tokens_total = activations.shape[0] * devices_all
    coef = 1.0 / math.sqrt(tokens_total * width)
    upper_bits = count_fsdp.bit_length() - 2
    uppers = 1 << upper_bits

    block = width // count_fsdp
    rows = master_w.shape[0]
    columns = master_w.shape[1]
    arranged = [r ^ (r >> 1) for r in range(uppers)][::-1]
    grads = [grad_out, exchange(grad_out, "fsdp", 1)]
    incoming = exchange(pack(activations, arranged, False, count_tp, block), "fsdp", 1)
    staying = pack(activations, arranged, True, count_tp, block)
    lefts = [staying, incoming]
    tokens_new = token_ids.shape[0]
    quarter = columns // 4
    eighth = columns // 8
    lines = rows * tokens_new // eighth

    places = [(r, unit) for r in arranged for unit in range(count_tp)]
    steps_upper = [("fsdp", bit) for bit in range(upper_bits)]
    steps_tp = [("tp", bit) for bit in range(count_tp.bit_length() - 1)]
    one, two, three = (
        steps_upper + steps_tp,
        steps_upper[::-1] + steps_tp,
        steps_tp + steps_upper,
    )
    edges = [0, quarter, 2 * quarter, 3 * quarter, 3 * quarter + eighth, columns]
    spans = list(zip(edges[:-1], edges[1:]))
    orders = [one, two, three, one, two]

    def has(place, step):
        return (place[step[0] == "tp"] >> step[1]) & 1

    def flip(place, step):
        mask = 1 << step[1]
        return (place[0], place[1] ^ mask) if step[0] == "tp" else (place[0] ^ mask, place[1])

    def split(held, step):
        return [p for p in held if has(p, step)], [p for p in held if not has(p, step)]

    def take(value, held, chosen, size):
        runs = runs_of([held.index(p) for p in chosen])
        return jnp.concatenate([value[low * size : high * size] for low, high in runs])

    def send(value, step):
        mask = 1 << step[1]
        return exchange(value, step[0], 2 * mask if step[0] == "fsdp" else mask)

    def compute(which, sent, factors):
        wanted = []
        for index in which:
            chosen = split(places, orders[index][0])[0 if sent else 1]
            units = [places.index(p) for p in chosen]
            kind = jnp.bfloat16 if sent else jnp.float32
            wanted.append((units, *spans[index], kind))
        return dict(zip(which, products(factors, grads, wanted, rows, uppers)))

    going = compute([2, 0, 1], True, lefts)
    got = {index: send(value, orders[index][0]) for index, value in going.items()}
    going |= compute([3, 4], True, lefts)
    got[3] = send(going[3], orders[3][0])

    theirs, ours = lookup(embed_table, token_ids, arranged, count_tp, block, eighth)
    asked = ours + exchange(theirs, "fsdp", 1)
    go, stay = split(places, orders[4][0])
    values = compute([0, 1, 2], False, lefts)
    token = jnp.concatenate([going[4], take(asked, places, go, lines)])
    got[4] = send(token, orders[4][0])
    values |= compute([3, 4], False, lefts)
    values = {index: [value] for index, value in values.items()}
    values[4].append(take(asked, places, stay, lines).astype(jnp.float32))
    sizes = {index: [rows] for index in range(5)}
    sizes[4].append(lines)
    held = {index: places for index in range(5)}

    def receive(index, step):
        gone, kept = split(held[index], step)
        landed = [flip(p, step) for p in gone]
        start = 0
        added = []
        for value, size in zip(values[index], sizes[index]):
            piece = got[index][start : start + len(gone) * size]
            start += len(gone) * size
            added.append(value + take(piece, landed, kept, size).astype(jnp.float32))
        values[index], held[index] = added, kept

    for at in range(len(one)):
        for group in ((0, 1), (2,), (3, 4)):
            tied = lax.optimization_barrier([got[index] for index in group] + [token])
            for index, arrived in zip(group, tied):
                got[index] = arrived
                receive(index, orders[index][at])
            if at + 1 == len(one):
                continue
            outgoing = []
            for index in group:
                gone, kept = split(held[index], orders[index][at + 1])
                pieces = [
                    take(value, held[index], gone, size).astype(jnp.bfloat16)
                    for value, size in zip(values[index], sizes[index])
                ]
                values[index] = [
                    take(value, held[index], kept, size)
                    for value, size in zip(values[index], sizes[index])
                ]
                outgoing.append(jnp.concatenate(pieces))
            outgoing = lax.optimization_barrier(outgoing)
            token = outgoing[-1]
            for index, value in zip(group, outgoing):
                got[index] = send(value, orders[index][at + 1])
    w_next = jnp.concatenate(
        [master_w[:, low:high] - coef * values[at][0] for at, (low, high) in enumerate(spans)],
        axis=1,
    )

    columns_own = unfold_unit(values[4][1].astype(jnp.bfloat16), rows)
    share_own = lax.dot_general(
        columns_own,
        w_next.astype(jnp.bfloat16),
        (((0,), (0,)), ((), ())),
        preferred_element_type=jnp.float32,
    )
    rows_f = tokens_new // count_fsdp
    col_width = columns // count_tp
    blocks_own = (
        share_own.reshape(count_fsdp, rows_f, count_tp, col_width)
        .transpose(0, 2, 1, 3)
        .reshape(devices_all, rows_f, col_width)
    )
    own_value = jnp.sum(
        lax.all_to_all(blocks_own, ("fsdp", "tp"), split_axis=0, concat_axis=0), axis=0
    )

    share = jnp.repeat(residual_mix, HD)[None, :]
    new_value = (share * own_value + (1.0 - share) * first_value.astype(jnp.float32)).astype(
        jnp.bfloat16
    )
    rows = queries.shape[0]
    heads_kv = residual_mix.shape[0]
    group = HEADS // KV
    context = cache_keys.shape[1]
    scale = 1.0 / math.sqrt(HD)
    query_b = queries.reshape(rows, heads_kv, group, HD)
    keys_b = cache_keys.reshape(rows, context, heads_kv, HD)
    vals_b = cache_values.reshape(rows, context, heads_kv, HD)
    newk_b = new_key.reshape(rows, heads_kv, HD)
    newv_b = new_value.reshape(rows, heads_kv, HD)
    scores = (
        jnp.einsum("rkgd,rckd->rkgc", query_b, keys_b, preferred_element_type=jnp.float32) * scale
    )
    fresh = jnp.einsum("rkgd,rkd->rkg", query_b, newk_b, preferred_element_type=jnp.float32) * scale
    valid = jnp.arange(context, dtype=jnp.int32)[None, :] < lengths[:, None]
    scores = jnp.where(valid[:, None, None, :], scores, -1e30)
    peak = jnp.maximum(jnp.max(scores, axis=-1), fresh)
    expo = jnp.exp(scores - peak[..., None])
    expo_new = jnp.exp(fresh - peak)
    total = jnp.sum(expo, axis=-1) + expo_new
    probs = (expo / total[..., None]).astype(jnp.bfloat16)
    probs_new = (expo_new / total).astype(jnp.bfloat16)
    mixed = lax.optimization_barrier(
        jnp.einsum("rkgc,rckd->rkgd", probs, vals_b, preferred_element_type=jnp.float32)
    )
    mixed = (
        mixed + probs_new.astype(jnp.float32)[..., None] * newv_b.astype(jnp.float32)[:, :, None, :]
    )
    attended = mixed.reshape(rows, group * heads_kv * HD).astype(jnp.bfloat16)
    return (w_next, new_value, attended)


def solution(mesh):
    return jax.shard_map(
        per_device,
        mesh=mesh,
        in_specs=(
            P(("fsdp", "tp"), None),
            P(("fsdp", "tp"), None),
            P(("fsdp", "tp"), None),
            P(("fsdp", "tp"), None),
            P(),
            P("fsdp", "tp"),
            P("fsdp", None, "tp"),
            P("fsdp", None, "tp"),
            P("fsdp", "tp"),
            P("fsdp", "tp"),
            P("tp"),
            P("fsdp"),
        ),
        out_specs=(P(("fsdp", "tp"), None), P("fsdp", "tp"), P("fsdp", "tp")),
        check_vma=False,
    )
```

```python
import functools
import math

import jax
import jax.numpy as jnp
from jax import lax
from jax.experimental import pallas as pl
from jax.experimental.pallas import tpu as pltpu
from jax.sharding import PartitionSpec as P

HEADS = 64
KV = 8
HD = 128
LANES = 128
SLAB = 16
VMEM = 56 << 20


def exchange(value, axis, mask):
    return lax.ppermute(value, axis, [(i, i ^ mask) for i in range(lax.axis_size(axis))])


def own_place():
    f = lax.axis_index("fsdp")
    return f & 1, f >> 1, lax.axis_index("tp")


def transpose_blocks(arranged, mine, units, source, out, wide, tall, arrived, left):
    core, upper, t = own_place()
    width = wide.shape[2]
    rows = width // units
    side = core if mine else 1 - core
    taken, given = [], []
    for j, r in enumerate(arranged):
        start = pl.multiple_of((((r ^ upper) << 1) | side) * width, LANES)
        copy = pltpu.make_async_copy(source.at[:, pl.ds(start, width)], wide.at[j], arrived.at[j])
        copy.start()
        taken.append(copy)
    for j in range(len(arranged)):
        taken[j].wait()
        for low in range(0, width, LANES):
            tall[j, low : low + LANES, :] = wide[j, :, low : low + LANES].T
        for unit in range(units):
            place = pl.multiple_of(j * width + (unit ^ t) * rows, 32)
            copy = pltpu.make_async_copy(
                tall.at[j, pl.ds(unit * rows, rows)],
                out.at[pl.ds(place, rows)],
                left.at[j * units + unit],
            )
            copy.start()
            given.append(copy)
    for copy in given:
        copy.wait()


def pack(activations, arranged, mine, units, width):
    tokens = activations.shape[0]
    count = len(arranged)
    rows = width // units
    if width % LANES or rows % 32:
        core, upper, t = own_place()
        side = core if mine else 1 - core
        flipped = activations.T
        return jnp.concatenate(
            [
                lax.dynamic_slice_in_dim(
                    flipped, (((r ^ upper) << 1) | side) * width + (unit ^ t) * rows, rows, 0
                )
                for r in arranged
                for unit in range(units)
            ]
        )
    kind = activations.dtype
    return pl.pallas_call(
        functools.partial(transpose_blocks, arranged, mine, units),
        in_specs=[pl.BlockSpec(memory_space=pltpu.HBM)],
        out_specs=pl.BlockSpec(memory_space=pltpu.HBM),
        out_shape=jax.ShapeDtypeStruct((count * width, tokens), kind),
        scratch_shapes=[
            pltpu.VMEM((count, tokens, width), kind),
            pltpu.VMEM((count, width, tokens), kind),
            pltpu.SemaphoreType.DMA((count,)),
            pltpu.SemaphoreType.DMA((count * units,)),
        ],
        compiler_params=pltpu.CompilerParams(vmem_limit_bytes=VMEM),
        cost_estimate=pl.CostEstimate(
            flops=0, bytes_accessed=4 * count * width * tokens, transcendentals=0
        ),
    )(activations)


def runs_of(units):
    runs = []
    for unit in units:
        if runs and runs[-1][1] == unit:
            runs[-1][1] = unit + 1
        else:
            runs.append([unit, unit + 1])
    return runs


def multiply(wanted, rows, blocks, base, *refs):
    count = len(wanted)
    sources = refs[:4]
    outs = refs[4 : 4 + count]
    left, right, sems = refs[4 + count :]
    tokens = left.shape[1] // 2
    per_block = left.shape[0] // blocks
    units_block = per_block // rows
    needed = [
        block
        for block in range(blocks)
        if any(unit // units_block == block for item in wanted for unit in item[0])
    ]
    columns = pl.ds(base, right.shape[1])
    halves = [pl.ds(0, tokens), pl.ds(tokens, tokens)]
    grads, lefts = [], {}
    for at, half in enumerate(halves):
        grads.append(
            pltpu.make_async_copy(sources[2 + at].at[:, columns], right.at[half], sems.at[at])
        )
        grads[at].start()
    for block in needed:
        span = pl.ds(block * per_block, per_block)
        for at, half in enumerate(halves):
            lefts[block, at] = pltpu.make_async_copy(
                sources[at].at[span], left.at[span, half], sems.at[2 + 2 * block + at]
            )
            lefts[block, at].start()
    for copy in grads:
        copy.wait()
    for block in needed:
        for at in range(2):
            lefts[block, at].wait()
        for (units, first, last, _), out in zip(wanted, outs):
            here = [unit for unit in units if unit // units_block == block]
            for low, high in runs_of(here):
                place = units.index(low) * rows
                product = dot32(
                    left[low * rows : high * rows, :], right[:, first - base : last - base]
                )
                out[place : place + (high - low) * rows, :] = product.astype(out.dtype)


def products(lefts, grads, wanted, rows, blocks):
    total, tokens = lefts[0].shape
    base = min(first for _, first, _, _ in wanted)
    columns = max(last for _, _, last, _ in wanted) - base
    if rows % 32 or any((first | last) % LANES for _, first, last, _ in wanted):
        return [
            jnp.concatenate(
                [
                    sum(
                        dot32(left[low * rows : high * rows], grad[:, first:last])
                        for left, grad in zip(lefts, grads)
                    )
                    for low, high in runs_of(units)
                ]
            ).astype(kind)
            for units, first, last, kind in wanted
        ]
    shapes = [
        jax.ShapeDtypeStruct((len(units) * rows, last - first), kind)
        for units, first, last, kind in wanted
    ]
    return pl.pallas_call(
        functools.partial(multiply, wanted, rows, blocks, base),
        out_shape=shapes,
        in_specs=[pl.BlockSpec(memory_space=pltpu.HBM)] * 4,
        out_specs=[pl.BlockSpec(memory_space=pltpu.VMEM)] * len(shapes),
        scratch_shapes=[
            pltpu.VMEM((total, 2 * tokens), lefts[0].dtype),
            pltpu.VMEM((2 * tokens, columns), grads[0].dtype),
            pltpu.SemaphoreType.DMA((2 + 2 * blocks,)),
        ],
        compiler_params=pltpu.CompilerParams(vmem_limit_bytes=VMEM // 2),
        cost_estimate=pl.CostEstimate(flops=1, bytes_accessed=1, transcendentals=0),
    )(*lefts, *grads)


def pick_rows(arranged, units, place, table, tail, *refs):
    outs, (slabs, found, flipped, sems) = refs[:2], refs[2:]
    whole = (table.shape[0] - 1) // SLAB * SLAB
    tokens, width_all = found.shape
    width = flipped.shape[0]
    rows = width // units
    lanes = outs[0].shape[1]
    folds = lanes // tokens
    lines = rows // folds

    def slab_copy(k):
        start = pl.multiple_of(lax.div(place[k], SLAB) * SLAB, SLAB)
        return pltpu.make_async_copy(table.at[pl.ds(start, SLAB)], slabs.at[k], sems.at[k])

    def add_row(k, held):
        at = lax.broadcasted_iota(jnp.int32, held.shape, 0)
        chosen = jnp.where(at == lax.rem(place[k], SLAB), held.astype(jnp.float32), 0.0)
        found[k : k + 1, :] = jnp.sum(chosen, axis=0, keepdims=True)

    for k in range(tokens):

        @pl.when((place[k] >= 0) & (place[k] < whole))
        def _():
            slab_copy(k).start()

    found[...] = jnp.zeros_like(found)
    for k in range(tokens):

        @pl.when((place[k] >= 0) & (place[k] < whole))
        def _():
            slab_copy(k).wait()
            add_row(k, slabs[k])

        @pl.when(place[k] >= whole)
        def _():
            add_row(k, tail[...])

    core, upper, t = own_place()
    for side, out in zip((1 - core, core), outs):
        for j, r in enumerate(arranged):
            start = pl.multiple_of((((r ^ upper) << 1) | side) * width, LANES)
            flipped[...] = found[:, pl.ds(start, width)].T
            for unit in range(units):
                from_row = (unit ^ t) * rows
                pieces = [
                    flipped[pl.ds(pl.multiple_of(from_row + fold * lines, 8), lines), :]
                    for fold in range(folds)
                ]
                put = (j * units + unit) * lines
                out[put : put + lines, :] = jnp.concatenate(pieces, axis=1).astype(out.dtype)


def add_and_split(plans, *refs):
    refs = list(refs)
    takes = [[refs.pop(0) for _ in plan] + [refs.pop(0)] for plan in plans]
    gives = [[refs.pop(0) for _ in plan] + [refs.pop(0)] for plan in plans]
    for plan, inputs, outputs in zip(plans, takes, gives):
        got, sent = inputs[-1], outputs[-1]
        start = put = 0
        for (size, order, go, keep), value, kept in zip(plan, inputs, outputs):

            def sum_of(low, high):
                pieces = []
                for at in range(low, high):
                    place, lies = order[at]
                    pieces.append(
                        value[place * size : (place + 1) * size, :]
                        + got[start + lies * size : start + (lies + 1) * size, :].astype(
                            jnp.float32
                        )
                    )
                return pieces

            for at, piece in enumerate(sum_of(0, go)):
                sent[put + at * size : put + (at + 1) * size, :] = piece.astype(sent.dtype)
            for at, piece in enumerate(sum_of(go, go + keep)):
                kept[at * size : (at + 1) * size, :] = piece
            start += len(order) * size
            put += go * size


def combine(plans, values, got):
    columns = [arrived.shape[1] for arrived in got]
    outs = []
    for plan, width in zip(plans, columns):
        outs += [
            jax.ShapeDtypeStruct((keep * size, width), jnp.float32) for size, _, _, keep in plan
        ]
        total = sum(size * go for size, _, go, _ in plan)
        outs.append(jax.ShapeDtypeStruct((total, width), jnp.bfloat16))
    arrays = [array for parts, arrived in zip(values, got) for array in parts + [arrived]]
    results = pl.pallas_call(
        functools.partial(add_and_split, plans),
        in_specs=[pl.BlockSpec(memory_space=pltpu.VMEM)] * len(arrays),
        out_specs=[pl.BlockSpec(memory_space=pltpu.VMEM)] * len(outs),
        out_shape=outs,
        compiler_params=pltpu.CompilerParams(vmem_limit_bytes=VMEM // 4),
        cost_estimate=pl.CostEstimate(flops=1, bytes_accessed=1, transcendentals=0),
    )(*arrays)
    results = list(results)
    kept, sent = [], []
    for plan in plans:
        kept.append([results.pop(0) for _ in plan])
        sent.append(results.pop(0))
    return kept, sent


def fold_unit(part, lanes):
    rows, tokens = part.shape
    if tokens >= lanes:
        return jnp.concatenate([part[:, at : at + lanes] for at in range(0, tokens, lanes)])
    lines = rows * tokens // lanes
    return jnp.concatenate([part[at : at + lines] for at in range(0, rows, lines)], axis=1)


def unfold_unit(folded, rows):
    lines, lanes = folded.shape
    tokens = lines * lanes // rows
    if tokens >= lanes:
        return jnp.concatenate([folded[at : at + rows] for at in range(0, lines, rows)], axis=1)
    return jnp.concatenate([folded[:, at : at + tokens] for at in range(0, lanes, tokens)])


def lookup(embed_table, token_ids, arranged, units, width, lanes):
    here, width_all = embed_table.shape
    tokens = token_ids.shape[0]
    rows = width // units
    core, upper, t = own_place()
    inside = token_ids - (lax.axis_index("fsdp") * units + t) * here
    place = jnp.where((inside >= 0) & (inside < here), inside, -1).astype(jnp.int32)
    kind = embed_table.dtype
    if width % LANES or lanes % tokens or (rows * tokens // lanes) % 16:
        found = jnp.where(
            (place >= 0)[:, None], embed_table[jnp.maximum(place, 0)], jnp.zeros((), kind)
        )
        flipped = found.T
        return [
            jnp.concatenate(
                [
                    fold_unit(
                        lax.dynamic_slice_in_dim(
                            flipped,
                            (((r ^ upper) << 1) | side) * width + (unit ^ t) * rows,
                            rows,
                            0,
                        ),
                        lanes,
                    )
                    for r in arranged
                    for unit in range(units)
                ]
            )
            for side in (1 - core, core)
        ]
    shape = jax.ShapeDtypeStruct((len(arranged) * width * tokens // lanes, lanes), kind)
    return pl.pallas_call(
        functools.partial(pick_rows, arranged, units),
        grid=(1,),
        in_specs=[
            pl.BlockSpec(memory_space=pltpu.SMEM),
            pl.BlockSpec(memory_space=pltpu.HBM),
            pl.BlockSpec((SLAB, width_all), lambda i: ((here - 1) // SLAB, 0)),
        ],
        out_specs=[pl.BlockSpec(memory_space=pltpu.VMEM)] * 2,
        out_shape=[shape, shape],
        scratch_shapes=[
            pltpu.VMEM((tokens, SLAB, width_all), kind),
            pltpu.VMEM((tokens, width_all), jnp.float32),
            pltpu.VMEM((width, tokens), jnp.float32),
            pltpu.SemaphoreType.DMA((tokens,)),
        ],
        compiler_params=pltpu.CompilerParams(vmem_limit_bytes=VMEM // 2),
        cost_estimate=pl.CostEstimate(flops=1, bytes_accessed=1, transcendentals=0),
    )(place, embed_table, embed_table)


def dot32(left, right):
    return jnp.dot(left, right, preferred_element_type=jnp.float32)


def per_device(
    activations,
    grad_out,
    master_w,
    embed_table,
    token_ids,
    queries,
    cache_keys,
    cache_values,
    new_key,
    first_value,
    residual_mix,
    lengths,
):
    count_fsdp = lax.axis_size("fsdp")
    count_tp = lax.axis_size("tp")
    devices_all = count_fsdp * count_tp
    width = activations.shape[1]
    tokens_total = activations.shape[0] * devices_all
    coef = 1.0 / math.sqrt(tokens_total * width)
    upper_bits = count_fsdp.bit_length() - 2
    uppers = 1 << upper_bits

    block = width // count_fsdp
    rows = master_w.shape[0]
    columns = master_w.shape[1]
    arranged = [r ^ (r >> 1) for r in range(uppers)][::-1]
    grads = [grad_out, exchange(grad_out, "fsdp", 1)]
    incoming = exchange(pack(activations, arranged, False, count_tp, block), "fsdp", 1)
    staying = pack(activations, arranged, True, count_tp, block)
    lefts = [staying, incoming]
    tokens_new = token_ids.shape[0]
    quarter = columns // 4
    eighth = columns // 8
    lines = rows * tokens_new // eighth

    places = [(r, unit) for r in arranged for unit in range(count_tp)]
    steps_upper = [("fsdp", bit) for bit in range(upper_bits)]
    steps_tp = [("tp", bit) for bit in range(count_tp.bit_length() - 1)]
    one, two, three = (
        steps_upper + steps_tp,
        steps_upper[::-1] + steps_tp,
        steps_tp + steps_upper,
    )
    edges = [0, quarter, 2 * quarter, 3 * quarter, 3 * quarter + eighth, columns]
    spans = list(zip(edges[:-1], edges[1:]))
    orders = [one, two, three, one, two]

    def has(place, step):
        return (place[step[0] == "tp"] >> step[1]) & 1

    def flip(place, step):
        mask = 1 << step[1]
        return (place[0], place[1] ^ mask) if step[0] == "tp" else (place[0] ^ mask, place[1])

    def split(held, step):
        return [p for p in held if has(p, step)], [p for p in held if not has(p, step)]

    def take(value, held, chosen, size):
        runs = runs_of([held.index(p) for p in chosen])
        return jnp.concatenate([value[low * size : high * size] for low, high in runs])

    def send(value, step):
        mask = 1 << step[1]
        return exchange(value, step[0], 2 * mask if step[0] == "fsdp" else mask)

    def compute(which, sent, factors):
        wanted = []
        for index in which:
            chosen = split(places, orders[index][0])[0 if sent else 1]
            units = [places.index(p) for p in chosen]
            kind = jnp.bfloat16 if sent else jnp.float32
            wanted.append((units, *spans[index], kind))
        return dict(zip(which, products(factors, grads, wanted, rows, uppers)))

    going = compute([2, 0, 1], True, lefts)
    got = {index: send(value, orders[index][0]) for index, value in going.items()}
    going |= compute([3, 4], True, lefts)
    got[3] = send(going[3], orders[3][0])

    theirs, ours = lookup(embed_table, token_ids, arranged, count_tp, block, eighth)
    asked = ours + exchange(theirs, "fsdp", 1)
    go, stay = split(places, orders[4][0])
    values = compute([0, 1, 2], False, lefts)
    token = jnp.concatenate([going[4], take(asked, places, go, lines)])
    got[4] = send(token, orders[4][0])
    values |= compute([3, 4], False, lefts)
    values = {index: [value] for index, value in values.items()}
    values[4].append(take(asked, places, stay, lines).astype(jnp.float32))
    sizes = {index: [rows] for index in range(5)}
    sizes[4].append(lines)
    held = {index: places for index in range(5)}

    def receive(index, step):
        gone, kept = split(held[index], step)
        landed = [flip(p, step) for p in gone]
        start = 0
        added = []
        for value, size in zip(values[index], sizes[index]):
            piece = got[index][start : start + len(gone) * size]
            start += len(gone) * size
            added.append(value + take(piece, landed, kept, size).astype(jnp.float32))
        values[index], held[index] = added, kept

    def forward(index, step, following):
        gone, kept = split(held[index], step)
        landed = [flip(p, step) for p in gone]
        go, keep = split(kept, following)
        plan = [
            (size, [(held_now[index].index(p), landed.index(p)) for p in go + keep], len(go), len(keep))
            for size in sizes[index]
        ]
        held[index], held_now[index] = kept, keep
        return plan

    held_now = {
        index: split(places, orders[index][0])[1] for index in range(5)
    }
    plain = rows % 32 or any(size % 16 for size in sizes[4])
    for at in range(len(one)):
        for group in ((0, 1), (2,), (3, 4)):
            tied = lax.optimization_barrier([got[index] for index in group] + [token])
            for index, arrived in zip(group, tied):
                got[index] = arrived
            if at + 1 == len(one):
                for index in group:
                    receive(index, orders[index][at])
                continue
            if plain:
                outgoing = []
                for index in group:
                    receive(index, orders[index][at])
                    gone, kept = split(held[index], orders[index][at + 1])
                    pieces = [
                        take(value, held[index], gone, size).astype(jnp.bfloat16)
                        for value, size in zip(values[index], sizes[index])
                    ]
                    values[index] = [
                        take(value, held[index], kept, size)
                        for value, size in zip(values[index], sizes[index])
                    ]
                    outgoing.append(jnp.concatenate(pieces))
            else:
                plans = [forward(i, orders[i][at], orders[i][at + 1]) for i in group]
                kept, outgoing = combine(
                    plans, [values[i] for i in group], [got[i] for i in group]
                )
                for index, value in zip(group, kept):
                    values[index] = value
            outgoing = lax.optimization_barrier(outgoing)
            token = outgoing[-1]
            for index, value in zip(group, outgoing):
                got[index] = send(value, orders[index][at + 1])
    w_next = jnp.concatenate(
        [master_w[:, low:high] - coef * values[at][0] for at, (low, high) in enumerate(spans)],
        axis=1,
    )

    columns_own = unfold_unit(values[4][1].astype(jnp.bfloat16), rows)
    share_own = lax.dot_general(
        columns_own,
        w_next.astype(jnp.bfloat16),
        (((0,), (0,)), ((), ())),
        preferred_element_type=jnp.float32,
    )
    rows_f = tokens_new // count_fsdp
    col_width = columns // count_tp
    blocks_own = (
        share_own.reshape(count_fsdp, rows_f, count_tp, col_width)
        .transpose(0, 2, 1, 3)
        .reshape(devices_all, rows_f, col_width)
    )
    own_value = jnp.sum(
        lax.all_to_all(blocks_own, ("fsdp", "tp"), split_axis=0, concat_axis=0), axis=0
    )

    share = jnp.repeat(residual_mix, HD)[None, :]
    new_value = (share * own_value + (1.0 - share) * first_value.astype(jnp.float32)).astype(
        jnp.bfloat16
    )
    rows = queries.shape[0]
    heads_kv = residual_mix.shape[0]
    group = HEADS // KV
    context = cache_keys.shape[1]
    scale = 1.0 / math.sqrt(HD)
    query_b = queries.reshape(rows, heads_kv, group, HD)
    keys_b = cache_keys.reshape(rows, context, heads_kv, HD)
    vals_b = cache_values.reshape(rows, context, heads_kv, HD)
    newk_b = new_key.reshape(rows, heads_kv, HD)
    newv_b = new_value.reshape(rows, heads_kv, HD)
    scores = (
        jnp.einsum("rkgd,rckd->rkgc", query_b, keys_b, preferred_element_type=jnp.float32) * scale
    )
    fresh = jnp.einsum("rkgd,rkd->rkg", query_b, newk_b, preferred_element_type=jnp.float32) * scale
    valid = jnp.arange(context, dtype=jnp.int32)[None, :] < lengths[:, None]
    scores = jnp.where(valid[:, None, None, :], scores, -1e30)
    peak = jnp.maximum(jnp.max(scores, axis=-1), fresh)
    expo = jnp.exp(scores - peak[..., None])
    expo_new = jnp.exp(fresh - peak)
    total = jnp.sum(expo, axis=-1) + expo_new
    probs = (expo / total[..., None]).astype(jnp.bfloat16)
    probs_new = (expo_new / total).astype(jnp.bfloat16)
    mixed = lax.optimization_barrier(
        jnp.einsum("rkgc,rckd->rkgd", probs, vals_b, preferred_element_type=jnp.float32)
    )
    mixed = (
        mixed + probs_new.astype(jnp.float32)[..., None] * newv_b.astype(jnp.float32)[:, :, None, :]
    )
    attended = mixed.reshape(rows, group * heads_kv * HD).astype(jnp.bfloat16)
    return (w_next, new_value, attended)


def solution(mesh):
    return jax.shard_map(
        per_device,
        mesh=mesh,
        in_specs=(
            P(("fsdp", "tp"), None),
            P(("fsdp", "tp"), None),
            P(("fsdp", "tp"), None),
            P(("fsdp", "tp"), None),
            P(),
            P("fsdp", "tp"),
            P("fsdp", None, "tp"),
            P("fsdp", None, "tp"),
            P("fsdp", "tp"),
            P("fsdp", "tp"),
            P("tp"),
            P("fsdp"),
        ),
        out_specs=(P(("fsdp", "tp"), None), P("fsdp", "tp"), P("fsdp", "tp")),
        check_vma=False,
    )
```

```python
import functools
import math

import jax
import jax.numpy as jnp
from jax import lax
from jax.experimental import pallas as pl
from jax.experimental.pallas import tpu as pltpu
from jax.sharding import PartitionSpec as P

HEADS = 64
KV = 8
HD = 128
LANES = 128
SLAB = 16
VMEM = 56 << 20


def exchange(value, axis, mask):
    return lax.ppermute(value, axis, [(i, i ^ mask) for i in range(lax.axis_size(axis))])


def own_place():
    f = lax.axis_index("fsdp")
    return f & 1, f >> 1, lax.axis_index("tp")


def transpose_blocks(arranged, mine, units, source, out, wide, tall, arrived, left):
    core, upper, t = own_place()
    width = wide.shape[2]
    rows = width // units
    side = core if mine else 1 - core
    taken, given = [], []
    for j, r in enumerate(arranged):
        start = pl.multiple_of((((r ^ upper) << 1) | side) * width, LANES)
        copy = pltpu.make_async_copy(source.at[:, pl.ds(start, width)], wide.at[j], arrived.at[j])
        copy.start()
        taken.append(copy)
    for j in range(len(arranged)):
        taken[j].wait()
        for low in range(0, width, LANES):
            tall[j, low : low + LANES, :] = wide[j, :, low : low + LANES].T
        for unit in range(units):
            place = pl.multiple_of(j * width + (unit ^ t) * rows, 32)
            copy = pltpu.make_async_copy(
                tall.at[j, pl.ds(unit * rows, rows)],
                out.at[pl.ds(place, rows)],
                left.at[j * units + unit],
            )
            copy.start()
            given.append(copy)
    for copy in given:
        copy.wait()


def pack(activations, arranged, mine, units, width):
    tokens = activations.shape[0]
    count = len(arranged)
    rows = width // units
    if width % LANES or rows % 32:
        core, upper, t = own_place()
        side = core if mine else 1 - core
        flipped = activations.T
        return jnp.concatenate(
            [
                lax.dynamic_slice_in_dim(
                    flipped, (((r ^ upper) << 1) | side) * width + (unit ^ t) * rows, rows, 0
                )
                for r in arranged
                for unit in range(units)
            ]
        )
    kind = activations.dtype
    return pl.pallas_call(
        functools.partial(transpose_blocks, arranged, mine, units),
        in_specs=[pl.BlockSpec(memory_space=pltpu.HBM)],
        out_specs=pl.BlockSpec(memory_space=pltpu.HBM),
        out_shape=jax.ShapeDtypeStruct((count * width, tokens), kind),
        scratch_shapes=[
            pltpu.VMEM((count, tokens, width), kind),
            pltpu.VMEM((count, width, tokens), kind),
            pltpu.SemaphoreType.DMA((count,)),
            pltpu.SemaphoreType.DMA((count * units,)),
        ],
        compiler_params=pltpu.CompilerParams(vmem_limit_bytes=VMEM),
        cost_estimate=pl.CostEstimate(
            flops=0, bytes_accessed=4 * count * width * tokens, transcendentals=0
        ),
    )(activations)


def runs_of(units):
    runs = []
    for unit in units:
        if runs and runs[-1][1] == unit:
            runs[-1][1] = unit + 1
        else:
            runs.append([unit, unit + 1])
    return runs


def multiply(wanted, rows, blocks, base, staged, *refs):
    count = len(wanted)
    sources = refs[:4]
    outs = refs[4 : 4 + count]
    left, right, sems = refs[4 + count : 7 + count]
    stages, given = refs[7 + count : -1] if staged else outs, []
    tokens = left.shape[1] // 2
    per_block = left.shape[0] // blocks
    units_block = per_block // rows
    needed = [
        block
        for block in range(blocks)
        if any(unit // units_block == block for item in wanted for unit in item[0])
    ]
    columns = pl.ds(base, right.shape[1])
    halves = [pl.ds(0, tokens), pl.ds(tokens, tokens)]
    grads, lefts = [], {}
    for at, half in enumerate(halves):
        grads.append(
            pltpu.make_async_copy(sources[2 + at].at[:, columns], right.at[half], sems.at[at])
        )
        grads[at].start()
    for block in needed:
        span = pl.ds(block * per_block, per_block)
        for at, half in enumerate(halves):
            lefts[block, at] = pltpu.make_async_copy(
                sources[at].at[span], left.at[span, half], sems.at[2 + 2 * block + at]
            )
            lefts[block, at].start()
    for copy in grads:
        copy.wait()
    for block in needed:
        for at in range(2):
            lefts[block, at].wait()
        for at, (units, first, last, _) in enumerate(wanted):
            here = [unit for unit in units if unit // units_block == block]
            for low, high in runs_of(here):
                place = units.index(low) * rows
                product = dot32(
                    left[low * rows : high * rows, :], right[:, first - base : last - base]
                )
                stages[at][place : place + (high - low) * rows, :] = product.astype(outs[at].dtype)
            if staged and here:
                span = pl.ds(units.index(here[0]) * rows, len(here) * rows)
                copy = pltpu.make_async_copy(
                    stages[at].at[span], outs[at].at[span], refs[-1].at[block, at]
                )
                copy.start()
                given.append(copy)
    for copy in given:
        copy.wait()


def products(lefts, grads, wanted, rows, blocks, staged):
    total, tokens = lefts[0].shape
    base = min(first for _, first, _, _ in wanted)
    columns = max(last for _, _, last, _ in wanted) - base
    if rows % 32 or any((first | last) % LANES for _, first, last, _ in wanted):
        return [
            jnp.concatenate(
                [
                    sum(
                        dot32(left[low * rows : high * rows], grad[:, first:last])
                        for left, grad in zip(lefts, grads)
                    )
                    for low, high in runs_of(units)
                ]
            ).astype(kind)
            for units, first, last, kind in wanted
        ]
    shapes = [
        jax.ShapeDtypeStruct((len(units) * rows, last - first), kind)
        for units, first, last, kind in wanted
    ]
    staging = []
    if staged:
        staging = [pltpu.VMEM(shape.shape, shape.dtype) for shape in shapes]
        staging.append(pltpu.SemaphoreType.DMA((blocks, len(shapes))))
    return pl.pallas_call(
        functools.partial(multiply, wanted, rows, blocks, base, staged),
        out_shape=shapes,
        in_specs=[pl.BlockSpec(memory_space=pltpu.HBM)] * 4,
        out_specs=[pl.BlockSpec(memory_space=pltpu.HBM if staged else pltpu.VMEM)] * len(shapes),
        scratch_shapes=[
            pltpu.VMEM((total, 2 * tokens), lefts[0].dtype),
            pltpu.VMEM((2 * tokens, columns), grads[0].dtype),
            pltpu.SemaphoreType.DMA((2 + 2 * blocks,)),
        ]
        + staging,
        compiler_params=pltpu.CompilerParams(vmem_limit_bytes=62 << 20 if staged else VMEM // 2),
        cost_estimate=pl.CostEstimate(flops=1, bytes_accessed=1, transcendentals=0),
    )(*lefts, *grads)


def pick_rows(arranged, units, place, table, tail, *refs):
    outs, (slabs, found, flipped, sems) = refs[:2], refs[2:]
    whole = (table.shape[0] - 1) // SLAB * SLAB
    tokens, width_all = found.shape
    width = flipped.shape[0]
    rows = width // units
    lanes = outs[0].shape[1]
    folds = lanes // tokens
    lines = rows // folds

    def slab_copy(k):
        start = pl.multiple_of(lax.div(place[k], SLAB) * SLAB, SLAB)
        return pltpu.make_async_copy(table.at[pl.ds(start, SLAB)], slabs.at[k], sems.at[k])

    def add_row(k, held):
        at = lax.broadcasted_iota(jnp.int32, held.shape, 0)
        chosen = jnp.where(at == lax.rem(place[k], SLAB), held.astype(jnp.float32), 0.0)
        found[k : k + 1, :] = jnp.sum(chosen, axis=0, keepdims=True)

    for k in range(tokens):

        @pl.when((place[k] >= 0) & (place[k] < whole))
        def _():
            slab_copy(k).start()

    found[...] = jnp.zeros_like(found)
    for k in range(tokens):

        @pl.when(place[k] >= 0)
        def _():
            @pl.when(place[k] < whole)
            def _():
                slab_copy(k).wait()
                add_row(k, slabs[k])

            @pl.when(place[k] >= whole)
            def _():
                add_row(k, tail[...])

    core, upper, t = own_place()
    for side, out in zip((1 - core, core), outs):
        for j, r in enumerate(arranged):
            start = pl.multiple_of((((r ^ upper) << 1) | side) * width, LANES)
            flipped[...] = found[:, pl.ds(start, width)].T
            for unit in range(units):
                from_row = (unit ^ t) * rows
                pieces = [
                    flipped[pl.ds(pl.multiple_of(from_row + fold * lines, 8), lines), :]
                    for fold in range(folds)
                ]
                put = (j * units + unit) * lines
                out[put : put + lines, :] = jnp.concatenate(pieces, axis=1).astype(out.dtype)


def add_and_split(plans, arrays, merged, *refs):
    refs = list(refs)
    takes = [[refs.pop(0) for _ in plan] for plan in plans]
    inbox = [refs.pop(0) for _ in range(arrays)]
    gives = [[refs.pop(0) for _ in plan] for plan in plans]
    start = put = 0
    for at_plan, (plan, inputs, outputs) in enumerate(zip(plans, takes, gives)):
        got, sent = inbox[min(at_plan, arrays - 1)], refs[0 if merged else at_plan]
        if arrays > 1:
            start = 0
        if not merged:
            put = 0
        for (size, order, go, keep), value, kept in zip(plan, inputs, outputs):

            def sum_of(low, high):
                pieces = []
                for at in range(low, high):
                    place, lies = order[at]
                    pieces.append(
                        value[place * size : (place + 1) * size, :]
                        + got[start + lies * size : start + (lies + 1) * size, :].astype(
                            jnp.float32
                        )
                    )
                return pieces

            for at, piece in enumerate(sum_of(0, go)):
                sent[put + at * size : put + (at + 1) * size, :] = piece.astype(sent.dtype)
            for at, piece in enumerate(sum_of(go, go + keep)):
                kept[at * size : (at + 1) * size, :] = piece
            start += len(order) * size
            put += go * size


def combine(plans, values, got, merged):
    columns = [parts[0].shape[1] for parts in values]
    totals = [sum(size * go for size, _, go, _ in plan) for plan in plans]
    outs = [
        jax.ShapeDtypeStruct((keep * size, width), jnp.float32)
        for plan, width in zip(plans, columns)
        for size, _, _, keep in plan
    ]
    if merged:
        outs.append(jax.ShapeDtypeStruct((sum(totals), columns[0]), jnp.bfloat16))
    else:
        for total, width in zip(totals, columns):
            outs.append(jax.ShapeDtypeStruct((total, width), jnp.bfloat16))
    arrays = [array for parts in values for array in parts] + list(got)
    results = pl.pallas_call(
        functools.partial(add_and_split, plans, len(got), merged),
        in_specs=[pl.BlockSpec(memory_space=pltpu.VMEM)] * len(arrays),
        out_specs=[pl.BlockSpec(memory_space=pltpu.VMEM)] * len(outs),
        out_shape=outs,
        compiler_params=pltpu.CompilerParams(vmem_limit_bytes=VMEM // 4),
        cost_estimate=pl.CostEstimate(flops=1, bytes_accessed=1, transcendentals=0),
    )(*arrays)
    results = list(results)
    kept = [[results.pop(0) for _ in plan] for plan in plans]
    return kept, results, totals


def fold_unit(part, lanes):
    rows, tokens = part.shape
    if tokens >= lanes:
        return jnp.concatenate([part[:, at : at + lanes] for at in range(0, tokens, lanes)])
    lines = rows * tokens // lanes
    return jnp.concatenate([part[at : at + lines] for at in range(0, rows, lines)], axis=1)


def unfold_unit(folded, rows):
    lines, lanes = folded.shape
    tokens = lines * lanes // rows
    if tokens >= lanes:
        return jnp.concatenate([folded[at : at + rows] for at in range(0, lines, rows)], axis=1)
    return jnp.concatenate([folded[:, at : at + tokens] for at in range(0, lanes, tokens)])


def lookup(embed_table, token_ids, arranged, units, width, lanes):
    here, width_all = embed_table.shape
    tokens = token_ids.shape[0]
    rows = width // units
    core, upper, t = own_place()
    inside = token_ids - (lax.axis_index("fsdp") * units + t) * here
    place = jnp.where((inside >= 0) & (inside < here), inside, -1).astype(jnp.int32)
    kind = embed_table.dtype
    if width % LANES or lanes % tokens or (rows * tokens // lanes) % 16:
        found = jnp.where(
            (place >= 0)[:, None], embed_table[jnp.maximum(place, 0)], jnp.zeros((), kind)
        )
        flipped = found.T
        return [
            jnp.concatenate(
                [
                    fold_unit(
                        lax.dynamic_slice_in_dim(
                            flipped,
                            (((r ^ upper) << 1) | side) * width + (unit ^ t) * rows,
                            rows,
                            0,
                        ),
                        lanes,
                    )
                    for r in arranged
                    for unit in range(units)
                ]
            )
            for side in (1 - core, core)
        ]
    shape = jax.ShapeDtypeStruct((len(arranged) * width * tokens // lanes, lanes), kind)
    return pl.pallas_call(
        functools.partial(pick_rows, arranged, units),
        grid=(1,),
        in_specs=[
            pl.BlockSpec(memory_space=pltpu.SMEM),
            pl.BlockSpec(memory_space=pltpu.HBM),
            pl.BlockSpec((SLAB, width_all), lambda i: ((here - 1) // SLAB, 0)),
        ],
        out_specs=[pl.BlockSpec(memory_space=pltpu.VMEM)] * 2,
        out_shape=[shape, shape],
        scratch_shapes=[
            pltpu.VMEM((tokens, SLAB, width_all), kind),
            pltpu.VMEM((tokens, width_all), jnp.float32),
            pltpu.VMEM((width, tokens), jnp.float32),
            pltpu.SemaphoreType.DMA((tokens,)),
        ],
        compiler_params=pltpu.CompilerParams(vmem_limit_bytes=VMEM // 2),
        cost_estimate=pl.CostEstimate(flops=1, bytes_accessed=1, transcendentals=0),
    )(place, embed_table, embed_table)


def dot32(left, right):
    return jnp.dot(left, right, preferred_element_type=jnp.float32)


def per_device(
    activations,
    grad_out,
    master_w,
    embed_table,
    token_ids,
    queries,
    cache_keys,
    cache_values,
    new_key,
    first_value,
    residual_mix,
    lengths,
):
    count_fsdp = lax.axis_size("fsdp")
    count_tp = lax.axis_size("tp")
    devices_all = count_fsdp * count_tp
    width = activations.shape[1]
    tokens_total = activations.shape[0] * devices_all
    coef = 1.0 / math.sqrt(tokens_total * width)
    upper_bits = count_fsdp.bit_length() - 2
    uppers = 1 << upper_bits

    block = width // count_fsdp
    rows = master_w.shape[0]
    columns = master_w.shape[1]
    arranged = [r ^ (r >> 1) for r in range(uppers)][::-1]
    grads = [grad_out, exchange(grad_out, "fsdp", 1)]
    incoming = exchange(pack(activations, arranged, False, count_tp, block), "fsdp", 1)
    staying = pack(activations, arranged, True, count_tp, block)
    lefts = [staying, incoming]
    tokens_new = token_ids.shape[0]
    quarter = columns // 4
    eighth = columns // 8
    lines = rows * tokens_new // eighth

    places = [(r, unit) for r in arranged for unit in range(count_tp)]
    steps_upper = [("fsdp", bit) for bit in range(upper_bits)]
    steps_tp = [("tp", bit) for bit in range(count_tp.bit_length() - 1)]
    one, two, three = (
        steps_upper + steps_tp,
        steps_upper[::-1] + steps_tp,
        steps_tp[:1] + steps_upper + steps_tp[1:],
    )
    edges = [0, quarter, 2 * quarter, 3 * quarter, 3 * quarter + eighth, columns]
    spans = list(zip(edges[:-1], edges[1:]))
    orders = [one, two, three, one, two]

    def has(place, step):
        return (place[step[0] == "tp"] >> step[1]) & 1

    def flip(place, step):
        mask = 1 << step[1]
        return (place[0], place[1] ^ mask) if step[0] == "tp" else (place[0] ^ mask, place[1])

    def split(held, step):
        return [p for p in held if has(p, step)], [p for p in held if not has(p, step)]

    def take(value, held, chosen, size):
        runs = runs_of([held.index(p) for p in chosen])
        return jnp.concatenate([value[low * size : high * size] for low, high in runs])

    def send(value, step):
        mask = 1 << step[1]
        return exchange(value, step[0], 2 * mask if step[0] == "fsdp" else mask)

    def compute(which, sent):
        wanted = []
        for index in which:
            chosen = split(places, orders[index][0])[0 if sent else 1]
            units = [places.index(p) for p in chosen]
            kind = jnp.bfloat16 if sent else jnp.float32
            wanted.append((units, *spans[index], kind))
        return dict(zip(which, products(lefts, grads, wanted, rows, uppers, sent)))

    going = compute([2, 0, 1], True)
    got = {index: send(value, orders[index][0]) for index, value in going.items()}
    going |= compute([3, 4], True)
    got[3] = send(going[3], orders[3][0])

    theirs, ours = lookup(embed_table, token_ids, arranged, count_tp, block, eighth)
    asked = ours + exchange(theirs, "fsdp", 1)
    go, stay = split(places, orders[4][0])
    values = compute([0, 1, 2], False)
    token = jnp.concatenate([going[4], take(asked, places, go, lines)])
    got[4] = send(token, orders[4][0])
    values |= compute([3, 4], False)
    values = {index: [value] for index, value in values.items()}
    values[4].append(take(asked, places, stay, lines).astype(jnp.float32))
    sizes = {index: [rows] for index in range(5)}
    sizes[4].append(lines)
    held = {index: places for index in range(5)}

    def receive(index, step):
        gone, kept = split(held[index], step)
        landed = [flip(p, step) for p in gone]
        start = 0
        added = []
        for value, size in zip(values[index], sizes[index]):
            piece = got[index][start : start + len(gone) * size]
            start += len(gone) * size
            added.append(value + take(piece, landed, kept, size).astype(jnp.float32))
        values[index], held[index] = added, kept

    def forward(index, step, following):
        gone, kept = split(held[index], step)
        landed = [flip(p, step) for p in gone]
        go, keep = split(kept, following)
        plan = [
            (size, [(held_now[index].index(p), landed.index(p)) for p in go + keep], len(go), len(keep))
            for size in sizes[index]
        ]
        held[index], held_now[index] = kept, keep
        return plan

    held_now = {
        index: split(places, orders[index][0])[1] for index in range(5)
    }
    plain = rows % 32 or any(size % 16 for size in sizes[4])
    groups = ((0, 1), (2,), (3, 4))
    inbox = {group: [got[index] for index in group] for group in groups}
    totals = {}
    for at in range(len(one)):
        for group in groups:
            *inbox[group], token = lax.optimization_barrier(inbox[group] + [token])
            last = at + 1 == len(one)
            if plain or last:
                if len(inbox[group]) < len(group):
                    whole = inbox[group][0]
                    cuts = [sum(totals[group][:place]) for place in range(len(group) + 1)]
                    inbox[group] = [whole[low:high] for low, high in zip(cuts[:-1], cuts[1:])]
                for index, arrived in zip(group, inbox[group]):
                    got[index] = arrived
                    receive(index, orders[index][at])
            if last:
                token = values[group[-1]][0]
                continue
            if plain:
                outgoing = []
                for index in group:
                    gone, kept = split(held[index], orders[index][at + 1])
                    pieces = [
                        take(value, held[index], gone, size).astype(jnp.bfloat16)
                        for value, size in zip(values[index], sizes[index])
                    ]
                    values[index] = [
                        take(value, held[index], kept, size)
                        for value, size in zip(values[index], sizes[index])
                    ]
                    outgoing.append(jnp.concatenate(pieces))
            else:
                plans = [forward(i, orders[i][at], orders[i][at + 1]) for i in group]
                merged = len({orders[i][at + 1] for i in group}) == 1
                kept, outgoing, totals[group] = combine(
                    plans, [values[i] for i in group], inbox[group], merged
                )
                values |= dict(zip(group, kept))
            outgoing = lax.optimization_barrier(outgoing)
            token = outgoing[-1]
            inbox[group] = [
                send(value, orders[index][at + 1]) for index, value in zip(group, outgoing)
            ]
    w_next = jnp.concatenate(
        [master_w[:, low:high] - coef * values[at][0] for at, (low, high) in enumerate(spans)],
        axis=1,
    )

    columns_own = unfold_unit(values[4][1].astype(jnp.bfloat16), rows)
    share_own = lax.dot_general(
        columns_own,
        w_next.astype(jnp.bfloat16),
        (((0,), (0,)), ((), ())),
        preferred_element_type=jnp.float32,
    )
    rows_f = tokens_new // count_fsdp
    col_width = columns // count_tp
    blocks_own = (
        share_own.astype(jnp.bfloat16)
        .reshape(count_fsdp, rows_f, count_tp, col_width)
        .transpose(0, 2, 1, 3)
        .reshape(devices_all, rows_f, col_width)
    )
    parts_own = lax.all_to_all(blocks_own, ("fsdp", "tp"), split_axis=0, concat_axis=0)
    own_value = jnp.sum(parts_own.astype(jnp.float32), axis=0)

    share = jnp.repeat(residual_mix, HD)[None, :]
    new_value = (share * own_value + (1.0 - share) * first_value.astype(jnp.float32)).astype(
        jnp.bfloat16
    )
    rows = queries.shape[0]
    heads_kv = residual_mix.shape[0]
    group = HEADS // KV
    context = cache_keys.shape[1]
    scale = 1.0 / math.sqrt(HD)
    query_b = queries.reshape(rows, heads_kv, group, HD)
    keys_b = cache_keys.reshape(rows, context, heads_kv, HD)
    vals_b = cache_values.reshape(rows, context, heads_kv, HD)
    newk_b = new_key.reshape(rows, heads_kv, HD)
    newv_b = new_value.reshape(rows, heads_kv, HD)
    scores = (
        jnp.einsum("rkgd,rckd->rkgc", query_b, keys_b, preferred_element_type=jnp.float32) * scale
    )
    fresh = jnp.einsum("rkgd,rkd->rkg", query_b, newk_b, preferred_element_type=jnp.float32) * scale
    valid = jnp.arange(context, dtype=jnp.int32)[None, :] < lengths[:, None]
    scores = jnp.where(valid[:, None, None, :], scores, -1e30)
    peak = jnp.maximum(jnp.max(scores, axis=-1), fresh)
    expo = jnp.exp(scores - peak[..., None])
    expo_new = jnp.exp(fresh - peak)
    total = jnp.sum(expo, axis=-1) + expo_new
    probs = (expo / total[..., None]).astype(jnp.bfloat16)
    probs_new = (expo_new / total).astype(jnp.bfloat16)
    mixed = lax.optimization_barrier(
        jnp.einsum("rkgc,rckd->rkgd", probs, vals_b, preferred_element_type=jnp.float32)
    )
    mixed = (
        mixed + probs_new.astype(jnp.float32)[..., None] * newv_b.astype(jnp.float32)[:, :, None, :]
    )
    attended = mixed.reshape(rows, group * heads_kv * HD).astype(jnp.bfloat16)
    return (w_next, new_value, attended)


def solution(mesh):
    return jax.shard_map(
        per_device,
        mesh=mesh,
        in_specs=(
            P(("fsdp", "tp"), None),
            P(("fsdp", "tp"), None),
            P(("fsdp", "tp"), None),
            P(("fsdp", "tp"), None),
            P(),
            P("fsdp", "tp"),
            P("fsdp", None, "tp"),
            P("fsdp", None, "tp"),
            P("fsdp", "tp"),
            P("fsdp", "tp"),
            P("tp"),
            P("fsdp"),
        ),
        out_specs=(P(("fsdp", "tp"), None), P("fsdp", "tp"), P("fsdp", "tp")),
        check_vma=False,
    )
```

```python
import functools
import math

import jax
import jax.numpy as jnp
from jax import lax
from jax.experimental import pallas as pl
from jax.experimental.pallas import tpu as pltpu
from jax.sharding import PartitionSpec as P

HEADS = 64
KV = 8
HD = 128
LANES = 128
SLAB = 16
VMEM = 56 << 20


def exchange(value, axis, mask):
    return lax.ppermute(value, axis, [(i, i ^ mask) for i in range(lax.axis_size(axis))])


def own_place():
    f = lax.axis_index("fsdp")
    return f & 1, f >> 1, lax.axis_index("tp")


def transpose_blocks(arranged, mine, units, source, out, wide, tall, arrived, left):
    core, upper, t = own_place()
    width = wide.shape[2]
    rows = width // units
    side = core if mine else 1 - core
    taken, given = [], []
    for j, r in enumerate(arranged):
        start = pl.multiple_of((((r ^ upper) << 1) | side) * width, LANES)
        copy = pltpu.make_async_copy(source.at[:, pl.ds(start, width)], wide.at[j], arrived.at[j])
        copy.start()
        taken.append(copy)
    for j in range(len(arranged)):
        taken[j].wait()
        for low in range(0, width, LANES):
            tall[j, low : low + LANES, :] = wide[j, :, low : low + LANES].T
        for unit in range(units):
            place = pl.multiple_of(j * width + (unit ^ t) * rows, 32)
            copy = pltpu.make_async_copy(
                tall.at[j, pl.ds(unit * rows, rows)],
                out.at[pl.ds(place, rows)],
                left.at[j * units + unit],
            )
            copy.start()
            given.append(copy)
    for copy in given:
        copy.wait()


def pack(activations, arranged, mine, units, width):
    tokens = activations.shape[0]
    count = len(arranged)
    rows = width // units
    if width % LANES or rows % 32:
        core, upper, t = own_place()
        side = core if mine else 1 - core
        flipped = activations.T
        return jnp.concatenate(
            [
                lax.dynamic_slice_in_dim(
                    flipped, (((r ^ upper) << 1) | side) * width + (unit ^ t) * rows, rows, 0
                )
                for r in arranged
                for unit in range(units)
            ]
        )
    kind = activations.dtype
    return pl.pallas_call(
        functools.partial(transpose_blocks, arranged, mine, units),
        in_specs=[pl.BlockSpec(memory_space=pltpu.HBM)],
        out_specs=pl.BlockSpec(memory_space=pltpu.HBM),
        out_shape=jax.ShapeDtypeStruct((count * width, tokens), kind),
        scratch_shapes=[
            pltpu.VMEM((count, tokens, width), kind),
            pltpu.VMEM((count, width, tokens), kind),
            pltpu.SemaphoreType.DMA((count,)),
            pltpu.SemaphoreType.DMA((count * units,)),
        ],
        compiler_params=pltpu.CompilerParams(vmem_limit_bytes=VMEM),
        cost_estimate=pl.CostEstimate(
            flops=0, bytes_accessed=4 * count * width * tokens, transcendentals=0
        ),
    )(activations)


def runs_of(units):
    runs = []
    for unit in units:
        if runs and runs[-1][1] == unit:
            runs[-1][1] = unit + 1
        else:
            runs.append([unit, unit + 1])
    return runs


def multiply(wanted, rows, blocks, base, staged, tail, *refs):
    count = len(wanted)
    sources = refs[:4]
    if tail:
        appended, refs = refs[4], refs[:4] + refs[5:]
    outs = refs[4 : 4 + count]
    left, right, sems = refs[4 + count : 7 + count]
    stages, given = refs[7 + count : -1] if staged else outs, []
    tokens = left.shape[1] // 2
    per_block = left.shape[0] // blocks
    units_block = per_block // rows
    needed = [
        block
        for block in range(blocks)
        if any(unit // units_block == block for item in wanted for unit in item[0])
    ]
    columns = pl.ds(base, right.shape[1])
    halves = [pl.ds(0, tokens), pl.ds(tokens, tokens)]
    grads, lefts = [], {}
    for at, half in enumerate(halves):
        grads.append(
            pltpu.make_async_copy(sources[2 + at].at[:, columns], right.at[half], sems.at[at])
        )
        grads[at].start()
    for block in needed:
        span = pl.ds(block * per_block, per_block)
        for at, half in enumerate(halves):
            lefts[block, at] = pltpu.make_async_copy(
                sources[at].at[span], left.at[span, half], sems.at[2 + 2 * block + at]
            )
            lefts[block, at].start()
    if tail:
        given.append(
            pltpu.make_async_copy(
                appended.at[pl.ds(tail, tail)],
                outs[0].at[pl.ds(len(wanted[0][0]) * rows, tail)],
                refs[-1].at[blocks, 0],
            )
        )
        given[0].start()
    for copy in grads:
        copy.wait()
    for block in needed:
        for at in range(2):
            lefts[block, at].wait()
        for at, (units, first, last, _) in enumerate(wanted):
            here = [unit for unit in units if unit // units_block == block]
            for low, high in runs_of(here):
                place = units.index(low) * rows
                product = dot32(
                    left[low * rows : high * rows, :], right[:, first - base : last - base]
                )
                stages[at][place : place + (high - low) * rows, :] = product.astype(outs[at].dtype)
            if staged and here:
                span = pl.ds(units.index(here[0]) * rows, len(here) * rows)
                copy = pltpu.make_async_copy(
                    stages[at].at[span], outs[at].at[span], refs[-1].at[block, at]
                )
                copy.start()
                given.append(copy)
    for copy in given:
        copy.wait()


def products(lefts, grads, wanted, rows, blocks, staged, appended=None):
    total, tokens = lefts[0].shape
    base = min(first for _, first, _, _ in wanted)
    columns = max(last for _, _, last, _ in wanted) - base
    if rows % 32 or any((first | last) % LANES for _, first, last, _ in wanted):
        results = [
            jnp.concatenate(
                [
                    sum(
                        dot32(left[low * rows : high * rows], grad[:, first:last])
                        for left, grad in zip(lefts, grads)
                    )
                    for low, high in runs_of(units)
                ]
            ).astype(kind)
            for units, first, last, kind in wanted
        ]
        if appended is not None:
            results[0] = jnp.concatenate([results[0], appended[appended.shape[0] // 2 :]])
        return results
    tail = 0 if appended is None else appended.shape[0] // 2
    shapes = [
        jax.ShapeDtypeStruct((len(units) * rows, last - first), kind)
        for units, first, last, kind in wanted
    ]
    staging = []
    if staged:
        staging = [pltpu.VMEM(shape.shape, shape.dtype) for shape in shapes]
        staging.append(pltpu.SemaphoreType.DMA((blocks + 1, len(shapes))))
    if tail:
        grown = (shapes[0].shape[0] + tail, shapes[0].shape[1])
        shapes[0] = jax.ShapeDtypeStruct(grown, shapes[0].dtype)
    return pl.pallas_call(
        functools.partial(multiply, wanted, rows, blocks, base, staged, tail),
        out_shape=shapes,
        in_specs=[pl.BlockSpec(memory_space=pltpu.HBM)] * (5 if tail else 4),
        out_specs=[pl.BlockSpec(memory_space=pltpu.HBM if staged else pltpu.VMEM)] * len(shapes),
        scratch_shapes=[
            pltpu.VMEM((total, 2 * tokens), lefts[0].dtype),
            pltpu.VMEM((2 * tokens, columns), grads[0].dtype),
            pltpu.SemaphoreType.DMA((2 + 2 * blocks,)),
        ]
        + staging,
        compiler_params=pltpu.CompilerParams(vmem_limit_bytes=127 << 19 if staged else VMEM // 2),
        cost_estimate=pl.CostEstimate(flops=1, bytes_accessed=1, transcendentals=0),
    )(*lefts, *grads, *([appended] if tail else []))


def pick_rows(arranged, units, place, table, tail, *refs):
    outs, (slabs, found, flipped, sems) = refs[:2], refs[2:]
    whole = (table.shape[0] - 1) // SLAB * SLAB
    tokens, width_all = found.shape
    width = flipped.shape[0]
    rows = width // units
    lanes = outs[0].shape[1]
    lanes = lanes // 2
    folds = lanes // tokens
    lines = rows // folds

    def slab_copy(k):
        start = pl.multiple_of(lax.div(place[k], SLAB) * SLAB, SLAB)
        return pltpu.make_async_copy(table.at[pl.ds(start, SLAB)], slabs.at[k], sems.at[k])

    def add_row(k, held):
        at = lax.broadcasted_iota(jnp.int32, held.shape, 0)
        chosen = jnp.where(at == lax.rem(place[k], SLAB), held.astype(jnp.float32), 0.0)
        found[k : k + 1, :] = jnp.sum(chosen, axis=0, keepdims=True)

    for k in range(tokens):

        @pl.when((place[k] >= 0) & (place[k] < whole))
        def _():
            slab_copy(k).start()

    found[...] = jnp.zeros_like(found)
    for k in range(tokens):

        @pl.when(place[k] >= 0)
        def _():
            @pl.when(place[k] < whole)
            def _():
                slab_copy(k).wait()
                add_row(k, slabs[k])

            @pl.when(place[k] >= whole)
            def _():
                add_row(k, tail[...])

    core, upper, t = own_place()
    for side, out in zip((1 - core, core), outs):
        for j, r in enumerate(arranged):
            start = pl.multiple_of((((r ^ upper) << 1) | side) * width, LANES)
            flipped[...] = found[:, pl.ds(start, width)].T
            for unit in range(units):
                from_row = (unit ^ t) * rows
                pieces = [
                    flipped[pl.ds(pl.multiple_of(from_row + fold * lines, 8), lines), :]
                    for fold in range(folds)
                ]
                put = ((unit & 1) * len(arranged) + j) * lines
                side_lanes = slice((unit >> 1) * lanes, ((unit >> 1) + 1) * lanes)
                out[put : put + lines, side_lanes] = jnp.concatenate(pieces, axis=1).astype(
                    out.dtype
                )


def add_and_split(plans, arrays, merged, *refs):
    refs = list(refs)
    takes = [[refs.pop(0) for _ in plan] for plan in plans]
    inbox = [refs.pop(0) for _ in range(arrays)]
    gives = [[refs.pop(0) for _ in plan] for plan in plans]
    start = put = 0
    for at_plan, (plan, inputs, outputs) in enumerate(zip(plans, takes, gives)):
        got, sent = inbox[min(at_plan, arrays - 1)], refs[0 if merged else at_plan]
        if arrays > 1:
            start = 0
        if not merged:
            put = 0
        for (size, order, go, keep, have), value, kept in zip(plan, inputs, outputs):

            def sum_of(low, high):
                pieces = []
                for at in range(low, high):
                    place, lies = order[at]
                    pieces.append(
                        value[place * size : (place + 1) * size, :]
                        + got[start + lies * size : start + (lies + 1) * size, :].astype(
                            jnp.float32
                        )
                    )
                return pieces

            for at, piece in enumerate(sum_of(0, go)):
                sent[put + at * size : put + (at + 1) * size, :] = piece.astype(sent.dtype)
            for at, piece in enumerate(sum_of(go, go + keep)):
                kept[at * size : (at + 1) * size, :] = piece
            start += have * size
            put += go * size


def combine(plans, values, got, merged):
    columns = [parts[0].shape[1] for parts in values]
    totals = [sum(size * go for size, _, go, _, _ in plan) for plan in plans]
    outs = [
        jax.ShapeDtypeStruct((keep * size, width), jnp.float32)
        for plan, width in zip(plans, columns)
        for size, _, _, keep, _ in plan
    ]
    if merged:
        outs.append(jax.ShapeDtypeStruct((sum(totals), columns[0]), jnp.bfloat16))
    else:
        for total, width in zip(totals, columns):
            outs.append(jax.ShapeDtypeStruct((total, width), jnp.bfloat16))
    arrays = [array for parts in values for array in parts] + list(got)
    results = pl.pallas_call(
        functools.partial(add_and_split, plans, len(got), merged),
        in_specs=[pl.BlockSpec(memory_space=pltpu.VMEM)] * len(arrays),
        out_specs=[pl.BlockSpec(memory_space=pltpu.VMEM)] * len(outs),
        out_shape=outs,
        compiler_params=pltpu.CompilerParams(vmem_limit_bytes=VMEM // 4),
        cost_estimate=pl.CostEstimate(flops=1, bytes_accessed=1, transcendentals=0),
    )(*arrays)
    results = list(results)
    kept = [[results.pop(0) for _ in plan] for plan in plans]
    return kept, results, totals


def own_share(coef, spans, plans, rows, tokens, blocks, *refs):
    emb, master, out = refs[0], refs[1], refs[-1]
    arrays = refs[2:-1]
    lanes = emb.shape[1] // blocks
    count_fsdp = tokens // out.shape[1]
    col_width = out.shape[2]
    folded = emb[...].astype(jnp.bfloat16)
    lefts = [
        jnp.concatenate(
            [
                folded[:, unit * lanes + at : unit * lanes + at + tokens]
                for at in range(0, lanes, tokens)
            ]
        )
        for unit in range(blocks)
    ]

    def both(left, right):
        high = right.astype(jnp.bfloat16)
        total = across(left, high)
        if right.dtype == jnp.float32:
            total += across(left, (right - high.astype(jnp.float32)).astype(jnp.bfloat16))
        return total

    pieces = []
    for (first, last), plan in zip(spans, plans):
        moved = jnp.zeros((tokens, last - first), jnp.float32)
        for array, units in plan:
            for at, unit in enumerate(units):
                moved += both(lefts[unit], arrays[array][at * rows : (at + 1) * rows, :])
        pieces.append(both(lefts[0], master[:, first:last]) - coef * moved)
    share = jnp.concatenate(pieces, axis=1)
    for f in range(count_fsdp):
        for t in range(out.shape[0] // count_fsdp):
            out[f * (out.shape[0] // count_fsdp) + t] = share[
                f * out.shape[1] : (f + 1) * out.shape[1], t * col_width : (t + 1) * col_width
            ]


def across(left, right):
    return lax.dot_general(
        left, right, (((0,), (0,)), ((), ())), preferred_element_type=jnp.float32
    )


def fold_unit(part, lanes):
    rows, tokens = part.shape
    if tokens >= lanes:
        return jnp.concatenate([part[:, at : at + lanes] for at in range(0, tokens, lanes)])
    lines = rows * tokens // lanes
    return jnp.concatenate([part[at : at + lines] for at in range(0, rows, lines)], axis=1)


def unfold_unit(folded, rows):
    lines, lanes = folded.shape
    tokens = lines * lanes // rows
    if tokens >= lanes:
        return jnp.concatenate([folded[at : at + rows] for at in range(0, lines, rows)], axis=1)
    return jnp.concatenate([folded[:, at : at + tokens] for at in range(0, lanes, tokens)])


def lookup(embed_table, token_ids, arranged, units, width, lanes):
    here, width_all = embed_table.shape
    tokens = token_ids.shape[0]
    rows = width // units
    core, upper, t = own_place()
    inside = token_ids - (lax.axis_index("fsdp") * units + t) * here
    place = jnp.where((inside >= 0) & (inside < here), inside, -1).astype(jnp.int32)
    kind = embed_table.dtype
    if width % LANES or lanes % tokens or (rows * tokens // lanes) % 16:
        found = jnp.where(
            (place >= 0)[:, None], embed_table[jnp.maximum(place, 0)], jnp.zeros((), kind)
        )
        flipped = found.T

        def folded(r, side, unit):
            start = (((r ^ upper) << 1) | side) * width + (unit ^ t) * rows
            return fold_unit(lax.dynamic_slice_in_dim(flipped, start, rows, 0), lanes)

        return [
            jnp.concatenate(
                [
                    jnp.concatenate(
                        [folded(r, side, unit) for unit in range(low, units, 2)], axis=1
                    )
                    for low in range(2)
                    for r in arranged
                ]
            )
            for side in (1 - core, core)
        ]
    shape = jax.ShapeDtypeStruct((len(arranged) * width * tokens // lanes // 2, 2 * lanes), kind)
    return pl.pallas_call(
        functools.partial(pick_rows, arranged, units),
        grid=(1,),
        in_specs=[
            pl.BlockSpec(memory_space=pltpu.SMEM),
            pl.BlockSpec(memory_space=pltpu.HBM),
            pl.BlockSpec((SLAB, width_all), lambda i: ((here - 1) // SLAB, 0)),
        ],
        out_specs=[pl.BlockSpec(memory_space=pltpu.VMEM)] * 2,
        out_shape=[shape, shape],
        scratch_shapes=[
            pltpu.VMEM((tokens, SLAB, width_all), kind),
            pltpu.VMEM((tokens, width_all), jnp.float32),
            pltpu.VMEM((width, tokens), jnp.float32),
            pltpu.SemaphoreType.DMA((tokens,)),
        ],
        compiler_params=pltpu.CompilerParams(vmem_limit_bytes=VMEM // 2),
        cost_estimate=pl.CostEstimate(flops=1, bytes_accessed=1, transcendentals=0),
    )(place, embed_table, embed_table)


def dot32(left, right):
    return jnp.dot(left, right, preferred_element_type=jnp.float32)


def per_device(
    activations,
    grad_out,
    master_w,
    embed_table,
    token_ids,
    queries,
    cache_keys,
    cache_values,
    new_key,
    first_value,
    residual_mix,
    lengths,
):
    count_fsdp = lax.axis_size("fsdp")
    count_tp = lax.axis_size("tp")
    devices_all = count_fsdp * count_tp
    width = activations.shape[1]
    tokens_total = activations.shape[0] * devices_all
    coef = 1.0 / math.sqrt(tokens_total * width)
    upper_bits = count_fsdp.bit_length() - 2
    uppers = 1 << upper_bits

    block = width // count_fsdp
    rows = master_w.shape[0]
    columns = master_w.shape[1]
    arranged = [r ^ (r >> 1) for r in range(uppers)][::-1]
    grads = [grad_out, exchange(grad_out, "fsdp", 1)]
    incoming = exchange(pack(activations, arranged, False, count_tp, block), "fsdp", 1)
    staying = pack(activations, arranged, True, count_tp, block)
    lefts = [staying, incoming]
    tokens_new = token_ids.shape[0]
    quarter = columns // 4
    eighth = columns // 8
    lines = rows * tokens_new // eighth

    places = [(r, unit) for r in arranged for unit in range(count_tp)]
    steps_upper = [("fsdp", bit) for bit in range(upper_bits)]
    steps_tp = [("tp", bit) for bit in range(count_tp.bit_length() - 1)]
    one, two, three = (
        steps_upper + steps_tp,
        steps_upper[::-1] + steps_tp,
        steps_tp[:1] + steps_upper + steps_tp[1:],
    )
    edges = [0, quarter, 2 * quarter, 3 * quarter, 3 * quarter + eighth, columns]
    spans = list(zip(edges[:-1], edges[1:]))
    orders = [one, two, three, one, two]

    def has(place, step):
        return (place[step[0] == "tp"] >> step[1]) & 1

    def flip(place, step):
        mask = 1 << step[1]
        return (place[0], place[1] ^ mask) if step[0] == "tp" else (place[0] ^ mask, place[1])

    def split(held, step):
        return [p for p in held if has(p, step)], [p for p in held if not has(p, step)]

    def take(value, held, chosen, size):
        runs = runs_of([held.index(p) for p in chosen])
        return jnp.concatenate([value[low * size : high * size] for low, high in runs])

    def send(value, step):
        mask = 1 << step[1]
        return exchange(value, step[0], 2 * mask if step[0] == "fsdp" else mask)

    def compute(which, sent, appended=None):
        wanted = []
        for index in which:
            chosen = split(places, orders[index][0])[0 if sent else 1]
            units = [places.index(p) for p in chosen]
            kind = jnp.bfloat16 if sent else jnp.float32
            wanted.append((units, *spans[index], kind))
        return dict(zip(which, products(lefts, grads, wanted, rows, uppers, sent, appended)))

    theirs, ours = lookup(embed_table, token_ids, arranged, count_tp, block, eighth)
    asked = ours + exchange(theirs, "fsdp", 1)
    pairs = [(r, low) for low in range(2) for r in arranged]
    going = compute([0, 1], True)
    got = {index: send(value, orders[index][0]) for index, value in going.items()}
    going |= compute([2, 3, 4], True, asked)
    got |= {index: send(going[index], orders[index][0]) for index in (3, 4, 2)}
    token = going[4]
    values = compute([0, 1, 2], False)
    values |= compute([3, 4], False)
    values = {index: [value] for index, value in values.items()}
    values[2].append(asked[: asked.shape[0] // 2].astype(jnp.float32))
    sizes = {index: [rows] for index in range(5)}
    sizes[2].append(lines)
    held = {index: [split(places, orders[index][0])[1]] for index in range(5)}
    held[2].append(split(pairs, orders[2][0])[1])
    gone = {index: [split(places, orders[index][0])[0]] for index in range(5)}
    gone[2].append(split(pairs, orders[2][0])[0])

    def receive(index, step, arrived):
        start = 0
        for part, (value, size) in enumerate(zip(values[index], sizes[index])):
            landed = [flip(p, step) for p in gone[index][part]]
            piece = arrived[start : start + len(landed) * size]
            start += len(landed) * size
            if part and step == last_tp:
                piece = jnp.roll(piece, piece.shape[1] // 2, axis=1)
            else:
                piece = take(piece, landed, held[index][part], size)
            values[index][part] = value + piece.astype(jnp.float32)

    def onward(index, step):
        return [
            (places_now, places_now) if part and step == last_tp else split(places_now, step)
            for part, places_now in enumerate(held[index])
        ]

    def forward(index, step, following):
        plan = []
        for part, (go, keep) in enumerate(onward(index, following)):
            landed = [flip(p, step) for p in gone[index][part]]
            order = [(held[index][part].index(p), landed.index(p)) for p in go + keep]
            plan.append((sizes[index][part], order, len(go), len(keep), len(landed)))
        return plan

    last_tp = steps_tp[-1]
    rows_f = tokens_new // count_fsdp
    col_width = columns // count_tp

    def share_of(sums, emb):
        if plain:
            lefts_own = [
                unfold_unit(emb[:, at * eighth : (at + 1) * eighth], rows) for at in range(2)
            ]

            def exact(left, right):
                return lax.dot_general(
                    left.astype(jnp.float32),
                    right.astype(jnp.float32),
                    (((0,), (0,)), ((), ())),
                    precision=lax.Precision.HIGHEST,
                )

            pieces = []
            for index, (first, last) in enumerate(spans):
                moved = sum(exact(left, array) for left, array in zip(lefts_own, sums[index]))
                pieces.append(exact(lefts_own[0], master_w[:, first:last]) - coef * moved)
            out = jnp.concatenate(pieces, axis=1)
            out = out.reshape(count_fsdp, rows_f, count_tp, col_width)
            out = out.transpose(0, 2, 1, 3).reshape(devices_all, rows_f, col_width)
            return out.astype(jnp.bfloat16)
        arrays = [array for index in range(5) for array in sums[index]]
        plans = [[(2 * index, [0]), (2 * index + 1, [1])] for index in range(5)]
        return pl.pallas_call(
            functools.partial(own_share, coef, spans, plans, rows, tokens_new, 2),
            in_specs=[pl.BlockSpec(memory_space=pltpu.VMEM)] * (2 + len(arrays)),
            out_specs=pl.BlockSpec(memory_space=pltpu.VMEM),
            out_shape=jax.ShapeDtypeStruct((devices_all, rows_f, col_width), jnp.float32),
            compiler_params=pltpu.CompilerParams(vmem_limit_bytes=VMEM // 4),
            cost_estimate=pl.CostEstimate(flops=1, bytes_accessed=1, transcendentals=0),
        )(emb, master_w, *arrays).astype(jnp.bfloat16)

    plain = rows % 32 or lines % 16 or block % LANES or eighth % tokens_new
    groups = ((0, 1), (2,), (3, 4))
    inbox = {group: [got[index] for index in group] for group in groups}
    totals = {}
    sums = {}
    steps = len(one)
    for at in range(steps):
        last = at + 1 == steps
        for group in ((2,), (0, 1), (3, 4)) if last else groups:
            *inbox[group], token = lax.optimization_barrier(inbox[group] + [token])
            if plain or last:
                if len(inbox[group]) < len(group):
                    whole = inbox[group][0]
                    cuts = [sum(totals[group][:place]) for place in range(len(group) + 1)]
                    inbox[group] = [whole[low:high] for low, high in zip(cuts[:-1], cuts[1:])]
                for index, arrived in zip(group, inbox[group]):
                    receive(index, orders[index][at], arrived)
            if last:
                token = values[group[-1]][0]
                if group == (2,):
                    parts_own, token = lax.optimization_barrier(
                        (share_of(sums, values[2][1]), token)
                    )
                    token = parts_own
                    parts_own = lax.all_to_all(
                        parts_own, ("fsdp", "tp"), split_axis=0, concat_axis=0
                    )
                continue
            if plain:
                outgoing = []
                for index in group:
                    pieces = []
                    for part, (go, keep) in enumerate(onward(index, orders[index][at + 1])):
                        value, size = values[index][part], sizes[index][part]
                        pieces.append(take(value, held[index][part], go, size))
                        values[index][part] = take(value, held[index][part], keep, size)
                    outgoing.append(jnp.concatenate(pieces).astype(jnp.bfloat16))
                totals[group] = [value.shape[0] for value in outgoing]
                merged = False
            else:
                plans = [forward(i, orders[i][at], orders[i][at + 1]) for i in group]
                merged = len({orders[i][at + 1] for i in group}) == 1
                kept, outgoing, totals[group] = combine(
                    plans, [values[i] for i in group], inbox[group], merged
                )
                values |= dict(zip(group, kept))
            for number, index in enumerate(group):
                now = onward(index, orders[index][at + 1])
                gone[index], held[index] = [list(parts) for parts in zip(*now)]
                if at + 2 == steps:
                    low = sum(totals[group][:number]) if merged else 0
                    sent = outgoing[0 if merged else number]
                    sums[index] = [values[index][0], sent[low : low + rows]]
            outgoing = lax.optimization_barrier(outgoing)
            token = outgoing[-1]
            inbox[group] = [
                send(value, orders[index][at + 1]) for index, value in zip(group, outgoing)
            ]
            if at == 1 and group == groups[0]:
                queries, new_key, lengths, token = lax.optimization_barrier(
                    (queries, new_key, lengths, token)
                )
    parts_own, _ = lax.optimization_barrier((parts_own, values[4][0]))
    own_value = jnp.sum(parts_own.astype(jnp.float32), axis=0)
    w_next = jnp.concatenate(
        [master_w[:, low:high] - coef * values[at][0] for at, (low, high) in enumerate(spans)],
        axis=1,
    )

    share = jnp.repeat(residual_mix, HD)[None, :]
    new_value = (share * own_value + (1.0 - share) * first_value.astype(jnp.float32)).astype(
        jnp.bfloat16
    )
    rows = queries.shape[0]
    heads_kv = residual_mix.shape[0]
    group = HEADS // KV
    context = cache_keys.shape[1]
    scale = 1.0 / math.sqrt(HD)
    query_b = queries.reshape(rows, heads_kv, group, HD)
    keys_b = cache_keys.reshape(rows, context, heads_kv, HD)
    vals_b = cache_values.reshape(rows, context, heads_kv, HD)
    newk_b = new_key.reshape(rows, heads_kv, HD)
    newv_b = new_value.reshape(rows, heads_kv, HD)
    scores = (
        jnp.einsum("rkgd,rckd->rkgc", query_b, keys_b, preferred_element_type=jnp.float32) * scale
    )
    fresh = jnp.einsum("rkgd,rkd->rkg", query_b, newk_b, preferred_element_type=jnp.float32) * scale
    valid = jnp.arange(context, dtype=jnp.int32)[None, :] < lengths[:, None]
    scores = jnp.where(valid[:, None, None, :], scores, -1e30)
    peak = jnp.maximum(jnp.max(scores, axis=-1), fresh)
    expo = jnp.exp(scores - peak[..., None])
    expo_new = jnp.exp(fresh - peak)
    total = jnp.sum(expo, axis=-1) + expo_new
    probs = (expo / total[..., None]).astype(jnp.bfloat16)
    probs_new = (expo_new / total).astype(jnp.bfloat16)
    mixed = lax.optimization_barrier(
        jnp.einsum("rkgc,rckd->rkgd", probs, vals_b, preferred_element_type=jnp.float32)
    )
    mixed = (
        mixed + probs_new.astype(jnp.float32)[..., None] * newv_b.astype(jnp.float32)[:, :, None, :]
    )
    attended = mixed.reshape(rows, group * heads_kv * HD).astype(jnp.bfloat16)
    return (w_next, new_value, attended)


def solution(mesh):
    return jax.shard_map(
        per_device,
        mesh=mesh,
        in_specs=(
            P(("fsdp", "tp"), None),
            P(("fsdp", "tp"), None),
            P(("fsdp", "tp"), None),
            P(("fsdp", "tp"), None),
            P(),
            P("fsdp", "tp"),
            P("fsdp", None, "tp"),
            P("fsdp", None, "tp"),
            P("fsdp", "tp"),
            P("fsdp", "tp"),
            P("tp"),
            P("fsdp"),
        ),
        out_specs=(P(("fsdp", "tp"), None), P("fsdp", "tp"), P("fsdp", "tp")),
        check_vma=False,
    )
```

```python
import functools
import math

import jax
import jax.numpy as jnp
from jax import lax
from jax.experimental import pallas as pl
from jax.experimental.pallas import tpu as pltpu
from jax.sharding import PartitionSpec as P

HEADS = 64
KV = 8
HD = 128
LANES = 128
SLAB = 16
VMEM = 56 << 20


def exchange(value, axis, mask):
    return lax.ppermute(value, axis, [(i, i ^ mask) for i in range(lax.axis_size(axis))])


def own_place():
    f = lax.axis_index("fsdp")
    return f & 1, f >> 1, lax.axis_index("tp")


def transpose_blocks(arranged, mine, units, source, out, wide, tall, arrived, left):
    core, upper, t = own_place()
    width = wide.shape[2]
    rows = width // units
    side = core if mine else 1 - core
    taken, given = [], []
    for j, r in enumerate(arranged):
        start = pl.multiple_of((((r ^ upper) << 1) | side) * width, LANES)
        copy = pltpu.make_async_copy(source.at[:, pl.ds(start, width)], wide.at[j], arrived.at[j])
        copy.start()
        taken.append(copy)
    for j in range(len(arranged)):
        taken[j].wait()
        for low in range(0, width, LANES):
            tall[j, low : low + LANES, :] = wide[j, :, low : low + LANES].T
        for unit in range(units):
            place = pl.multiple_of(j * width + (unit ^ t) * rows, 32)
            copy = pltpu.make_async_copy(
                tall.at[j, pl.ds(unit * rows, rows)],
                out.at[pl.ds(place, rows)],
                left.at[j * units + unit],
            )
            copy.start()
            given.append(copy)
    for copy in given:
        copy.wait()


def pack(activations, arranged, mine, units, width):
    tokens = activations.shape[0]
    count = len(arranged)
    rows = width // units
    if width % LANES or rows % 32:
        core, upper, t = own_place()
        side = core if mine else 1 - core
        flipped = activations.T
        return jnp.concatenate(
            [
                lax.dynamic_slice_in_dim(
                    flipped, (((r ^ upper) << 1) | side) * width + (unit ^ t) * rows, rows, 0
                )
                for r in arranged
                for unit in range(units)
            ]
        )
    kind = activations.dtype
    return pl.pallas_call(
        functools.partial(transpose_blocks, arranged, mine, units),
        in_specs=[pl.BlockSpec(memory_space=pltpu.HBM)],
        out_specs=pl.BlockSpec(memory_space=pltpu.HBM),
        out_shape=jax.ShapeDtypeStruct((count * width, tokens), kind),
        scratch_shapes=[
            pltpu.VMEM((count, tokens, width), kind),
            pltpu.VMEM((count, width, tokens), kind),
            pltpu.SemaphoreType.DMA((count,)),
            pltpu.SemaphoreType.DMA((count * units,)),
        ],
        compiler_params=pltpu.CompilerParams(vmem_limit_bytes=VMEM),
        cost_estimate=pl.CostEstimate(
            flops=0, bytes_accessed=4 * count * width * tokens, transcendentals=0
        ),
    )(activations)


def runs_of(units):
    runs = []
    for unit in units:
        if runs and runs[-1][1] == unit:
            runs[-1][1] = unit + 1
        else:
            runs.append([unit, unit + 1])
    return runs


def multiply(wanted, rows, blocks, base, after, *refs):
    count = len(wanted)
    sources = refs[:4]
    refs = refs[:4] + refs[4 + after :]
    outs = refs[4 : 4 + count]
    left, right, sems, given_sems = refs[4 + count : 8 + count]
    spare, given = list(refs[8 + count :]), []
    stages = [spare.pop(0) if item[3] == jnp.bfloat16 else out for item, out in zip(wanted, outs)]
    tokens = left.shape[1] // 2
    per_block = left.shape[0] // blocks
    units_block = per_block // rows
    needed = [
        block
        for block in range(blocks)
        if any(unit // units_block == block for item in wanted for unit in item[0])
    ]
    columns = pl.ds(base, right.shape[1])
    halves = [pl.ds(0, tokens), pl.ds(tokens, tokens)]
    grads, lefts = [], {}
    for at, half in enumerate(halves):
        grads.append(
            pltpu.make_async_copy(sources[2 + at].at[:, columns], right.at[half], sems.at[at])
        )
        grads[at].start()
    for block in needed:
        span = pl.ds(block * per_block, per_block)
        for at, half in enumerate(halves):
            lefts[block, at] = pltpu.make_async_copy(
                sources[at].at[span], left.at[span, half], sems.at[2 + 2 * block + at]
            )
            lefts[block, at].start()
    for copy in grads:
        copy.wait()
    for block in needed:
        for at in range(2):
            lefts[block, at].wait()
        for at, (units, first, last, _) in enumerate(wanted):
            here = [unit for unit in units if unit // units_block == block]
            for low, high in runs_of(here):
                place = units.index(low) * rows
                product = dot32(
                    left[low * rows : high * rows, :], right[:, first - base : last - base]
                )
                stages[at][place : place + (high - low) * rows, :] = product.astype(outs[at].dtype)
            if here and stages[at] is not outs[at]:
                span = pl.ds(units.index(here[0]) * rows, len(here) * rows)
                copy = pltpu.make_async_copy(
                    stages[at].at[span], outs[at].at[span], given_sems.at[block, at]
                )
                copy.start()
                given.append(copy)
    for copy in given:
        copy.wait()


def products(lefts, grads, wanted, rows, blocks, after, limit):
    total, tokens = lefts[0].shape
    base = min(first for _, first, _, _ in wanted)
    columns = max(last for _, _, last, _ in wanted) - base
    if rows % 32 or any((first | last) % LANES for _, first, last, _ in wanted):
        return [
            jnp.concatenate(
                [
                    sum(
                        dot32(left[low * rows : high * rows], grad[:, first:last])
                        for left, grad in zip(lefts, grads)
                    )
                    for low, high in runs_of(units)
                ]
            ).astype(kind)
            for units, first, last, kind in wanted
        ]
    shapes = [
        jax.ShapeDtypeStruct((len(units) * rows, last - first), kind)
        for units, first, last, kind in wanted
    ]
    sent = [item[3] == jnp.bfloat16 for item in wanted]
    staging = [pltpu.VMEM(shape.shape, shape.dtype) for shape, is_sent in zip(shapes, sent) if is_sent]
    return pl.pallas_call(
        functools.partial(multiply, wanted, rows, blocks, base, len(after)),
        out_shape=shapes,
        in_specs=[pl.BlockSpec(memory_space=pltpu.HBM)] * 4
        + [pl.BlockSpec(memory_space=pl.ANY)] * len(after),
        out_specs=[
            pl.BlockSpec(memory_space=pltpu.HBM if is_sent else pltpu.VMEM) for is_sent in sent
        ],
        scratch_shapes=[
            pltpu.VMEM((total, 2 * tokens), lefts[0].dtype),
            pltpu.VMEM((2 * tokens, columns), grads[0].dtype),
            pltpu.SemaphoreType.DMA((2 + 2 * blocks,)),
            pltpu.SemaphoreType.DMA((blocks, len(shapes))),
        ]
        + staging,
        compiler_params=pltpu.CompilerParams(vmem_limit_bytes=limit),
        cost_estimate=pl.CostEstimate(flops=1, bytes_accessed=1, transcendentals=0),
    )(*lefts, *grads, *after)


def pick_rows(arranged, units, place, table, tail, _, *refs):
    outs, (slabs, found, flipped, sems) = refs[:2], refs[2:]
    whole = (table.shape[0] - 1) // SLAB * SLAB
    tokens, width_all = found.shape
    width = flipped.shape[0]
    rows = width // units
    lanes = outs[0].shape[1]
    lanes = lanes // 2
    folds = lanes // tokens
    lines = rows // folds

    def slab_copy(k):
        start = pl.multiple_of(lax.div(place[k], SLAB) * SLAB, SLAB)
        return pltpu.make_async_copy(table.at[pl.ds(start, SLAB)], slabs.at[k], sems.at[k])

    def add_row(k, held):
        at = lax.broadcasted_iota(jnp.int32, held.shape, 0)
        chosen = jnp.where(at == lax.rem(place[k], SLAB), held.astype(jnp.float32), 0.0)
        found[k : k + 1, :] = jnp.sum(chosen, axis=0, keepdims=True)

    for k in range(tokens):

        @pl.when((place[k] >= 0) & (place[k] < whole))
        def _():
            slab_copy(k).start()

    found[...] = jnp.zeros_like(found)
    for k in range(tokens):

        @pl.when(place[k] >= 0)
        def _():
            @pl.when(place[k] < whole)
            def _():
                slab_copy(k).wait()
                add_row(k, slabs[k])

            @pl.when(place[k] >= whole)
            def _():
                add_row(k, tail[...])

    core, upper, t = own_place()
    for side, out in zip((1 - core, core), outs):
        for j, r in enumerate(arranged):
            start = pl.multiple_of((((r ^ upper) << 1) | side) * width, LANES)
            flipped[...] = found[:, pl.ds(start, width)].T
            for unit in range(units):
                from_row = (unit ^ t) * rows
                pieces = [
                    flipped[pl.ds(pl.multiple_of(from_row + fold * lines, 8), lines), :]
                    for fold in range(folds)
                ]
                put = ((unit & 1) * len(arranged) + j) * lines
                side_lanes = slice((unit >> 1) * lanes, ((unit >> 1) + 1) * lanes)
                out[put : put + lines, side_lanes] = jnp.concatenate(pieces, axis=1).astype(
                    out.dtype
                )


def add_and_split(plans, arrays, merged, after, *refs):
    refs = list(refs[after:])
    takes = [[refs.pop(0) for _ in plan] for plan in plans]
    inbox = [refs.pop(0) for _ in range(arrays)]
    gives = [[refs.pop(0) for _ in plan] for plan in plans]
    start = put = 0
    for at_plan, (plan, inputs, outputs) in enumerate(zip(plans, takes, gives)):
        got, sent = inbox[min(at_plan, arrays - 1)], refs[0 if merged else at_plan]
        if arrays > 1:
            start = 0
        if not merged:
            put = 0
        for (size, order, go, keep, have), value, kept in zip(plan, inputs, outputs):

            def sum_of(low, high):
                pieces = []
                for at in range(low, high):
                    place, lies = order[at]
                    pieces.append(
                        value[place * size : (place + 1) * size, :]
                        + got[start + lies * size : start + (lies + 1) * size, :].astype(
                            jnp.float32
                        )
                    )
                return pieces

            for at, piece in enumerate(sum_of(0, go)):
                sent[put + at * size : put + (at + 1) * size, :] = piece.astype(sent.dtype)
            for at, piece in enumerate(sum_of(go, go + keep)):
                kept[at * size : (at + 1) * size, :] = piece
            start += have * size
            put += go * size


def combine(plans, values, got, merged, after):
    columns = [parts[0].shape[1] for parts in values]
    totals = [sum(size * go for size, _, go, _, _ in plan) for plan in plans]
    outs = [
        jax.ShapeDtypeStruct((keep * size, width), jnp.float32)
        for plan, width in zip(plans, columns)
        for size, _, _, keep, _ in plan
    ]
    if merged:
        outs.append(jax.ShapeDtypeStruct((sum(totals), columns[0]), jnp.bfloat16))
    else:
        for total, width in zip(totals, columns):
            outs.append(jax.ShapeDtypeStruct((total, width), jnp.bfloat16))
    arrays = [array for parts in values for array in parts] + list(got)
    results = pl.pallas_call(
        functools.partial(add_and_split, plans, len(got), merged, len(after)),
        in_specs=[pl.BlockSpec(memory_space=pl.ANY)] * len(after)
        + [pl.BlockSpec(memory_space=pltpu.VMEM)] * len(arrays),
        out_specs=[pl.BlockSpec(memory_space=pltpu.VMEM)] * len(outs),
        out_shape=outs,
        compiler_params=pltpu.CompilerParams(vmem_limit_bytes=VMEM // 4),
        cost_estimate=pl.CostEstimate(flops=1, bytes_accessed=1, transcendentals=0),
    )(*after, *arrays)
    results = list(results)
    kept = [[results.pop(0) for _ in plan] for plan in plans]
    return kept, results, totals


def own_share(coef, spans, plans, rows, tokens, _, *refs):
    emb, emb_got, master, out = refs[0], refs[1], refs[2], refs[-1]
    arrays = refs[3:-1]
    lines, lanes = emb.shape[0] // 2, emb.shape[1] // 2
    count_fsdp = tokens // out.shape[1]
    col_width = out.shape[2]
    arrived = emb_got[...].astype(jnp.float32)
    swapped = jnp.concatenate([arrived[:, lanes:], arrived[:, :lanes]], axis=1)
    folded = (emb[...] + swapped).astype(jnp.bfloat16)
    lefts = [
        jnp.concatenate(
            [
                folded[(unit & 1) * lines : ((unit & 1) + 1) * lines, at : at + tokens]
                for at in range((unit >> 1) * lanes, ((unit >> 1) + 1) * lanes, tokens)
            ]
        )
        for unit in range(4)
    ]

    def both(left, right):
        high = right.astype(jnp.bfloat16)
        total = across(left, high)
        if right.dtype == jnp.float32:
            total += across(left, (right - high.astype(jnp.float32)).astype(jnp.bfloat16))
        return total

    pieces = []
    for (first, last), plan in zip(spans, plans):
        moved = jnp.zeros((tokens, last - first), jnp.float32)
        for array, units in plan:
            for at, unit in enumerate(units):
                moved += both(lefts[unit], arrays[array][at * rows : (at + 1) * rows, :])
        pieces.append(both(lefts[0], master[:, first:last]) - coef * moved)
    share = jnp.concatenate(pieces, axis=1)
    for f in range(count_fsdp):
        for t in range(out.shape[0] // count_fsdp):
            out[f * (out.shape[0] // count_fsdp) + t] = share[
                f * out.shape[1] : (f + 1) * out.shape[1], t * col_width : (t + 1) * col_width
            ]


def add_parts(_, parts, out):
    out[...] = jnp.sum(parts[...].astype(jnp.float32), axis=0)


def across(left, right):
    return lax.dot_general(
        left, right, (((0,), (0,)), ((), ())), preferred_element_type=jnp.float32
    )


def fold_unit(part, lanes):
    rows, tokens = part.shape
    if tokens >= lanes:
        return jnp.concatenate([part[:, at : at + lanes] for at in range(0, tokens, lanes)])
    lines = rows * tokens // lanes
    return jnp.concatenate([part[at : at + lines] for at in range(0, rows, lines)], axis=1)


def unfold_unit(folded, rows):
    lines, lanes = folded.shape
    tokens = lines * lanes // rows
    if tokens >= lanes:
        return jnp.concatenate([folded[at : at + rows] for at in range(0, lines, rows)], axis=1)
    return jnp.concatenate([folded[:, at : at + tokens] for at in range(0, lanes, tokens)])


def lookup(embed_table, token_ids, arranged, units, width, lanes, after):
    here, width_all = embed_table.shape
    tokens = token_ids.shape[0]
    rows = width // units
    core, upper, t = own_place()
    inside = token_ids - (lax.axis_index("fsdp") * units + t) * here
    place = jnp.where((inside >= 0) & (inside < here), inside, -1).astype(jnp.int32)
    kind = embed_table.dtype
    if width % LANES or lanes % tokens or (rows * tokens // lanes) % 16:
        found = jnp.where(
            (place >= 0)[:, None], embed_table[jnp.maximum(place, 0)], jnp.zeros((), kind)
        )
        flipped = found.T

        def folded(r, side, unit):
            start = (((r ^ upper) << 1) | side) * width + (unit ^ t) * rows
            return fold_unit(lax.dynamic_slice_in_dim(flipped, start, rows, 0), lanes)

        return [
            jnp.concatenate(
                [
                    jnp.concatenate(
                        [folded(r, side, unit) for unit in range(low, units, 2)], axis=1
                    )
                    for low in range(2)
                    for r in arranged
                ]
            )
            for side in (1 - core, core)
        ]
    shape = jax.ShapeDtypeStruct((len(arranged) * width * tokens // lanes // 2, 2 * lanes), kind)
    return pl.pallas_call(
        functools.partial(pick_rows, arranged, units),
        grid=(1,),
        in_specs=[
            pl.BlockSpec(memory_space=pltpu.SMEM),
            pl.BlockSpec(memory_space=pltpu.HBM),
            pl.BlockSpec((SLAB, width_all), lambda i: ((here - 1) // SLAB, 0)),
            pl.BlockSpec(memory_space=pl.ANY),
        ],
        out_specs=[pl.BlockSpec(memory_space=pltpu.VMEM)] * 2,
        out_shape=[shape, shape],
        scratch_shapes=[
            pltpu.VMEM((tokens, SLAB, width_all), kind),
            pltpu.VMEM((tokens, width_all), jnp.float32),
            pltpu.VMEM((width, tokens), jnp.float32),
            pltpu.SemaphoreType.DMA((tokens,)),
        ],
        compiler_params=pltpu.CompilerParams(vmem_limit_bytes=VMEM // 2),
        cost_estimate=pl.CostEstimate(flops=1, bytes_accessed=1, transcendentals=0),
    )(place, embed_table, embed_table, after)


def dot32(left, right):
    return jnp.dot(left, right, preferred_element_type=jnp.float32)


def per_device(
    activations,
    grad_out,
    master_w,
    embed_table,
    token_ids,
    queries,
    cache_keys,
    cache_values,
    new_key,
    first_value,
    residual_mix,
    lengths,
):
    count_fsdp = lax.axis_size("fsdp")
    count_tp = lax.axis_size("tp")
    devices_all = count_fsdp * count_tp
    width = activations.shape[1]
    tokens_total = activations.shape[0] * devices_all
    coef = 1.0 / math.sqrt(tokens_total * width)
    upper_bits = count_fsdp.bit_length() - 2
    uppers = 1 << upper_bits

    block = width // count_fsdp
    rows = master_w.shape[0]
    columns = master_w.shape[1]
    arranged = [r ^ (r >> 1) for r in range(uppers)][::-1]
    grads = [grad_out, exchange(grad_out, "fsdp", 1)]
    outward = pack(activations, arranged, False, count_tp, block)
    incoming = exchange(outward, "fsdp", 1)
    staying = pack(activations, arranged, True, count_tp, block)
    lefts = [staying, incoming]
    tokens_new = token_ids.shape[0]
    quarter = columns // 4
    eighth = columns // 8
    lines = rows * tokens_new // eighth

    places = [(r, unit) for r in arranged for unit in range(count_tp)]
    steps_upper = [("fsdp", bit) for bit in range(upper_bits)]
    steps_tp = [("tp", bit) for bit in range(count_tp.bit_length() - 1)]
    one, two = steps_upper + steps_tp, steps_upper[::-1] + steps_tp
    edges = [0, quarter, 2 * quarter] + [2 * quarter + at * eighth for at in range(1, 5)]
    spans = list(zip(edges[:-1], edges[1:]))
    orders = [one, two] * 3
    chunks = range(len(spans))

    def has(place, step):
        return (place[step[0] == "tp"] >> step[1]) & 1

    def flip(place, step):
        mask = 1 << step[1]
        return (place[0], place[1] ^ mask) if step[0] == "tp" else (place[0] ^ mask, place[1])

    def split(held, step):
        return [p for p in held if has(p, step)], [p for p in held if not has(p, step)]

    def take(value, held, chosen, size):
        runs = runs_of([held.index(p) for p in chosen])
        return jnp.concatenate([value[low * size : high * size] for low, high in runs])

    def send(value, step):
        mask = 1 << step[1]
        return exchange(value, step[0], 2 * mask if step[0] == "fsdp" else mask)

    def compute(which, after, limit=127 << 19):
        wanted = []
        for index, sent in which:
            chosen = split(places, orders[index][0])[0 if sent else 1]
            units = [places.index(p) for p in chosen]
            kind = jnp.bfloat16 if sent else jnp.float32
            wanted.append((units, *spans[index], kind))
        return products(lefts, grads, wanted, rows, uppers, after, limit)

    theirs, ours = lookup(
        embed_table, token_ids, arranged, count_tp, block, eighth, outward
    )
    emb = ours + exchange(theirs, "fsdp", 1)
    emb_held = [(r, low) for low in range(2) for r in arranged]
    emb_steps = steps_upper + steps_tp

    def emb_split(step):
        return (emb_held, emb_held) if step[0] == "tp" else split(emb_held, step)

    def emb_forward(emb, got, step, following, after):
        go, keep = emb_split(following)
        landed = [flip(p, step) for p in emb_go]
        if plain:
            emb = emb + take(got, landed, emb_held, lines).astype(jnp.float32)
            out = take(emb, emb_held, go, lines).astype(jnp.bfloat16)
            return out, take(emb, emb_held, keep, lines), go, keep
        order = [(emb_held.index(p), landed.index(p)) for p in go + keep]
        plan = [(lines, order, len(go), len(keep), len(landed))]
        kept, sent, _ = combine([plan], [[emb]], [got], False, [after])
        return sent[0], kept[0][0], go, keep

    plain = rows % 32 or lines % 16 or block % LANES or eighth % tokens_new
    last_tp = steps_tp[-1]
    emb_go, emb_keep = emb_split(emb_steps[0])
    emb_out = take(emb, emb_held, emb_go, lines)
    emb = take(emb, emb_held, emb_keep, lines).astype(jnp.float32)
    emb_held = emb_keep
    emb_got = send(emb_out, emb_steps[0])
    lefts = [staying, incoming]
    going = compute([(0, True), (1, True)], [emb_out])
    inbox = [[send(value, orders[at][0]) for at, value in enumerate(going)], None, None]
    emb_out, emb, emb_go, emb_held = emb_forward(
        emb, emb_got, emb_steps[0], emb_steps[1], going[0]
    )
    emb_got = send(emb_out, emb_steps[1])
    emb_at = 1
    going = compute([(2, True), (3, True)], [going[0]])
    inbox[1] = [send(value, orders[2 + at][0]) for at, value in enumerate(going)]
    values = [[value] for value in compute([(at, False) for at in range(4)], [going[0]])]
    token = values[0][0]
    sizes = [[rows] for _ in chunks]
    gone, held = [
        [[split(places, orders[index][0])[side]] for index in chunks] for side in range(2)
    ]

    def receive(index, step, arrived):
        landed = [flip(p, step) for p in gone[index][0]]
        piece = take(arrived, landed, held[index][0], rows)
        values[index][0] = values[index][0] + piece.astype(jnp.float32)

    def forward(index, step, following):
        go, keep = split(held[index][0], following)
        landed = [flip(p, step) for p in gone[index][0]]
        order = [(held[index][0].index(p), landed.index(p)) for p in go + keep]
        return [(rows, order, len(go), len(keep), len(landed))]

    rows_f = tokens_new // count_fsdp
    col_width = columns // count_tp

    def share_of(sums, emb, emb_got, after):
        if plain:
            emb = emb + jnp.roll(emb_got, emb_got.shape[1] // 2, axis=1).astype(jnp.float32)
            lefts_own = {
                (0, low + 2 * high): unfold_unit(
                    emb[low * lines : (low + 1) * lines, high * eighth : (high + 1) * eighth], rows
                )
                for low in range(2)
                for high in range(2)
            }

            def exact(left, right):
                return lax.dot_general(
                    left.astype(jnp.float32),
                    right.astype(jnp.float32),
                    (((0,), (0,)), ((), ())),
                    precision=lax.Precision.HIGHEST,
                )

            pieces = []
            for index, (first, last) in enumerate(spans):
                moved = sum(
                    exact(lefts_own[p], array[at * rows : (at + 1) * rows])
                    for array, chosen in sums[index]
                    for at, p in enumerate(chosen)
                )
                pieces.append(exact(lefts_own[0, 0], master_w[:, first:last]) - coef * moved)
            out = jnp.concatenate(pieces, axis=1)
            out = out.reshape(count_fsdp, rows_f, count_tp, col_width)
            out = out.transpose(0, 2, 1, 3).reshape(devices_all, rows_f, col_width)
            return out.astype(jnp.bfloat16)
        arrays = [array for index in chunks for array, _ in sums[index]]
        plans = [
            [(2 * index + at, [p[1] for p in chosen]) for at, (_, chosen) in enumerate(sums[index])]
            for index in chunks
        ]
        return pl.pallas_call(
            functools.partial(own_share, coef, spans, plans, rows, tokens_new),
            in_specs=[pl.BlockSpec(memory_space=pl.ANY)]
            + [pl.BlockSpec(memory_space=pltpu.VMEM)] * (3 + len(arrays)),
            out_specs=pl.BlockSpec(memory_space=pltpu.VMEM),
            out_shape=jax.ShapeDtypeStruct((devices_all, rows_f, col_width), jnp.float32),
            compiler_params=pltpu.CompilerParams(vmem_limit_bytes=VMEM // 4),
            cost_estimate=pl.CostEstimate(flops=1, bytes_accessed=1, transcendentals=0),
        )(after, emb, emb_got, master_w, *arrays).astype(jnp.bfloat16)

    totals = [None] * 3
    sums = {}
    steps = len(one)
    events = [(pair, at) for at in range(steps) for pair in range(3)]
    if steps == 4:
        ranks = ((0, 2, 4, 9), (1, 5, 8, 11), (3, 6, 10, 12))
        events.sort(key=lambda event: ranks[event[0]][event[1]])
    parts_own, ended = None, []

    for pair, at in events:
        group = (2 * pair, 2 * pair + 1)
        if emb_at + 1 < len(emb_steps) and pair < 2:
            emb_out, emb, emb_go, emb_held = emb_forward(
                emb, emb_got, emb_steps[emb_at], emb_steps[emb_at + 1], token
            )
            emb_at += 1
            emb_got = send(emb_out, emb_steps[emb_at])
            token = emb_out
        last = at + 1 == steps
        if plain or last:
            if len(inbox[pair]) < 2:
                whole, cut = inbox[pair][0], totals[pair][0]
                inbox[pair] = [whole[:cut], whole[cut:]]
            for index, arrived in zip(group, inbox[pair]):
                receive(index, orders[index][at], arrived)
        if last:
            ended.append(values[group[-1]][0])
            continue
        following = [orders[index][at + 1] for index in group]
        if plain:
            outgoing = []
            for index, step in zip(group, following):
                go, keep = split(held[index][0], step)
                value = values[index][0]
                values[index] = [take(value, held[index][0], keep, rows)]
                outgoing.append(take(value, held[index][0], go, rows).astype(jnp.bfloat16))
            totals[pair] = [value.shape[0] for value in outgoing]
            merged = False
        else:
            plans = [forward(i, orders[i][at], orders[i][at + 1]) for i in group]
            merged = following[0] == following[1]
            kept, outgoing, totals[pair] = combine(
                plans, [values[i] for i in group], inbox[pair], merged, [token] + ended
            )
            for index, value in zip(group, kept):
                values[index] = value
        for number, index in enumerate(group):
            go, keep = split(held[index][0], following[number])
            gone[index], held[index] = [go], [keep]
            if at + 1 == upper_bits:
                low = number * totals[pair][0] if merged else 0
                sent = outgoing[0 if merged else number]
                sums[index] = [(values[index][0], keep), (sent[low : low + totals[pair][number]], go)]
        token = last_sent = outgoing[-1]
        inbox[pair] = [send(value, step) for value, step in zip(outgoing, following)]
        if inbox[2] is None:
            going = compute(
                [(4, True), (5, True), (4, False), (5, False)], [token], 44 << 20
            )
            inbox[2] = [send(value, orders[4 + at][0]) for at, value in enumerate(going[:2])]
            values += [[value] for value in going[2:]]
            token = going[0]
        if len(sums) == len(spans) and emb_at + 1 == len(emb_steps) and parts_own is None:
            parts_own = share_of(sums, emb, emb_got, token)
            token = parts_own
            parts_own = lax.all_to_all(parts_own, ("fsdp", "tp"), split_axis=0, concat_axis=0)
    own_value = pl.pallas_call(
        add_parts,
        in_specs=[pl.BlockSpec(memory_space=pl.ANY), pl.BlockSpec(memory_space=pltpu.VMEM)],
        out_specs=pl.BlockSpec(memory_space=pltpu.VMEM),
        out_shape=jax.ShapeDtypeStruct(parts_own.shape[1:], jnp.float32),
        compiler_params=pltpu.CompilerParams(vmem_limit_bytes=VMEM // 4),
    )(last_sent, parts_own)
    w_next = jnp.concatenate(
        [master_w[:, low:high] - coef * values[at][0] for at, (low, high) in enumerate(spans)],
        axis=1,
    )

    share = jnp.repeat(residual_mix, HD)[None, :]
    new_value = (share * own_value + (1.0 - share) * first_value.astype(jnp.float32)).astype(
        jnp.bfloat16
    )
    rows = queries.shape[0]
    heads_kv = residual_mix.shape[0]
    group = HEADS // KV
    context = cache_keys.shape[1]
    scale = 1.0 / math.sqrt(HD)
    query_b = queries.reshape(rows, heads_kv, group, HD)
    keys_b = cache_keys.reshape(rows, context, heads_kv, HD)
    vals_b = cache_values.reshape(rows, context, heads_kv, HD)
    newk_b = new_key.reshape(rows, heads_kv, HD)
    newv_b = new_value.reshape(rows, heads_kv, HD)
    scores = (
        jnp.einsum("rkgd,rckd->rkgc", query_b, keys_b, preferred_element_type=jnp.float32) * scale
    )
    fresh = jnp.einsum("rkgd,rkd->rkg", query_b, newk_b, preferred_element_type=jnp.float32) * scale
    valid = jnp.arange(context, dtype=jnp.int32)[None, :] < lengths[:, None]
    scores = jnp.where(valid[:, None, None, :], scores, -1e30)
    peak = jnp.maximum(jnp.max(scores, axis=-1), fresh)
    expo = jnp.exp(scores - peak[..., None])
    expo_new = jnp.exp(fresh - peak)
    total = jnp.sum(expo, axis=-1) + expo_new
    probs = (expo / total[..., None]).astype(jnp.bfloat16)
    probs_new = (expo_new / total).astype(jnp.bfloat16)
    mixed = lax.optimization_barrier(
        jnp.einsum("rkgc,rckd->rkgd", probs, vals_b, preferred_element_type=jnp.float32)
    )
    mixed = (
        mixed + probs_new.astype(jnp.float32)[..., None] * newv_b.astype(jnp.float32)[:, :, None, :]
    )
    attended = mixed.reshape(rows, group * heads_kv * HD).astype(jnp.bfloat16)
    return (w_next, new_value, attended)


def solution(mesh):
    return jax.shard_map(
        per_device,
        mesh=mesh,
        in_specs=(
            P(("fsdp", "tp"), None),
            P(("fsdp", "tp"), None),
            P(("fsdp", "tp"), None),
            P(("fsdp", "tp"), None),
            P(),
            P("fsdp", "tp"),
            P("fsdp", None, "tp"),
            P("fsdp", None, "tp"),
            P("fsdp", "tp"),
            P("fsdp", "tp"),
            P("tp"),
            P("fsdp"),
        ),
        out_specs=(P(("fsdp", "tp"), None), P("fsdp", "tp"), P("fsdp", "tp")),
        check_vma=False,
    )
```

```python
import functools
import math

import jax
import jax.numpy as jnp
from jax import lax
from jax.experimental import pallas as pl
from jax.experimental.pallas import tpu as pltpu
from jax.sharding import PartitionSpec as P

HEADS = 64
KV = 8
HD = 128
LANES = 128
SLAB = 16
VMEM = 56 << 20
TOKEN = (8, 128)


def exchange(value, axis, mask):
    return lax.ppermute(value, axis, [(i, i ^ mask) for i in range(lax.axis_size(axis))])


def own_place():
    f = lax.axis_index("fsdp")
    return f & 1, f >> 1, lax.axis_index("tp")


def transpose_blocks(arranged, mine, units, source, out, wide, tall, arrived, left):
    core, upper, t = own_place()
    width = wide.shape[2]
    rows = width // units
    side = core if mine else 1 - core
    taken, given = [], []
    for j, r in enumerate(arranged):
        start = pl.multiple_of((((r ^ upper) << 1) | side) * width, LANES)
        copy = pltpu.make_async_copy(source.at[:, pl.ds(start, width)], wide.at[j], arrived.at[j])
        copy.start()
        taken.append(copy)
    for j in range(len(arranged)):
        taken[j].wait()
        for low in range(0, width, LANES):
            tall[j, low : low + LANES, :] = wide[j, :, low : low + LANES].T
        for unit in range(units):
            place = pl.multiple_of(j * width + (unit ^ t) * rows, 32)
            copy = pltpu.make_async_copy(
                tall.at[j, pl.ds(unit * rows, rows)],
                out.at[pl.ds(place, rows)],
                left.at[j * units + unit],
            )
            copy.start()
            given.append(copy)
    for copy in given:
        copy.wait()


def pack(activations, arranged, mine, units, width):
    tokens = activations.shape[0]
    count = len(arranged)
    rows = width // units
    if width % LANES or rows % 32:
        core, upper, t = own_place()
        side = core if mine else 1 - core
        flipped = activations.T
        return jnp.concatenate(
            [
                lax.dynamic_slice_in_dim(
                    flipped, (((r ^ upper) << 1) | side) * width + (unit ^ t) * rows, rows, 0
                )
                for r in arranged
                for unit in range(units)
            ]
        )
    kind = activations.dtype
    return pl.pallas_call(
        functools.partial(transpose_blocks, arranged, mine, units),
        in_specs=[pl.BlockSpec(memory_space=pltpu.HBM)],
        out_specs=pl.BlockSpec(memory_space=pltpu.HBM),
        out_shape=jax.ShapeDtypeStruct((count * width, tokens), kind),
        scratch_shapes=[
            pltpu.VMEM((count, tokens, width), kind),
            pltpu.VMEM((count, width, tokens), kind),
            pltpu.SemaphoreType.DMA((count,)),
            pltpu.SemaphoreType.DMA((count * units,)),
        ],
        compiler_params=pltpu.CompilerParams(vmem_limit_bytes=VMEM),
        cost_estimate=pl.CostEstimate(
            flops=0, bytes_accessed=4 * count * width * tokens, transcendentals=0
        ),
    )(activations)


def runs_of(units):
    runs = []
    for unit in units:
        if runs and runs[-1][1] == unit:
            runs[-1][1] = unit + 1
        else:
            runs.append([unit, unit + 1])
    return runs


def multiply(wanted, rows, blocks, base, staged, tail, *refs):
    count = len(wanted)
    sources = refs[:4]
    if tail:
        appended, refs = refs[4:6], refs[:4] + refs[6:]
    outs = refs[4 : 4 + count]
    left, right, sems = refs[4 + count : 7 + count]
    stages, given = refs[7 + count : 7 + 2 * count] if staged else outs, []
    tokens = left.shape[1] // 2
    per_block = left.shape[0] // blocks
    units_block = per_block // rows
    needed = [
        block
        for block in range(blocks)
        if any(unit // units_block == block for item in wanted for unit in item[0])
    ]
    columns = pl.ds(base, right.shape[1])
    halves = [pl.ds(0, tokens), pl.ds(tokens, tokens)]
    grads, lefts = [], {}
    for at, half in enumerate(halves):
        grads.append(
            pltpu.make_async_copy(sources[2 + at].at[:, columns], right.at[half], sems.at[at])
        )
        grads[at].start()
    for block in needed:
        span = pl.ds(block * per_block, per_block)
        for at, half in enumerate(halves):
            lefts[block, at] = pltpu.make_async_copy(
                sources[at].at[span], left.at[span, half], sems.at[2 + 2 * block + at]
            )
            lefts[block, at].start()
    if tail:
        addends, addend_sems = refs[-2:]
        for at in range(2):
            pltpu.make_async_copy(
                appended[at].at[pl.ds(tail, tail)], addends.at[at], addend_sems.at[at]
            ).start()
    for copy in grads:
        copy.wait()
    for block in needed:
        for at in range(2):
            lefts[block, at].wait()
        for at, (units, first, last, _) in enumerate(wanted):
            here = [unit for unit in units if unit // units_block == block]
            for low, high in runs_of(here):
                place = units.index(low) * rows
                product = dot32(
                    left[low * rows : high * rows, :], right[:, first - base : last - base]
                )
                stages[at][place : place + (high - low) * rows, :] = product.astype(outs[at].dtype)
            if staged and here:
                span = pl.ds(units.index(here[0]) * rows, len(here) * rows)
                copy = pltpu.make_async_copy(
                    stages[at].at[span], outs[at].at[span], refs[7 + 2 * count].at[block, at]
                )
                copy.start()
                given.append(copy)
    if tail:
        for at in range(2):
            pltpu.make_async_copy(
                appended[at].at[pl.ds(tail, tail)], addends.at[at], addend_sems.at[at]
            ).wait()
        low = len(wanted[0][0]) * rows
        stages[0][low : low + tail, :] = addends[0] + addends[1]
        span = pl.ds(low, tail)
        copy = pltpu.make_async_copy(
            stages[0].at[span], outs[0].at[span], refs[7 + 2 * count].at[blocks, 0]
        )
        copy.start()
        given.append(copy)
    for copy in given:
        copy.wait()


def products(lefts, grads, wanted, rows, blocks, staged, appended=None):
    total, tokens = lefts[0].shape
    base = min(first for _, first, _, _ in wanted)
    columns = max(last for _, _, last, _ in wanted) - base
    if rows % 32 or any((first | last) % LANES for _, first, last, _ in wanted):
        results = [
            jnp.concatenate(
                [
                    sum(
                        dot32(left[low * rows : high * rows], grad[:, first:last])
                        for left, grad in zip(lefts, grads)
                    )
                    for low, high in runs_of(units)
                ]
            ).astype(kind)
            for units, first, last, kind in wanted
        ]
        if appended is not None:
            both = appended[0] + appended[1]
            results[0] = jnp.concatenate([results[0], both[both.shape[0] // 2 :]])
        return results
    tail = 0 if appended is None else appended[0].shape[0] // 2
    shapes = [
        jax.ShapeDtypeStruct((len(units) * rows, last - first), kind)
        for units, first, last, kind in wanted
    ]
    if tail:
        grown = (shapes[0].shape[0] + tail, shapes[0].shape[1])
        shapes[0] = jax.ShapeDtypeStruct(grown, shapes[0].dtype)
    staging = []
    if staged:
        staging = [pltpu.VMEM(shape.shape, shape.dtype) for shape in shapes]
        staging.append(pltpu.SemaphoreType.DMA((blocks + 1, len(shapes))))
    if tail:
        staging.append(pltpu.VMEM((2, tail, shapes[0].shape[1]), shapes[0].dtype))
        staging.append(pltpu.SemaphoreType.DMA((2,)))
    return pl.pallas_call(
        functools.partial(multiply, wanted, rows, blocks, base, staged, tail),
        out_shape=shapes,
        in_specs=[pl.BlockSpec(memory_space=pltpu.HBM)] * (6 if tail else 4),
        out_specs=[pl.BlockSpec(memory_space=pltpu.HBM if staged else pltpu.VMEM)] * len(shapes),
        scratch_shapes=[
            pltpu.VMEM((total, 2 * tokens), lefts[0].dtype),
            pltpu.VMEM((2 * tokens, columns), grads[0].dtype),
            pltpu.SemaphoreType.DMA((2 + 2 * blocks,)),
        ]
        + staging,
        compiler_params=pltpu.CompilerParams(vmem_limit_bytes=VMEM // 2),
        cost_estimate=pl.CostEstimate(flops=1, bytes_accessed=1, transcendentals=0),
    )(*lefts, *grads, *(appended or []))


def pick_rows(arranged, units, place, table, tail, *refs):
    outs, (slabs, found, flipped, sems) = refs[:2], refs[2:]
    whole = (table.shape[0] - 1) // SLAB * SLAB
    tokens, width_all = found.shape
    width = flipped.shape[0]
    rows = width // units
    lanes = outs[0].shape[1]
    lanes = lanes // 2
    folds = lanes // tokens
    lines = rows // folds

    def slab_copy(k):
        start = pl.multiple_of(lax.div(place[k], SLAB) * SLAB, SLAB)
        return pltpu.make_async_copy(table.at[pl.ds(start, SLAB)], slabs.at[k], sems.at[k])

    def add_row(k, held):
        at = lax.broadcasted_iota(jnp.int32, held.shape, 0)
        chosen = jnp.where(at == lax.rem(place[k], SLAB), held.astype(jnp.float32), 0.0)
        found[k : k + 1, :] = jnp.sum(chosen, axis=0, keepdims=True)

    for k in range(tokens):

        @pl.when((place[k] >= 0) & (place[k] < whole))
        def _():
            slab_copy(k).start()

    found[...] = jnp.zeros_like(found)
    for k in range(tokens):

        @pl.when(place[k] >= 0)
        def _():
            @pl.when(place[k] < whole)
            def _():
                slab_copy(k).wait()
                add_row(k, slabs[k])

            @pl.when(place[k] >= whole)
            def _():
                add_row(k, tail[...])

    core, upper, t = own_place()
    for side, out in zip((1 - core, core), outs):
        for j, r in enumerate(arranged):
            start = pl.multiple_of((((r ^ upper) << 1) | side) * width, LANES)
            flipped[...] = found[:, pl.ds(start, width)].T
            for unit in range(units):
                from_row = (unit ^ t) * rows
                pieces = [
                    flipped[pl.ds(pl.multiple_of(from_row + fold * lines, 8), lines), :]
                    for fold in range(folds)
                ]
                put = ((unit & 1) * len(arranged) + j) * lines
                side_lanes = slice((unit >> 1) * lanes, ((unit >> 1) + 1) * lanes)
                out[put : put + lines, side_lanes] = jnp.concatenate(pieces, axis=1).astype(
                    out.dtype
                )


def add_and_split(plans, arrays, merged, _, *refs):
    refs, done = list(refs[:-1]), refs[-1]
    done[...] = jnp.zeros_like(done)
    takes = [[refs.pop(0) for _ in plan] for plan in plans]
    inbox = [refs.pop(0) for _ in range(arrays)]
    gives = [[refs.pop(0) for _ in plan] for plan in plans]
    start = put = 0
    for at_plan, (plan, inputs, outputs) in enumerate(zip(plans, takes, gives)):
        got, sent = inbox[min(at_plan, arrays - 1)], refs[0 if merged else at_plan]
        if arrays > 1:
            start = 0
        if not merged:
            put = 0
        for (size, order, go, keep, have), value, kept in zip(plan, inputs, outputs):

            def sum_of(low, high):
                pieces = []
                for at in range(low, high):
                    place, lies = order[at]
                    pieces.append(
                        value[place * size : (place + 1) * size, :]
                        + got[start + lies * size : start + (lies + 1) * size, :].astype(
                            jnp.float32
                        )
                    )
                return pieces

            for at, piece in enumerate(sum_of(0, go)):
                sent[put + at * size : put + (at + 1) * size, :] = piece.astype(sent.dtype)
            for at, piece in enumerate(sum_of(go, go + keep)):
                kept[at * size : (at + 1) * size, :] = piece
            start += have * size
            put += go * size


def combine(plans, values, got, merged, after):
    columns = [parts[0].shape[1] for parts in values]
    totals = [sum(size * go for size, _, go, _, _ in plan) for plan in plans]
    outs = [
        jax.ShapeDtypeStruct((keep * size, width), jnp.float32)
        for plan, width in zip(plans, columns)
        for size, _, _, keep, _ in plan
    ]
    if merged:
        outs.append(jax.ShapeDtypeStruct((sum(totals), columns[0]), jnp.bfloat16))
    else:
        for total, width in zip(totals, columns):
            outs.append(jax.ShapeDtypeStruct((total, width), jnp.bfloat16))
    outs.append(jax.ShapeDtypeStruct(TOKEN, jnp.float32))
    arrays = [array for parts in values for array in parts] + list(got)
    results = pl.pallas_call(
        functools.partial(add_and_split, plans, len(got), merged),
        in_specs=[pl.BlockSpec(memory_space=pl.ANY)]
        + [pl.BlockSpec(memory_space=pltpu.VMEM)] * len(arrays),
        out_specs=[pl.BlockSpec(memory_space=pltpu.VMEM)] * len(outs),
        out_shape=outs,
        compiler_params=pltpu.CompilerParams(vmem_limit_bytes=VMEM // 4),
        cost_estimate=pl.CostEstimate(flops=1, bytes_accessed=1, transcendentals=0),
    )(after, *arrays)
    *results, done = results
    kept = [[results.pop(0) for _ in plan] for plan in plans]
    return kept, results, totals, done


def own_share(coef, spans, plans, rows, tokens, blocks, _, *refs):
    emb, master, out = refs[0], refs[1], refs[-1]
    arrays = refs[2:-1]
    lanes = emb.shape[1] // blocks
    count_fsdp = tokens // out.shape[1]
    col_width = out.shape[2]
    folded = emb[...].astype(jnp.bfloat16)
    lefts = [
        jnp.concatenate(
            [
                folded[:, unit * lanes + at : unit * lanes + at + tokens]
                for at in range(0, lanes, tokens)
            ]
        )
        for unit in range(blocks)
    ]

    def both(left, right):
        high = right.astype(jnp.bfloat16)
        total = across(left, high)
        if right.dtype == jnp.float32:
            total += across(left, (right - high.astype(jnp.float32)).astype(jnp.bfloat16))
        return total

    pieces = []
    for (first, last), plan in zip(spans, plans):
        moved = jnp.zeros((tokens, last - first), jnp.float32)
        for array, units in plan:
            for at, unit in enumerate(units):
                moved += both(lefts[unit], arrays[array][at * rows : (at + 1) * rows, :])
        pieces.append(both(lefts[0], master[:, first:last]) - coef * moved)
    share = jnp.concatenate(pieces, axis=1)
    for f in range(count_fsdp):
        for t in range(out.shape[0] // count_fsdp):
            out[f * (out.shape[0] // count_fsdp) + t] = share[
                f * out.shape[1] : (f + 1) * out.shape[1], t * col_width : (t + 1) * col_width
            ]


def across(left, right):
    return lax.dot_general(
        left, right, (((0,), (0,)), ((), ())), preferred_element_type=jnp.float32
    )


def fold_unit(part, lanes):
    rows, tokens = part.shape
    if tokens >= lanes:
        return jnp.concatenate([part[:, at : at + lanes] for at in range(0, tokens, lanes)])
    lines = rows * tokens // lanes
    return jnp.concatenate([part[at : at + lines] for at in range(0, rows, lines)], axis=1)


def unfold_unit(folded, rows):
    lines, lanes = folded.shape
    tokens = lines * lanes // rows
    if tokens >= lanes:
        return jnp.concatenate([folded[at : at + rows] for at in range(0, lines, rows)], axis=1)
    return jnp.concatenate([folded[:, at : at + tokens] for at in range(0, lanes, tokens)])


def lookup(embed_table, token_ids, arranged, units, width, lanes):
    here, width_all = embed_table.shape
    tokens = token_ids.shape[0]
    rows = width // units
    core, upper, t = own_place()
    inside = token_ids - (lax.axis_index("fsdp") * units + t) * here
    place = jnp.where((inside >= 0) & (inside < here), inside, -1).astype(jnp.int32)
    kind = embed_table.dtype
    if width % LANES or lanes % tokens or (rows * tokens // lanes) % 16:
        found = jnp.where(
            (place >= 0)[:, None], embed_table[jnp.maximum(place, 0)], jnp.zeros((), kind)
        )
        flipped = found.T

        def folded(r, side, unit):
            start = (((r ^ upper) << 1) | side) * width + (unit ^ t) * rows
            return fold_unit(lax.dynamic_slice_in_dim(flipped, start, rows, 0), lanes)

        return [
            jnp.concatenate(
                [
                    jnp.concatenate(
                        [folded(r, side, unit) for unit in range(low, units, 2)], axis=1
                    )
                    for low in range(2)
                    for r in arranged
                ]
            )
            for side in (1 - core, core)
        ]
    shape = jax.ShapeDtypeStruct((len(arranged) * width * tokens // lanes // 2, 2 * lanes), kind)
    return pl.pallas_call(
        functools.partial(pick_rows, arranged, units),
        grid=(1,),
        in_specs=[
            pl.BlockSpec(memory_space=pltpu.SMEM),
            pl.BlockSpec(memory_space=pltpu.HBM),
            pl.BlockSpec((SLAB, width_all), lambda i: ((here - 1) // SLAB, 0)),
        ],
        out_specs=[pl.BlockSpec(memory_space=pltpu.VMEM)] * 2,
        out_shape=[shape, shape],
        scratch_shapes=[
            pltpu.VMEM((tokens, SLAB, width_all), kind),
            pltpu.VMEM((tokens, width_all), jnp.float32),
            pltpu.VMEM((width, tokens), jnp.float32),
            pltpu.SemaphoreType.DMA((tokens,)),
        ],
        compiler_params=pltpu.CompilerParams(vmem_limit_bytes=VMEM // 2),
        cost_estimate=pl.CostEstimate(flops=1, bytes_accessed=1, transcendentals=0),
    )(place, embed_table, embed_table)


def dot32(left, right):
    return jnp.dot(left, right, preferred_element_type=jnp.float32)


def per_device(
    activations,
    grad_out,
    master_w,
    embed_table,
    token_ids,
    queries,
    cache_keys,
    cache_values,
    new_key,
    first_value,
    residual_mix,
    lengths,
):
    count_fsdp = lax.axis_size("fsdp")
    count_tp = lax.axis_size("tp")
    devices_all = count_fsdp * count_tp
    width = activations.shape[1]
    tokens_total = activations.shape[0] * devices_all
    coef = 1.0 / math.sqrt(tokens_total * width)
    upper_bits = count_fsdp.bit_length() - 2
    uppers = 1 << upper_bits

    block = width // count_fsdp
    rows = master_w.shape[0]
    columns = master_w.shape[1]
    arranged = [r ^ (r >> 1) for r in range(uppers)][::-1]
    grads = [grad_out, exchange(grad_out, "fsdp", 1)]
    incoming = exchange(pack(activations, arranged, False, count_tp, block), "fsdp", 1)
    staying = pack(activations, arranged, True, count_tp, block)
    lefts = [staying, incoming]
    tokens_new = token_ids.shape[0]
    quarter = columns // 4
    eighth = columns // 8
    lines = rows * tokens_new // eighth

    places = [(r, unit) for r in arranged for unit in range(count_tp)]
    steps_upper = [("fsdp", bit) for bit in range(upper_bits)]
    steps_tp = [("tp", bit) for bit in range(count_tp.bit_length() - 1)]
    one, two, three = (
        steps_upper + steps_tp,
        steps_upper[::-1] + steps_tp,
        steps_tp[:1] + steps_upper + steps_tp[1:],
    )
    edges = [0, quarter, 2 * quarter, 3 * quarter, 3 * quarter + eighth, columns]
    spans = list(zip(edges[:-1], edges[1:]))
    orders = [one, two, three, one, two]

    def has(place, step):
        return (place[step[0] == "tp"] >> step[1]) & 1

    def flip(place, step):
        mask = 1 << step[1]
        return (place[0], place[1] ^ mask) if step[0] == "tp" else (place[0] ^ mask, place[1])

    def split(held, step):
        return [p for p in held if has(p, step)], [p for p in held if not has(p, step)]

    def take(value, held, chosen, size):
        runs = runs_of([held.index(p) for p in chosen])
        return jnp.concatenate([value[low * size : high * size] for low, high in runs])

    def send(value, step):
        mask = 1 << step[1]
        return exchange(value, step[0], 2 * mask if step[0] == "fsdp" else mask)

    def compute(which, sent, appended=None):
        wanted = []
        for index in which:
            chosen = split(places, orders[index][0])[0 if sent else 1]
            units = [places.index(p) for p in chosen]
            kind = jnp.bfloat16 if sent else jnp.float32
            wanted.append((units, *spans[index], kind))
        return dict(zip(which, products(lefts, grads, wanted, rows, uppers, sent, appended)))

    theirs, ours = lookup(embed_table, token_ids, arranged, count_tp, block, eighth)
    asked = [ours, exchange(theirs, "fsdp", 1)]
    pairs = [(r, low) for low in range(2) for r in arranged]
    going = compute([0, 1], True)
    got = {index: send(value, orders[index][0]) for index, value in going.items()}
    going |= compute([2, 3, 4], True, asked)
    got |= {index: send(going[index], orders[index][0]) for index in (3, 4, 2)}
    values = compute([0, 1, 2], False)
    values |= compute([3, 4], False)
    values = {index: [value] for index, value in values.items()}
    halves = [array[: array.shape[0] // 2].astype(jnp.float32) for array in asked]
    values[2].append(halves[0] + halves[1])
    sizes = {index: [rows] for index in range(5)}
    sizes[2].append(lines)
    held = {index: [split(places, orders[index][0])[1]] for index in range(5)}
    held[2].append(split(pairs, orders[2][0])[1])
    gone = {index: [split(places, orders[index][0])[0]] for index in range(5)}
    gone[2].append(split(pairs, orders[2][0])[0])

    def receive(index, step, arrived):
        start = 0
        for part, (value, size) in enumerate(zip(values[index], sizes[index])):
            landed = [flip(p, step) for p in gone[index][part]]
            piece = arrived[start : start + len(landed) * size]
            start += len(landed) * size
            if part and step == last_tp:
                piece = jnp.roll(piece, piece.shape[1] // 2, axis=1)
            else:
                piece = take(piece, landed, held[index][part], size)
            values[index][part] = value + piece.astype(jnp.float32)

    def onward(index, step):
        return [
            (places_now, places_now) if part and step == last_tp else split(places_now, step)
            for part, places_now in enumerate(held[index])
        ]

    def forward(index, step, following):
        plan = []
        for part, (go, keep) in enumerate(onward(index, following)):
            landed = [flip(p, step) for p in gone[index][part]]
            order = [(held[index][part].index(p), landed.index(p)) for p in go + keep]
            plan.append((sizes[index][part], order, len(go), len(keep), len(landed)))
        return plan

    last_tp = steps_tp[-1]
    rows_f = tokens_new // count_fsdp
    col_width = columns // count_tp

    def share_of(sums, emb, after):
        if plain:
            lefts_own = [
                unfold_unit(emb[:, at * eighth : (at + 1) * eighth], rows) for at in range(2)
            ]

            def exact(left, right):
                return lax.dot_general(
                    left.astype(jnp.float32),
                    right.astype(jnp.float32),
                    (((0,), (0,)), ((), ())),
                    precision=lax.Precision.HIGHEST,
                )

            pieces = []
            for index, (first, last) in enumerate(spans):
                moved = sum(exact(left, array) for left, array in zip(lefts_own, sums[index]))
                pieces.append(exact(lefts_own[0], master_w[:, first:last]) - coef * moved)
            out = jnp.concatenate(pieces, axis=1)
            out = out.reshape(count_fsdp, rows_f, count_tp, col_width)
            out = out.transpose(0, 2, 1, 3).reshape(devices_all, rows_f, col_width)
            return out.astype(jnp.bfloat16)
        arrays = [array for index in range(5) for array in sums[index]]
        plans = [[(2 * index, [0]), (2 * index + 1, [1])] for index in range(5)]
        return pl.pallas_call(
            functools.partial(own_share, coef, spans, plans, rows, tokens_new, 2),
            in_specs=[pl.BlockSpec(memory_space=pl.ANY)]
            + [pl.BlockSpec(memory_space=pltpu.VMEM)] * (2 + len(arrays)),
            out_specs=pl.BlockSpec(memory_space=pltpu.VMEM),
            out_shape=jax.ShapeDtypeStruct((devices_all, rows_f, col_width), jnp.float32),
            compiler_params=pltpu.CompilerParams(vmem_limit_bytes=VMEM // 4),
            cost_estimate=pl.CostEstimate(flops=1, bytes_accessed=1, transcendentals=0),
        )(after, emb, master_w, *arrays).astype(jnp.bfloat16)

    plain = rows % 32 or lines % 16 or block % LANES or eighth % tokens_new
    groups = ((0, 1), (2,), (3, 4))
    inbox = {group: [got[index] for index in group] for group in groups}
    totals = {}
    sums = {}
    steps = len(one)
    events = [(group, at) for at in range(steps) for group in groups]
    if steps == 4:
        first, second, third = groups
        events = [(first, 0), (second, 0), (third, 0), (first, 1), (second, 1), (first, 2)]
        events += [(third, 1), (second, 2), (third, 2), (second, 3), (first, 3), (third, 3)]
    done = jnp.zeros(TOKEN, jnp.float32)
    for group, at in events:
        last = at + 1 == steps
        if plain or last:
            if len(inbox[group]) < len(group):
                whole = inbox[group][0]
                cuts = [sum(totals[group][:place]) for place in range(len(group) + 1)]
                inbox[group] = [whole[low:high] for low, high in zip(cuts[:-1], cuts[1:])]
            for index, arrived in zip(group, inbox[group]):
                receive(index, orders[index][at], arrived)
        if last:
            if group == (2,):
                parts_own = lax.all_to_all(
                    share_of(sums, values[2][1], done),
                    ("fsdp", "tp"),
                    split_axis=0,
                    concat_axis=0,
                )
            continue
        if plain:
            outgoing = []
            for index in group:
                pieces = []
                for part, (go, keep) in enumerate(onward(index, orders[index][at + 1])):
                    value, size = values[index][part], sizes[index][part]
                    pieces.append(take(value, held[index][part], go, size))
                    values[index][part] = take(value, held[index][part], keep, size)
                outgoing.append(jnp.concatenate(pieces).astype(jnp.bfloat16))
            totals[group] = [value.shape[0] for value in outgoing]
            merged = False
        else:
            plans = [forward(i, orders[i][at], orders[i][at + 1]) for i in group]
            merged = len({orders[i][at + 1] for i in group}) == 1
            kept, outgoing, totals[group], done = combine(
                plans, [values[i] for i in group], inbox[group], merged, done
            )
            values |= dict(zip(group, kept))
        for number, index in enumerate(group):
            now = onward(index, orders[index][at + 1])
            gone[index], held[index] = [list(parts) for parts in zip(*now)]
            if at + 2 == steps:
                low = sum(totals[group][:number]) if merged else 0
                sent = outgoing[0 if merged else number]
                sums[index] = [values[index][0], sent[low : low + rows]]
        inbox[group] = [
            send(value, orders[index][at + 1]) for index, value in zip(group, outgoing)
        ]
        if at == 1 and group == groups[0]:
            queries, new_key, lengths, outgoing[0] = lax.optimization_barrier(
                (queries, new_key, lengths, outgoing[0])
            )
    own_value = jnp.sum(parts_own.astype(jnp.float32), axis=0)
    w_next = jnp.concatenate(
        [master_w[:, low:high] - coef * values[at][0] for at, (low, high) in enumerate(spans)],
        axis=1,
    )

    share = jnp.repeat(residual_mix, HD)[None, :]
    new_value = (share * own_value + (1.0 - share) * first_value.astype(jnp.float32)).astype(
        jnp.bfloat16
    )
    rows = queries.shape[0]
    heads_kv = residual_mix.shape[0]
    group = HEADS // KV
    context = cache_keys.shape[1]
    scale = 1.0 / math.sqrt(HD)
    query_b = queries.reshape(rows, heads_kv, group, HD)
    keys_b = cache_keys.reshape(rows, context, heads_kv, HD)
    vals_b = cache_values.reshape(rows, context, heads_kv, HD)
    newk_b = new_key.reshape(rows, heads_kv, HD)
    newv_b = new_value.reshape(rows, heads_kv, HD)
    scores = (
        jnp.einsum("rkgd,rckd->rkgc", query_b, keys_b, preferred_element_type=jnp.float32) * scale
    )
    fresh = jnp.einsum("rkgd,rkd->rkg", query_b, newk_b, preferred_element_type=jnp.float32) * scale
    valid = jnp.arange(context, dtype=jnp.int32)[None, :] < lengths[:, None]
    scores = jnp.where(valid[:, None, None, :], scores, -1e30)
    peak = jnp.maximum(jnp.max(scores, axis=-1), fresh)
    expo = jnp.exp(scores - peak[..., None])
    expo_new = jnp.exp(fresh - peak)
    total = jnp.sum(expo, axis=-1) + expo_new
    probs = (expo / total[..., None]).astype(jnp.bfloat16)
    probs_new = (expo_new / total).astype(jnp.bfloat16)
    mixed = lax.optimization_barrier(
        jnp.einsum("rkgc,rckd->rkgd", probs, vals_b, preferred_element_type=jnp.float32)
    )
    mixed = (
        mixed + probs_new.astype(jnp.float32)[..., None] * newv_b.astype(jnp.float32)[:, :, None, :]
    )
    attended = mixed.reshape(rows, group * heads_kv * HD).astype(jnp.bfloat16)
    return (w_next, new_value, attended)


def solution(mesh):
    return jax.shard_map(
        per_device,
        mesh=mesh,
        in_specs=(
            P(("fsdp", "tp"), None),
            P(("fsdp", "tp"), None),
            P(("fsdp", "tp"), None),
            P(("fsdp", "tp"), None),
            P(),
            P("fsdp", "tp"),
            P("fsdp", None, "tp"),
            P("fsdp", None, "tp"),
            P("fsdp", "tp"),
            P("fsdp", "tp"),
            P("tp"),
            P("fsdp"),
        ),
        out_specs=(P(("fsdp", "tp"), None), P("fsdp", "tp"), P("fsdp", "tp")),
        check_vma=False,
    )
```

```python
import functools
import math

import jax
import jax.numpy as jnp
from jax import lax
from jax.experimental import pallas as pl
from jax.experimental.pallas import tpu as pltpu
from jax.sharding import PartitionSpec as P

HEADS = 64
KV = 8
HD = 128
LANES = 128
SLAB = 16
VMEM = 56 << 20
TOKEN = (8, 128)


def exchange(value, axis, mask):
    return lax.ppermute(value, axis, [(i, i ^ mask) for i in range(lax.axis_size(axis))])


def own_place():
    f = lax.axis_index("fsdp")
    return f & 1, f >> 1, lax.axis_index("tp")


def transpose_blocks(arranged, mine, units, source, out, wide, tall, arrived, left):
    core, upper, t = own_place()
    width = wide.shape[2]
    rows = width // units
    side = core if mine else 1 - core
    taken, given = [], []
    for j, r in enumerate(arranged):
        start = pl.multiple_of((((r ^ upper) << 1) | side) * width, LANES)
        copy = pltpu.make_async_copy(source.at[:, pl.ds(start, width)], wide.at[j], arrived.at[j])
        copy.start()
        taken.append(copy)
    for j in range(len(arranged)):
        taken[j].wait()
        for low in range(0, width, LANES):
            tall[j, low : low + LANES, :] = wide[j, :, low : low + LANES].T
        for unit in range(units):
            place = pl.multiple_of(j * width + (unit ^ t) * rows, 32)
            copy = pltpu.make_async_copy(
                tall.at[j, pl.ds(unit * rows, rows)],
                out.at[pl.ds(place, rows)],
                left.at[j * units + unit],
            )
            copy.start()
            given.append(copy)
    for copy in given:
        copy.wait()


def pack(activations, arranged, mine, units, width):
    tokens = activations.shape[0]
    count = len(arranged)
    rows = width // units
    if width % LANES or rows % 32:
        core, upper, t = own_place()
        side = core if mine else 1 - core
        flipped = activations.T
        return jnp.concatenate(
            [
                lax.dynamic_slice_in_dim(
                    flipped, (((r ^ upper) << 1) | side) * width + (unit ^ t) * rows, rows, 0
                )
                for r in arranged
                for unit in range(units)
            ]
        )
    kind = activations.dtype
    return pl.pallas_call(
        functools.partial(transpose_blocks, arranged, mine, units),
        in_specs=[pl.BlockSpec(memory_space=pltpu.HBM)],
        out_specs=pl.BlockSpec(memory_space=pltpu.HBM),
        out_shape=jax.ShapeDtypeStruct((count * width, tokens), kind),
        scratch_shapes=[
            pltpu.VMEM((count, tokens, width), kind),
            pltpu.VMEM((count, width, tokens), kind),
            pltpu.SemaphoreType.DMA((count,)),
            pltpu.SemaphoreType.DMA((count * units,)),
        ],
        compiler_params=pltpu.CompilerParams(vmem_limit_bytes=VMEM),
        cost_estimate=pl.CostEstimate(
            flops=0, bytes_accessed=4 * count * width * tokens, transcendentals=0
        ),
    )(activations)


def runs_of(units):
    runs = []
    for unit in units:
        if runs and runs[-1][1] == unit:
            runs[-1][1] = unit + 1
        else:
            runs.append([unit, unit + 1])
    return runs


def multiply(wanted, rows, blocks, base, staged, tail, *refs):
    count = len(wanted)
    sources = refs[:4]
    if tail:
        appended, refs = refs[4:6], refs[:4] + refs[6:]
    outs = refs[4 : 4 + count]
    left, right, sems = refs[4 + count : 7 + count]
    stages, given = refs[7 + count : 7 + 2 * count] if staged else outs, []
    tokens = left.shape[1] // 2
    per_block = left.shape[0] // blocks
    units_block = per_block // rows
    needed = [
        block
        for block in range(blocks)
        if any(unit // units_block == block for item in wanted for unit in item[0])
    ]
    columns = pl.ds(base, right.shape[1])
    halves = [pl.ds(0, tokens), pl.ds(tokens, tokens)]
    grads, lefts = [], {}
    for at, half in enumerate(halves):
        grads.append(
            pltpu.make_async_copy(sources[2 + at].at[:, columns], right.at[half], sems.at[at])
        )
        grads[at].start()
    for block in needed:
        span = pl.ds(block * per_block, per_block)
        for at, half in enumerate(halves):
            lefts[block, at] = pltpu.make_async_copy(
                sources[at].at[span], left.at[span, half], sems.at[2 + 2 * block + at]
            )
            lefts[block, at].start()
    if tail:
        addends, addend_sems = refs[-2:]
        for at in range(2):
            pltpu.make_async_copy(
                appended[at].at[pl.ds(tail, tail)], addends.at[at], addend_sems.at[at]
            ).start()
    if tail:
        for at in range(2):
            pltpu.make_async_copy(
                appended[at].at[pl.ds(tail, tail)], addends.at[at], addend_sems.at[at]
            ).wait()
        low = len(wanted[0][0]) * rows
        stages[0][low : low + tail, :] = addends[0] + addends[1]
        span = pl.ds(low, tail)
        copy = pltpu.make_async_copy(
            stages[0].at[span], outs[0].at[span], refs[7 + 2 * count].at[blocks, 0]
        )
        copy.start()
        given.append(copy)
    for copy in grads:
        copy.wait()
    for block in needed:
        for at in range(2):
            lefts[block, at].wait()
        for at, (units, first, last, _) in enumerate(wanted):
            here = [unit for unit in units if unit // units_block == block]
            for low, high in runs_of(here):
                place = units.index(low) * rows
                product = dot32(
                    left[low * rows : high * rows, :], right[:, first - base : last - base]
                )
                stages[at][place : place + (high - low) * rows, :] = product.astype(outs[at].dtype)
            if staged and here:
                span = pl.ds(units.index(here[0]) * rows, len(here) * rows)
                copy = pltpu.make_async_copy(
                    stages[at].at[span], outs[at].at[span], refs[7 + 2 * count].at[block, at]
                )
                copy.start()
                given.append(copy)
    for copy in given:
        copy.wait()


def products(lefts, grads, wanted, rows, blocks, staged, appended=None):
    total, tokens = lefts[0].shape
    base = min(first for _, first, _, _ in wanted)
    columns = max(last for _, _, last, _ in wanted) - base
    if rows % 32 or any((first | last) % LANES for _, first, last, _ in wanted):
        results = [
            jnp.concatenate(
                [
                    sum(
                        dot32(left[low * rows : high * rows], grad[:, first:last])
                        for left, grad in zip(lefts, grads)
                    )
                    for low, high in runs_of(units)
                ]
            ).astype(kind)
            for units, first, last, kind in wanted
        ]
        if appended is not None:
            both = appended[0] + appended[1]
            results[0] = jnp.concatenate([results[0], both[both.shape[0] // 2 :]])
        return results
    tail = 0 if appended is None else appended[0].shape[0] // 2
    shapes = [
        jax.ShapeDtypeStruct((len(units) * rows, last - first), kind)
        for units, first, last, kind in wanted
    ]
    if tail:
        grown = (shapes[0].shape[0] + tail, shapes[0].shape[1])
        shapes[0] = jax.ShapeDtypeStruct(grown, shapes[0].dtype)
    staging = []
    if staged:
        staging = [pltpu.VMEM(shape.shape, shape.dtype) for shape in shapes]
        staging.append(pltpu.SemaphoreType.DMA((blocks + 1, len(shapes))))
    if tail:
        staging.append(pltpu.VMEM((2, tail, shapes[0].shape[1]), shapes[0].dtype))
        staging.append(pltpu.SemaphoreType.DMA((2,)))
    return pl.pallas_call(
        functools.partial(multiply, wanted, rows, blocks, base, staged, tail),
        out_shape=shapes,
        in_specs=[pl.BlockSpec(memory_space=pltpu.HBM)] * (6 if tail else 4),
        out_specs=[pl.BlockSpec(memory_space=pltpu.HBM if staged else pltpu.VMEM)] * len(shapes),
        scratch_shapes=[
            pltpu.VMEM((total, 2 * tokens), lefts[0].dtype),
            pltpu.VMEM((2 * tokens, columns), grads[0].dtype),
            pltpu.SemaphoreType.DMA((2 + 2 * blocks,)),
        ]
        + staging,
        compiler_params=pltpu.CompilerParams(vmem_limit_bytes=VMEM // 2),
        cost_estimate=pl.CostEstimate(flops=1, bytes_accessed=1, transcendentals=0),
    )(*lefts, *grads, *(appended or []))


def pick_rows(arranged, units, place, table, tail, *refs):
    outs, (slabs, found, flipped, sems) = refs[:2], refs[2:]
    whole = (table.shape[0] - 1) // SLAB * SLAB
    tokens, width_all = found.shape
    width = flipped.shape[0]
    rows = width // units
    lanes = outs[0].shape[1]
    lanes = lanes // 2
    folds = lanes // tokens
    lines = rows // folds

    def slab_copy(k):
        start = pl.multiple_of(lax.div(place[k], SLAB) * SLAB, SLAB)
        return pltpu.make_async_copy(table.at[pl.ds(start, SLAB)], slabs.at[k], sems.at[k])

    def add_row(k, held):
        at = lax.broadcasted_iota(jnp.int32, held.shape, 0)
        chosen = jnp.where(at == lax.rem(place[k], SLAB), held.astype(jnp.float32), 0.0)
        found[k : k + 1, :] = jnp.sum(chosen, axis=0, keepdims=True)

    for k in range(tokens):

        @pl.when((place[k] >= 0) & (place[k] < whole))
        def _():
            slab_copy(k).start()

    found[...] = jnp.zeros_like(found)
    for k in range(tokens):

        @pl.when(place[k] >= 0)
        def _():
            @pl.when(place[k] < whole)
            def _():
                slab_copy(k).wait()
                add_row(k, slabs[k])

            @pl.when(place[k] >= whole)
            def _():
                add_row(k, tail[...])

    core, upper, t = own_place()
    for side, out in zip((1 - core, core), outs):
        for j, r in enumerate(arranged):
            start = pl.multiple_of((((r ^ upper) << 1) | side) * width, LANES)
            flipped[...] = found[:, pl.ds(start, width)].T
            for unit in range(units):
                from_row = (unit ^ t) * rows
                pieces = [
                    flipped[pl.ds(pl.multiple_of(from_row + fold * lines, 8), lines), :]
                    for fold in range(folds)
                ]
                put = ((unit & 1) * len(arranged) + j) * lines
                side_lanes = slice((unit >> 1) * lanes, ((unit >> 1) + 1) * lanes)
                out[put : put + lines, side_lanes] = jnp.concatenate(pieces, axis=1).astype(
                    out.dtype
                )


def add_and_split(plans, arrays, merged, _, *refs):
    refs, done = list(refs[:-1]), refs[-1]
    done[...] = jnp.zeros_like(done)
    takes = [[refs.pop(0) for _ in plan] for plan in plans]
    inbox = [refs.pop(0) for _ in range(arrays)]
    gives = [[refs.pop(0) for _ in plan] for plan in plans]
    start = put = 0
    for at_plan, (plan, inputs, outputs) in enumerate(zip(plans, takes, gives)):
        got, sent = inbox[min(at_plan, arrays - 1)], refs[0 if merged else at_plan]
        if arrays > 1:
            start = 0
        if not merged:
            put = 0
        for (size, order, go, keep, have), value, kept in zip(plan, inputs, outputs):

            def sum_of(low, high):
                pieces = []
                for at in range(low, high):
                    place, lies = order[at]
                    pieces.append(
                        value[place * size : (place + 1) * size, :]
                        + got[start + lies * size : start + (lies + 1) * size, :].astype(
                            jnp.float32
                        )
                    )
                return pieces

            for at, piece in enumerate(sum_of(0, go)):
                sent[put + at * size : put + (at + 1) * size, :] = piece.astype(sent.dtype)
            for at, piece in enumerate(sum_of(go, go + keep)):
                kept[at * size : (at + 1) * size, :] = piece
            start += have * size
            put += go * size


def combine(plans, values, got, merged, after):
    columns = [parts[0].shape[1] for parts in values]
    totals = [sum(size * go for size, _, go, _, _ in plan) for plan in plans]
    outs = [
        jax.ShapeDtypeStruct((keep * size, width), jnp.float32)
        for plan, width in zip(plans, columns)
        for size, _, _, keep, _ in plan
    ]
    if merged:
        outs.append(jax.ShapeDtypeStruct((sum(totals), columns[0]), jnp.bfloat16))
    else:
        for total, width in zip(totals, columns):
            outs.append(jax.ShapeDtypeStruct((total, width), jnp.bfloat16))
    outs.append(jax.ShapeDtypeStruct(TOKEN, jnp.float32))
    arrays = [array for parts in values for array in parts] + list(got)
    results = pl.pallas_call(
        functools.partial(add_and_split, plans, len(got), merged),
        in_specs=[pl.BlockSpec(memory_space=pl.ANY)]
        + [pl.BlockSpec(memory_space=pltpu.VMEM)] * len(arrays),
        out_specs=[pl.BlockSpec(memory_space=pltpu.VMEM)] * len(outs),
        out_shape=outs,
        compiler_params=pltpu.CompilerParams(vmem_limit_bytes=VMEM // 4),
        cost_estimate=pl.CostEstimate(flops=1, bytes_accessed=1, transcendentals=0),
    )(after, *arrays)
    *results, done = results
    kept = [[results.pop(0) for _ in plan] for plan in plans]
    return kept, results, totals, done


def own_share(coef, spans, plans, rows, tokens, blocks, _, *refs):
    emb, master, out = refs[0], refs[1], refs[-1]
    arrays = refs[2:-1]
    lanes = emb.shape[1] // blocks
    count_fsdp = tokens // out.shape[1]
    col_width = out.shape[2]
    folded = emb[...].astype(jnp.bfloat16)
    lefts = [
        jnp.concatenate(
            [
                folded[:, unit * lanes + at : unit * lanes + at + tokens]
                for at in range(0, lanes, tokens)
            ]
        )
        for unit in range(blocks)
    ]

    def both(left, right):
        high = right.astype(jnp.bfloat16)
        total = across(left, high)
        if right.dtype == jnp.float32:
            total += across(left, (right - high.astype(jnp.float32)).astype(jnp.bfloat16))
        return total

    pieces = []
    for (first, last), plan in zip(spans, plans):
        moved = jnp.zeros((tokens, last - first), jnp.float32)
        for array, units in plan:
            for at, unit in enumerate(units):
                moved += both(lefts[unit], arrays[array][at * rows : (at + 1) * rows, :])
        pieces.append(both(lefts[0], master[:, first:last]) - coef * moved)
    share = jnp.concatenate(pieces, axis=1)
    for f in range(count_fsdp):
        for t in range(out.shape[0] // count_fsdp):
            out[f * (out.shape[0] // count_fsdp) + t] = share[
                f * out.shape[1] : (f + 1) * out.shape[1], t * col_width : (t + 1) * col_width
            ]


def across(left, right):
    return lax.dot_general(
        left, right, (((0,), (0,)), ((), ())), preferred_element_type=jnp.float32
    )


def fold_unit(part, lanes):
    rows, tokens = part.shape
    if tokens >= lanes:
        return jnp.concatenate([part[:, at : at + lanes] for at in range(0, tokens, lanes)])
    lines = rows * tokens // lanes
    return jnp.concatenate([part[at : at + lines] for at in range(0, rows, lines)], axis=1)


def unfold_unit(folded, rows):
    lines, lanes = folded.shape
    tokens = lines * lanes // rows
    if tokens >= lanes:
        return jnp.concatenate([folded[at : at + rows] for at in range(0, lines, rows)], axis=1)
    return jnp.concatenate([folded[:, at : at + tokens] for at in range(0, lanes, tokens)])


def lookup(embed_table, token_ids, arranged, units, width, lanes):
    here, width_all = embed_table.shape
    tokens = token_ids.shape[0]
    rows = width // units
    core, upper, t = own_place()
    inside = token_ids - (lax.axis_index("fsdp") * units + t) * here
    place = jnp.where((inside >= 0) & (inside < here), inside, -1).astype(jnp.int32)
    kind = embed_table.dtype
    if width % LANES or lanes % tokens or (rows * tokens // lanes) % 16:
        found = jnp.where(
            (place >= 0)[:, None], embed_table[jnp.maximum(place, 0)], jnp.zeros((), kind)
        )
        flipped = found.T

        def folded(r, side, unit):
            start = (((r ^ upper) << 1) | side) * width + (unit ^ t) * rows
            return fold_unit(lax.dynamic_slice_in_dim(flipped, start, rows, 0), lanes)

        return [
            jnp.concatenate(
                [
                    jnp.concatenate(
                        [folded(r, side, unit) for unit in range(low, units, 2)], axis=1
                    )
                    for low in range(2)
                    for r in arranged
                ]
            )
            for side in (1 - core, core)
        ]
    shape = jax.ShapeDtypeStruct((len(arranged) * width * tokens // lanes // 2, 2 * lanes), kind)
    return pl.pallas_call(
        functools.partial(pick_rows, arranged, units),
        grid=(1,),
        in_specs=[
            pl.BlockSpec(memory_space=pltpu.SMEM),
            pl.BlockSpec(memory_space=pltpu.HBM),
            pl.BlockSpec((SLAB, width_all), lambda i: ((here - 1) // SLAB, 0)),
        ],
        out_specs=[pl.BlockSpec(memory_space=pltpu.VMEM)] * 2,
        out_shape=[shape, shape],
        scratch_shapes=[
            pltpu.VMEM((tokens, SLAB, width_all), kind),
            pltpu.VMEM((tokens, width_all), jnp.float32),
            pltpu.VMEM((width, tokens), jnp.float32),
            pltpu.SemaphoreType.DMA((tokens,)),
        ],
        compiler_params=pltpu.CompilerParams(vmem_limit_bytes=VMEM // 2),
        cost_estimate=pl.CostEstimate(flops=1, bytes_accessed=1, transcendentals=0),
    )(place, embed_table, embed_table)


def dot32(left, right):
    return jnp.dot(left, right, preferred_element_type=jnp.float32)


def per_device(
    activations,
    grad_out,
    master_w,
    embed_table,
    token_ids,
    queries,
    cache_keys,
    cache_values,
    new_key,
    first_value,
    residual_mix,
    lengths,
):
    count_fsdp = lax.axis_size("fsdp")
    count_tp = lax.axis_size("tp")
    devices_all = count_fsdp * count_tp
    width = activations.shape[1]
    tokens_total = activations.shape[0] * devices_all
    coef = 1.0 / math.sqrt(tokens_total * width)
    upper_bits = count_fsdp.bit_length() - 2
    uppers = 1 << upper_bits

    block = width // count_fsdp
    rows = master_w.shape[0]
    columns = master_w.shape[1]
    arranged = [r ^ (r >> 1) for r in range(uppers)][::-1]
    grads = [grad_out, exchange(grad_out, "fsdp", 1)]
    incoming = exchange(pack(activations, arranged, False, count_tp, block), "fsdp", 1)
    staying = pack(activations, arranged, True, count_tp, block)
    lefts = [staying, incoming]
    tokens_new = token_ids.shape[0]
    quarter = columns // 4
    eighth = columns // 8
    lines = rows * tokens_new // eighth

    places = [(r, unit) for r in arranged for unit in range(count_tp)]
    steps_upper = [("fsdp", bit) for bit in range(upper_bits)]
    steps_tp = [("tp", bit) for bit in range(count_tp.bit_length() - 1)]
    one, two, three = (
        steps_upper + steps_tp,
        steps_upper[::-1] + steps_tp,
        steps_tp[:1] + steps_upper + steps_tp[1:],
    )
    edges = [0, quarter, 2 * quarter, 3 * quarter, 3 * quarter + eighth, columns]
    spans = list(zip(edges[:-1], edges[1:]))
    orders = [one, two, three, one, two]

    def has(place, step):
        return (place[step[0] == "tp"] >> step[1]) & 1

    def flip(place, step):
        mask = 1 << step[1]
        return (place[0], place[1] ^ mask) if step[0] == "tp" else (place[0] ^ mask, place[1])

    def split(held, step):
        return [p for p in held if has(p, step)], [p for p in held if not has(p, step)]

    def take(value, held, chosen, size):
        runs = runs_of([held.index(p) for p in chosen])
        return jnp.concatenate([value[low * size : high * size] for low, high in runs])

    def send(value, step):
        mask = 1 << step[1]
        return exchange(value, step[0], 2 * mask if step[0] == "fsdp" else mask)

    def compute(which, sent, appended=None):
        wanted = []
        for index in which:
            chosen = split(places, orders[index][0])[0 if sent else 1]
            units = [places.index(p) for p in chosen]
            kind = jnp.bfloat16 if sent else jnp.float32
            wanted.append((units, *spans[index], kind))
        return dict(zip(which, products(lefts, grads, wanted, rows, uppers, sent, appended)))

    theirs, ours = lookup(embed_table, token_ids, arranged, count_tp, block, eighth)
    asked = [ours, exchange(theirs, "fsdp", 1)]
    pairs = [(r, low) for low in range(2) for r in arranged]
    going = compute([2, 0, 1], True, asked)
    got = {index: send(going[index], orders[index][0]) for index in (0, 1, 2)}
    going |= compute([3, 4], True)
    got |= {index: send(going[index], orders[index][0]) for index in (3, 4)}
    values = compute([0, 1, 2], False)
    values |= compute([3, 4], False)
    values = {index: [value] for index, value in values.items()}
    halves = [array[: array.shape[0] // 2].astype(jnp.float32) for array in asked]
    values[2].append(halves[0] + halves[1])
    sizes = {index: [rows] for index in range(5)}
    sizes[2].append(lines)
    held = {index: [split(places, orders[index][0])[1]] for index in range(5)}
    held[2].append(split(pairs, orders[2][0])[1])
    gone = {index: [split(places, orders[index][0])[0]] for index in range(5)}
    gone[2].append(split(pairs, orders[2][0])[0])

    def receive(index, step, arrived):
        start = 0
        for part, (value, size) in enumerate(zip(values[index], sizes[index])):
            landed = [flip(p, step) for p in gone[index][part]]
            piece = arrived[start : start + len(landed) * size]
            start += len(landed) * size
            if part and step == last_tp:
                piece = jnp.roll(piece, piece.shape[1] // 2, axis=1)
            else:
                piece = take(piece, landed, held[index][part], size)
            values[index][part] = value + piece.astype(jnp.float32)

    def onward(index, step):
        return [
            (places_now, places_now) if part and step == last_tp else split(places_now, step)
            for part, places_now in enumerate(held[index])
        ]

    def forward(index, step, following):
        plan = []
        for part, (go, keep) in enumerate(onward(index, following)):
            landed = [flip(p, step) for p in gone[index][part]]
            order = [(held[index][part].index(p), landed.index(p)) for p in go + keep]
            plan.append((sizes[index][part], order, len(go), len(keep), len(landed)))
        return plan

    last_tp = steps_tp[-1]
    rows_f = tokens_new // count_fsdp
    col_width = columns // count_tp

    def share_of(sums, emb, after):
        if plain:
            lefts_own = [
                unfold_unit(emb[:, at * eighth : (at + 1) * eighth], rows) for at in range(2)
            ]

            def exact(left, right):
                return lax.dot_general(
                    left.astype(jnp.float32),
                    right.astype(jnp.float32),
                    (((0,), (0,)), ((), ())),
                    precision=lax.Precision.HIGHEST,
                )

            pieces = []
            for index, (first, last) in enumerate(spans):
                moved = sum(exact(left, array) for left, array in zip(lefts_own, sums[index]))
                pieces.append(exact(lefts_own[0], master_w[:, first:last]) - coef * moved)
            out = jnp.concatenate(pieces, axis=1)
            out = out.reshape(count_fsdp, rows_f, count_tp, col_width)
            out = out.transpose(0, 2, 1, 3).reshape(devices_all, rows_f, col_width)
            return out.astype(jnp.bfloat16)
        arrays = [array for index in range(5) for array in sums[index]]
        plans = [[(2 * index, [0]), (2 * index + 1, [1])] for index in range(5)]
        return pl.pallas_call(
            functools.partial(own_share, coef, spans, plans, rows, tokens_new, 2),
            in_specs=[pl.BlockSpec(memory_space=pl.ANY)]
            + [pl.BlockSpec(memory_space=pltpu.VMEM)] * (2 + len(arrays)),
            out_specs=pl.BlockSpec(memory_space=pltpu.VMEM),
            out_shape=jax.ShapeDtypeStruct((devices_all, rows_f, col_width), jnp.float32),
            compiler_params=pltpu.CompilerParams(vmem_limit_bytes=VMEM // 4),
            cost_estimate=pl.CostEstimate(flops=1, bytes_accessed=1, transcendentals=0),
        )(after, emb, master_w, *arrays).astype(jnp.bfloat16)

    plain = rows % 32 or lines % 16 or block % LANES or eighth % tokens_new
    groups = ((0, 1), (2,), (3, 4))
    inbox = {group: [got[index] for index in group] for group in groups}
    totals = {}
    sums = {}
    steps = len(one)
    events = [(group, at) for at in range(steps) for group in groups]
    if steps == 4:
        first, second, third = groups
        events = [(first, 0), (second, 0), (third, 0), (first, 1), (second, 1), (first, 2)]
        events += [(third, 1), (second, 2), (third, 2), (second, 3), (first, 3), (third, 3)]
    done = jnp.zeros(TOKEN, jnp.float32)
    for group, at in events:
        last = at + 1 == steps
        if plain or last:
            if len(inbox[group]) < len(group):
                whole = inbox[group][0]
                cuts = [sum(totals[group][:place]) for place in range(len(group) + 1)]
                inbox[group] = [whole[low:high] for low, high in zip(cuts[:-1], cuts[1:])]
            for index, arrived in zip(group, inbox[group]):
                receive(index, orders[index][at], arrived)
        if last:
            if group == (2,):
                parts_own = lax.all_to_all(
                    share_of(sums, values[2][1], done),
                    ("fsdp", "tp"),
                    split_axis=0,
                    concat_axis=0,
                )
            continue
        if plain:
            outgoing = []
            for index in group:
                pieces = []
                for part, (go, keep) in enumerate(onward(index, orders[index][at + 1])):
                    value, size = values[index][part], sizes[index][part]
                    pieces.append(take(value, held[index][part], go, size))
                    values[index][part] = take(value, held[index][part], keep, size)
                outgoing.append(jnp.concatenate(pieces).astype(jnp.bfloat16))
            totals[group] = [value.shape[0] for value in outgoing]
            merged = False
        else:
            plans = [forward(i, orders[i][at], orders[i][at + 1]) for i in group]
            merged = len({orders[i][at + 1] for i in group}) == 1
            kept, outgoing, totals[group], done = combine(
                plans, [values[i] for i in group], inbox[group], merged, done
            )
            values |= dict(zip(group, kept))
        for number, index in enumerate(group):
            now = onward(index, orders[index][at + 1])
            gone[index], held[index] = [list(parts) for parts in zip(*now)]
            if at + 2 == steps:
                low = sum(totals[group][:number]) if merged else 0
                sent = outgoing[0 if merged else number]
                sums[index] = [values[index][0], sent[low : low + rows]]
        inbox[group] = [
            send(value, orders[index][at + 1]) for index, value in zip(group, outgoing)
        ]
        if at == 1 and group == groups[0]:
            queries, new_key, lengths, outgoing[0] = lax.optimization_barrier(
                (queries, new_key, lengths, outgoing[0])
            )
    own_value = jnp.sum(parts_own.astype(jnp.float32), axis=0)
    w_next = jnp.concatenate(
        [master_w[:, low:high] - coef * values[at][0] for at, (low, high) in enumerate(spans)],
        axis=1,
    )

    share = jnp.repeat(residual_mix, HD)[None, :]
    new_value = (share * own_value + (1.0 - share) * first_value.astype(jnp.float32)).astype(
        jnp.bfloat16
    )
    rows = queries.shape[0]
    heads_kv = residual_mix.shape[0]
    group = HEADS // KV
    context = cache_keys.shape[1]
    scale = 1.0 / math.sqrt(HD)
    query_b = queries.reshape(rows, heads_kv, group, HD)
    keys_b = cache_keys.reshape(rows, context, heads_kv, HD)
    vals_b = cache_values.reshape(rows, context, heads_kv, HD)
    newk_b = new_key.reshape(rows, heads_kv, HD)
    newv_b = new_value.reshape(rows, heads_kv, HD)
    scores = (
        jnp.einsum("rkgd,rckd->rkgc", query_b, keys_b, preferred_element_type=jnp.float32) * scale
    )
    fresh = jnp.einsum("rkgd,rkd->rkg", query_b, newk_b, preferred_element_type=jnp.float32) * scale
    valid = jnp.arange(context, dtype=jnp.int32)[None, :] < lengths[:, None]
    scores = jnp.where(valid[:, None, None, :], scores, -1e30)
    peak = jnp.maximum(jnp.max(scores, axis=-1), fresh)
    expo = jnp.exp(scores - peak[..., None])
    expo_new = jnp.exp(fresh - peak)
    total = jnp.sum(expo, axis=-1) + expo_new
    probs = (expo / total[..., None]).astype(jnp.bfloat16)
    probs_new = (expo_new / total).astype(jnp.bfloat16)
    mixed = lax.optimization_barrier(
        jnp.einsum("rkgc,rckd->rkgd", probs, vals_b, preferred_element_type=jnp.float32)
    )
    mixed = (
        mixed + probs_new.astype(jnp.float32)[..., None] * newv_b.astype(jnp.float32)[:, :, None, :]
    )
    attended = mixed.reshape(rows, group * heads_kv * HD).astype(jnp.bfloat16)
    return (w_next, new_value, attended)


def solution(mesh):
    return jax.shard_map(
        per_device,
        mesh=mesh,
        in_specs=(
            P(("fsdp", "tp"), None),
            P(("fsdp", "tp"), None),
            P(("fsdp", "tp"), None),
            P(("fsdp", "tp"), None),
            P(),
            P("fsdp", "tp"),
            P("fsdp", None, "tp"),
            P("fsdp", None, "tp"),
            P("fsdp", "tp"),
            P("fsdp", "tp"),
            P("tp"),
            P("fsdp"),
        ),
        out_specs=(P(("fsdp", "tp"), None), P("fsdp", "tp"), P("fsdp", "tp")),
        check_vma=False,
    )
```

```python
import functools
import math

import jax
import jax.numpy as jnp
from jax import lax
from jax.experimental import pallas as pl
from jax.experimental.pallas import tpu as pltpu
from jax.sharding import PartitionSpec as P

HEADS = 64
KV = 8
HD = 128
LANES = 128
SLAB = 16
VMEM = 56 << 20
TOKEN = (8, 128)


def exchange(value, axis, mask):
    return lax.ppermute(value, axis, [(i, i ^ mask) for i in range(lax.axis_size(axis))])


def own_place():
    f = lax.axis_index("fsdp")
    return f & 1, f >> 1, lax.axis_index("tp")


def transpose_blocks(arranged, mine, units, source, out, wide, tall, arrived, left):
    core, upper, t = own_place()
    width = wide.shape[2]
    rows = width // units
    side = core if mine else 1 - core
    taken, given = [], []
    for j, r in enumerate(arranged):
        start = pl.multiple_of((((r ^ upper) << 1) | side) * width, LANES)
        copy = pltpu.make_async_copy(source.at[:, pl.ds(start, width)], wide.at[j], arrived.at[j])
        copy.start()
        taken.append(copy)
    for j in range(len(arranged)):
        taken[j].wait()
        for low in range(0, width, LANES):
            tall[j, low : low + LANES, :] = wide[j, :, low : low + LANES].T
        for unit in range(units):
            place = pl.multiple_of(j * width + (unit ^ t) * rows, 32)
            copy = pltpu.make_async_copy(
                tall.at[j, pl.ds(unit * rows, rows)],
                out.at[pl.ds(place, rows)],
                left.at[j * units + unit],
            )
            copy.start()
            given.append(copy)
    for copy in given:
        copy.wait()


def pack(activations, arranged, mine, units, width):
    tokens = activations.shape[0]
    count = len(arranged)
    rows = width // units
    if width % LANES or rows % 32:
        core, upper, t = own_place()
        side = core if mine else 1 - core
        flipped = activations.T
        return jnp.concatenate(
            [
                lax.dynamic_slice_in_dim(
                    flipped, (((r ^ upper) << 1) | side) * width + (unit ^ t) * rows, rows, 0
                )
                for r in arranged
                for unit in range(units)
            ]
        )
    kind = activations.dtype
    return pl.pallas_call(
        functools.partial(transpose_blocks, arranged, mine, units),
        in_specs=[pl.BlockSpec(memory_space=pltpu.HBM)],
        out_specs=pl.BlockSpec(memory_space=pltpu.HBM),
        out_shape=jax.ShapeDtypeStruct((count * width, tokens), kind),
        scratch_shapes=[
            pltpu.VMEM((count, tokens, width), kind),
            pltpu.VMEM((count, width, tokens), kind),
            pltpu.SemaphoreType.DMA((count,)),
            pltpu.SemaphoreType.DMA((count * units,)),
        ],
        compiler_params=pltpu.CompilerParams(vmem_limit_bytes=VMEM),
        cost_estimate=pl.CostEstimate(
            flops=0, bytes_accessed=4 * count * width * tokens, transcendentals=0
        ),
    )(activations)


def runs_of(units):
    runs = []
    for unit in units:
        if runs and runs[-1][1] == unit:
            runs[-1][1] = unit + 1
        else:
            runs.append([unit, unit + 1])
    return runs


def multiply(wanted, rows, blocks, base, tail, *refs):
    count = len(wanted)
    sources = refs[:4]
    if tail:
        appended, refs = refs[4:6], refs[:4] + refs[6:]
    outs = refs[4 : 4 + count]
    left, right, sems = refs[4 + count : 7 + count]
    tokens = left.shape[1] // 2
    per_block = left.shape[0] // blocks
    units_block = per_block // rows
    needed = [
        block
        for block in range(blocks)
        if any(unit // units_block == block for item in wanted for unit in item[0])
    ]
    columns = pl.ds(base, right.shape[1])
    halves = [pl.ds(0, tokens), pl.ds(tokens, tokens)]
    grads, lefts = [], {}
    for at, half in enumerate(halves):
        grads.append(
            pltpu.make_async_copy(sources[2 + at].at[:, columns], right.at[half], sems.at[at])
        )
        grads[at].start()
    for block in needed:
        span = pl.ds(block * per_block, per_block)
        for at, half in enumerate(halves):
            lefts[block, at] = pltpu.make_async_copy(
                sources[at].at[span], left.at[span, half], sems.at[2 + 2 * block + at]
            )
            lefts[block, at].start()
    if tail:
        addends, addend_sems = refs[-2:]
        for at in range(2):
            pltpu.make_async_copy(
                appended[at], addends.at[at], addend_sems.at[at]
            ).start()
    if tail:
        for at in range(2):
            pltpu.make_async_copy(
                appended[at], addends.at[at], addend_sems.at[at]
            ).wait()
        low = len(wanted[0][0]) * rows
        outs[0][low : low + tail, :] = addends[0] + addends[1]
    for copy in grads:
        copy.wait()
    for block in needed:
        for at in range(2):
            lefts[block, at].wait()
        for at, (units, first, last, _) in enumerate(wanted):
            here = [unit for unit in units if unit // units_block == block]
            for low, high in runs_of(here):
                place = units.index(low) * rows
                product = dot32(
                    left[low * rows : high * rows, :], right[:, first - base : last - base]
                )
                outs[at][place : place + (high - low) * rows, :] = product.astype(outs[at].dtype)


def products(lefts, grads, wanted, rows, blocks, appended=None):
    total, tokens = lefts[0].shape
    base = min(first for _, first, _, _ in wanted)
    columns = max(last for _, _, last, _ in wanted) - base
    if rows % 32 or any((first | last) % LANES for _, first, last, _ in wanted):
        results = [
            jnp.concatenate(
                [
                    sum(
                        dot32(left[low * rows : high * rows], grad[:, first:last])
                        for left, grad in zip(lefts, grads)
                    )
                    for low, high in runs_of(units)
                ]
            ).astype(kind)
            for units, first, last, kind in wanted
        ]
        if appended is not None:
            results[0] = jnp.concatenate([results[0], appended[0] + appended[1]])
        return results
    tail = 0 if appended is None else appended[0].shape[0]
    shapes = [
        jax.ShapeDtypeStruct((len(units) * rows, last - first), kind)
        for units, first, last, kind in wanted
    ]
    if tail:
        grown = (shapes[0].shape[0] + tail, shapes[0].shape[1])
        shapes[0] = jax.ShapeDtypeStruct(grown, shapes[0].dtype)
    staging = []
    if tail:
        staging.append(pltpu.VMEM((2, tail, shapes[0].shape[1]), shapes[0].dtype))
        staging.append(pltpu.SemaphoreType.DMA((2,)))
    return pl.pallas_call(
        functools.partial(multiply, wanted, rows, blocks, base, tail),
        out_shape=shapes,
        in_specs=[pl.BlockSpec(memory_space=pltpu.HBM)] * (6 if tail else 4),
        out_specs=[pl.BlockSpec(memory_space=pltpu.VMEM)] * len(shapes),
        scratch_shapes=[
            pltpu.VMEM((total, 2 * tokens), lefts[0].dtype),
            pltpu.VMEM((2 * tokens, columns), grads[0].dtype),
            pltpu.SemaphoreType.DMA((2 + 2 * blocks,)),
        ]
        + staging,
        compiler_params=pltpu.CompilerParams(vmem_limit_bytes=VMEM // 2),
        cost_estimate=pl.CostEstimate(flops=1, bytes_accessed=1, transcendentals=0),
    )(*lefts, *grads, *(appended or []))


def pick_rows(arranged, units, place, table, tail, *refs):
    outs, (slabs, found, flipped, sems) = refs[:2], refs[2:]
    whole = (table.shape[0] - 1) // SLAB * SLAB
    tokens, width_all = found.shape
    width = flipped.shape[0]
    rows = width // units
    lanes = outs[0].shape[1]
    lanes = lanes // 2
    folds = lanes // tokens
    lines = rows // folds

    def slab_copy(k):
        start = pl.multiple_of(lax.div(place[k], SLAB) * SLAB, SLAB)
        return pltpu.make_async_copy(table.at[pl.ds(start, SLAB)], slabs.at[k], sems.at[k])

    def add_row(k, held):
        at = lax.broadcasted_iota(jnp.int32, held.shape, 0)
        chosen = jnp.where(at == lax.rem(place[k], SLAB), held.astype(jnp.float32), 0.0)
        found[k : k + 1, :] = jnp.sum(chosen, axis=0, keepdims=True)

    for k in range(tokens):

        @pl.when((place[k] >= 0) & (place[k] < whole))
        def _():
            slab_copy(k).start()

    found[...] = jnp.zeros_like(found)
    for k in range(tokens):

        @pl.when(place[k] >= 0)
        def _():
            @pl.when(place[k] < whole)
            def _():
                slab_copy(k).wait()
                add_row(k, slabs[k])

            @pl.when(place[k] >= whole)
            def _():
                add_row(k, tail[...])

    core, upper, t = own_place()
    for side, out in zip((1 - core, core), outs):
        for j, r in enumerate(arranged):
            start = pl.multiple_of((((r ^ upper) << 1) | side) * width, LANES)
            flipped[...] = found[:, pl.ds(start, width)].T
            for unit in range(units):
                from_row = (unit ^ t) * rows
                pieces = [
                    flipped[pl.ds(pl.multiple_of(from_row + fold * lines, 8), lines), :]
                    for fold in range(folds)
                ]
                put = (2 * j + (unit & 1)) * lines
                side_lanes = slice((unit >> 1) * lanes, ((unit >> 1) + 1) * lanes)
                out[put : put + lines, side_lanes] = jnp.concatenate(pieces, axis=1).astype(
                    out.dtype
                )


def add_and_split(plans, arrays, merged, _, *refs):
    refs, done = list(refs[:-1]), refs[-1]
    done[...] = jnp.zeros_like(done)
    takes = [[refs.pop(0) for _ in plan] for plan in plans]
    inbox = [refs.pop(0) for _ in range(arrays)]
    gives = [[refs.pop(0) for _ in plan] for plan in plans]
    start = put = 0
    for at_plan, (plan, inputs, outputs) in enumerate(zip(plans, takes, gives)):
        got, sent = inbox[min(at_plan, arrays - 1)], refs[0 if merged else at_plan]
        if arrays > 1:
            start = 0
        if not merged:
            put = 0
        for (size, order, go, keep, have), value, kept in zip(plan, inputs, outputs):

            def sum_of(low, high):
                pieces = []
                for at in range(low, high):
                    place, lies = order[at]
                    pieces.append(
                        value[place * size : (place + 1) * size, :]
                        + got[start + lies * size : start + (lies + 1) * size, :].astype(
                            jnp.float32
                        )
                    )
                return pieces

            for at, piece in enumerate(sum_of(0, go)):
                sent[put + at * size : put + (at + 1) * size, :] = piece.astype(sent.dtype)
            for at, piece in enumerate(sum_of(go, go + keep)):
                kept[at * size : (at + 1) * size, :] = piece
            start += have * size
            put += go * size


def combine(plans, values, got, merged, after):
    columns = [parts[0].shape[1] for parts in values]
    totals = [sum(size * go for size, _, go, _, _ in plan) for plan in plans]
    outs = [
        jax.ShapeDtypeStruct((keep * size, width), jnp.float32)
        for plan, width in zip(plans, columns)
        for size, _, _, keep, _ in plan
    ]
    if merged:
        outs.append(jax.ShapeDtypeStruct((sum(totals), columns[0]), jnp.bfloat16))
    else:
        for total, width in zip(totals, columns):
            outs.append(jax.ShapeDtypeStruct((total, width), jnp.bfloat16))
    outs.append(jax.ShapeDtypeStruct(TOKEN, jnp.float32))
    arrays = [array for parts in values for array in parts] + list(got)
    results = pl.pallas_call(
        functools.partial(add_and_split, plans, len(got), merged),
        in_specs=[pl.BlockSpec(memory_space=pl.ANY)]
        + [pl.BlockSpec(memory_space=pltpu.VMEM)] * len(arrays),
        out_specs=[pl.BlockSpec(memory_space=pltpu.VMEM)] * len(outs),
        out_shape=outs,
        compiler_params=pltpu.CompilerParams(vmem_limit_bytes=VMEM // 4),
        cost_estimate=pl.CostEstimate(flops=1, bytes_accessed=1, transcendentals=0),
    )(after, *arrays)
    *results, done = results
    kept = [[results.pop(0) for _ in plan] for plan in plans]
    return kept, results, totals, done


def own_share(coef, spans, plans, rows, tokens, blocks, _, *refs):
    emb, master, out = refs[0], refs[1], refs[-1]
    arrays = refs[2:-1]
    lanes = emb.shape[1] // blocks
    count_fsdp = tokens // out.shape[1]
    col_width = out.shape[2]
    folded = emb[...].astype(jnp.bfloat16)
    lefts = [
        jnp.concatenate(
            [
                folded[:, unit * lanes + at : unit * lanes + at + tokens]
                for at in range(0, lanes, tokens)
            ]
        )
        for unit in range(blocks)
    ]

    def both(left, right):
        high = right.astype(jnp.bfloat16)
        total = across(left, high)
        if right.dtype == jnp.float32:
            total += across(left, (right - high.astype(jnp.float32)).astype(jnp.bfloat16))
        return total

    pieces = []
    for (first, last), plan in zip(spans, plans):
        moved = jnp.zeros((tokens, last - first), jnp.float32)
        for array, units in plan:
            for at, unit in enumerate(units):
                moved += both(lefts[unit], arrays[array][at * rows : (at + 1) * rows, :])
        pieces.append(both(lefts[0], master[:, first:last]) - coef * moved)
    share = jnp.concatenate(pieces, axis=1)
    for f in range(count_fsdp):
        for t in range(out.shape[0] // count_fsdp):
            out[f * (out.shape[0] // count_fsdp) + t] = share[
                f * out.shape[1] : (f + 1) * out.shape[1], t * col_width : (t + 1) * col_width
            ]


def across(left, right):
    return lax.dot_general(
        left, right, (((0,), (0,)), ((), ())), preferred_element_type=jnp.float32
    )


def fold_unit(part, lanes):
    rows, tokens = part.shape
    if tokens >= lanes:
        return jnp.concatenate([part[:, at : at + lanes] for at in range(0, tokens, lanes)])
    lines = rows * tokens // lanes
    return jnp.concatenate([part[at : at + lines] for at in range(0, rows, lines)], axis=1)


def unfold_unit(folded, rows):
    lines, lanes = folded.shape
    tokens = lines * lanes // rows
    if tokens >= lanes:
        return jnp.concatenate([folded[at : at + rows] for at in range(0, lines, rows)], axis=1)
    return jnp.concatenate([folded[:, at : at + tokens] for at in range(0, lanes, tokens)])


def lookup(embed_table, token_ids, arranged, units, width, lanes):
    here, width_all = embed_table.shape
    tokens = token_ids.shape[0]
    rows = width // units
    core, upper, t = own_place()
    inside = token_ids - (lax.axis_index("fsdp") * units + t) * here
    place = jnp.where((inside >= 0) & (inside < here), inside, -1).astype(jnp.int32)
    kind = embed_table.dtype
    if width % LANES or lanes % tokens or (rows * tokens // lanes) % 16:
        found = jnp.where(
            (place >= 0)[:, None], embed_table[jnp.maximum(place, 0)], jnp.zeros((), kind)
        )
        flipped = found.T

        def folded(r, side, unit):
            start = (((r ^ upper) << 1) | side) * width + (unit ^ t) * rows
            return fold_unit(lax.dynamic_slice_in_dim(flipped, start, rows, 0), lanes)

        return [
            jnp.concatenate(
                [
                    jnp.concatenate(
                        [folded(r, side, unit) for unit in range(low, units, 2)], axis=1
                    )
                    for r in arranged
                    for low in range(2)
                ]
            )
            for side in (1 - core, core)
        ]
    shape = jax.ShapeDtypeStruct((len(arranged) * width * tokens // lanes // 2, 2 * lanes), kind)
    return pl.pallas_call(
        functools.partial(pick_rows, arranged, units),
        grid=(1,),
        in_specs=[
            pl.BlockSpec(memory_space=pltpu.SMEM),
            pl.BlockSpec(memory_space=pltpu.HBM),
            pl.BlockSpec((SLAB, width_all), lambda i: ((here - 1) // SLAB, 0)),
        ],
        out_specs=[pl.BlockSpec(memory_space=pltpu.VMEM)] * 2,
        out_shape=[shape, shape],
        scratch_shapes=[
            pltpu.VMEM((tokens, SLAB, width_all), kind),
            pltpu.VMEM((tokens, width_all), jnp.float32),
            pltpu.VMEM((width, tokens), jnp.float32),
            pltpu.SemaphoreType.DMA((tokens,)),
        ],
        compiler_params=pltpu.CompilerParams(vmem_limit_bytes=VMEM // 2),
        cost_estimate=pl.CostEstimate(flops=1, bytes_accessed=1, transcendentals=0),
    )(place, embed_table, embed_table)


def dot32(left, right):
    return jnp.dot(left, right, preferred_element_type=jnp.float32)


def per_device(
    activations,
    grad_out,
    master_w,
    embed_table,
    token_ids,
    queries,
    cache_keys,
    cache_values,
    new_key,
    first_value,
    residual_mix,
    lengths,
):
    count_fsdp = lax.axis_size("fsdp")
    count_tp = lax.axis_size("tp")
    devices_all = count_fsdp * count_tp
    width = activations.shape[1]
    tokens_total = activations.shape[0] * devices_all
    coef = 1.0 / math.sqrt(tokens_total * width)
    upper_bits = count_fsdp.bit_length() - 2
    uppers = 1 << upper_bits

    block = width // count_fsdp
    rows = master_w.shape[0]
    columns = master_w.shape[1]
    arranged = [r ^ (r >> 1) for r in range(uppers)][::-1]
    grads = [grad_out, exchange(grad_out, "fsdp", 1)]
    incoming = exchange(pack(activations, arranged, False, count_tp, block), "fsdp", 1)
    staying = pack(activations, arranged, True, count_tp, block)
    lefts = [staying, incoming]
    tokens_new = token_ids.shape[0]
    quarter = columns // 4
    eighth = columns // 8
    lines = rows * tokens_new // eighth

    places = [(r, unit) for r in arranged for unit in range(count_tp)]
    steps_upper = [("fsdp", bit) for bit in range(upper_bits)]
    steps_tp = [("tp", bit) for bit in range(count_tp.bit_length() - 1)]
    one, two = steps_upper + steps_tp, steps_upper[::-1] + steps_tp
    spans = [(at * quarter, (at + 1) * quarter) for at in range(4)]
    orders = [one, two, one, two]
    chunks = range(len(spans))

    def has(place, step):
        return (place[step[0] == "tp"] >> step[1]) & 1

    def flip(place, step):
        mask = 1 << step[1]
        return (place[0], place[1] ^ mask) if step[0] == "tp" else (place[0] ^ mask, place[1])

    def split(held, step):
        return [p for p in held if has(p, step)], [p for p in held if not has(p, step)]

    def take(value, held, chosen, size):
        runs = runs_of([held.index(p) for p in chosen])
        return jnp.concatenate([value[low * size : high * size] for low, high in runs])

    def send(value, step):
        mask = 1 << step[1]
        return exchange(value, step[0], 2 * mask if step[0] == "fsdp" else mask)

    def compute(which, sent, appended=None):
        wanted = []
        for index in which:
            chosen = split(places, orders[index][0])[0 if sent else 1]
            units = [places.index(p) for p in chosen]
            kind = jnp.bfloat16 if sent else jnp.float32
            wanted.append((units, *spans[index], kind))
        return dict(zip(which, products(lefts, grads, wanted, rows, uppers, appended)))

    theirs, ours = lookup(embed_table, token_ids, arranged, count_tp, block, eighth)
    asked = [ours, exchange(theirs, "fsdp", 1)]
    pairs = [(r, low) for r in arranged for low in range(2)]
    pairs_go, pairs_keep = split(pairs, orders[0][0])

    def chosen_pairs(array, wanted):
        return take(array, pairs, wanted, lines)

    going = compute([0, 1], True, [chosen_pairs(array, pairs_go) for array in asked])
    got = {index: send(going[index], orders[index][0]) for index in (0, 1)}
    going |= compute([2, 3], True)
    got |= {index: send(going[index], orders[index][0]) for index in (2, 3)}
    values = compute([0, 1], False)
    values |= compute([2, 3], False)
    values = {index: [value] for index, value in values.items()}
    kept_pairs = [chosen_pairs(array, pairs_keep).astype(jnp.float32) for array in asked]
    values[0].append(kept_pairs[0] + kept_pairs[1])
    sizes = {index: [rows] for index in chunks}
    sizes[0].append(lines)
    gone, held = [
        {index: [split(places, orders[index][0])[side]] for index in chunks} for side in range(2)
    ]
    gone[0].append(pairs_go)
    held[0].append(pairs_keep)

    def receive(index, step, arrived):
        start = 0
        for part, (value, size) in enumerate(zip(values[index], sizes[index])):
            landed = [flip(p, step) for p in gone[index][part]]
            piece = arrived[start : start + len(landed) * size]
            start += len(landed) * size
            if part and step == last_tp:
                piece = jnp.roll(piece, piece.shape[1] // 2, axis=1)
            else:
                piece = take(piece, landed, held[index][part], size)
            values[index][part] = value + piece.astype(jnp.float32)

    def onward(index, step):
        return [
            (places_now, places_now) if part and step == last_tp else split(places_now, step)
            for part, places_now in enumerate(held[index])
        ]

    def forward(index, step, following):
        plan = []
        for part, (go, keep) in enumerate(onward(index, following)):
            landed = [flip(p, step) for p in gone[index][part]]
            order = [(held[index][part].index(p), landed.index(p)) for p in go + keep]
            plan.append((sizes[index][part], order, len(go), len(keep), len(landed)))
        return plan

    last_tp = steps_tp[-1]
    rows_f = tokens_new // count_fsdp
    col_width = columns // count_tp

    def share_of(sums, emb, after):
        if plain:
            lefts_own = [
                unfold_unit(emb[:, at * eighth : (at + 1) * eighth], rows) for at in range(2)
            ]

            def exact(left, right):
                return lax.dot_general(
                    left.astype(jnp.float32),
                    right.astype(jnp.float32),
                    (((0,), (0,)), ((), ())),
                    precision=lax.Precision.HIGHEST,
                )

            pieces = []
            for index, (first, last) in enumerate(spans):
                moved = sum(exact(left, array) for left, array in zip(lefts_own, sums[index]))
                pieces.append(exact(lefts_own[0], master_w[:, first:last]) - coef * moved)
            out = jnp.concatenate(pieces, axis=1)
            out = out.reshape(count_fsdp, rows_f, count_tp, col_width)
            out = out.transpose(0, 2, 1, 3).reshape(devices_all, rows_f, col_width)
            return out.astype(jnp.bfloat16)
        arrays = [array for index in chunks for array in sums[index]]
        plans = [[(2 * index, [0]), (2 * index + 1, [1])] for index in chunks]
        return pl.pallas_call(
            functools.partial(own_share, coef, spans, plans, rows, tokens_new, 2),
            in_specs=[pl.BlockSpec(memory_space=pl.ANY)]
            + [pl.BlockSpec(memory_space=pltpu.VMEM)] * (2 + len(arrays)),
            out_specs=pl.BlockSpec(memory_space=pltpu.VMEM),
            out_shape=jax.ShapeDtypeStruct((devices_all, rows_f, col_width), jnp.float32),
            compiler_params=pltpu.CompilerParams(vmem_limit_bytes=VMEM // 4),
            cost_estimate=pl.CostEstimate(flops=1, bytes_accessed=1, transcendentals=0),
        )(after, emb, master_w, *arrays).astype(jnp.bfloat16)

    plain = rows % 32 or lines % 16 or block % LANES or eighth % tokens_new
    groups = ((0, 1), (2, 3))
    inbox = {group: [got[index] for index in group] for group in groups}
    totals = {}
    sums = {}
    steps = len(one)
    events = [(group, at) for at in range(steps) for group in groups]
    events[-3:-1] = events[-2:-4:-1]
    done = jnp.zeros(TOKEN, jnp.float32)
    for group, at in events:
        last = at + 1 == steps
        if plain or last:
            if len(inbox[group]) < len(group):
                whole = inbox[group][0]
                cuts = [sum(totals[group][:place]) for place in range(len(group) + 1)]
                inbox[group] = [whole[low:high] for low, high in zip(cuts[:-1], cuts[1:])]
            for index, arrived in zip(group, inbox[group]):
                receive(index, orders[index][at], arrived)
        if last:
            done = values[0][1]
            continue
        if plain:
            outgoing = []
            for index in group:
                pieces = []
                for part, (go, keep) in enumerate(onward(index, orders[index][at + 1])):
                    value, size = values[index][part], sizes[index][part]
                    pieces.append(take(value, held[index][part], go, size))
                    values[index][part] = take(value, held[index][part], keep, size)
                outgoing.append(jnp.concatenate(pieces).astype(jnp.bfloat16))
            totals[group] = [value.shape[0] for value in outgoing]
            merged = False
        else:
            plans = [forward(i, orders[i][at], orders[i][at + 1]) for i in group]
            merged = len({orders[i][at + 1] for i in group}) == 1
            kept, outgoing, totals[group], done = combine(
                plans, [values[i] for i in group], inbox[group], merged, done
            )
            values |= dict(zip(group, kept))
        for number, index in enumerate(group):
            now = onward(index, orders[index][at + 1])
            gone[index], held[index] = [list(parts) for parts in zip(*now)]
            if at + 2 == steps:
                low = sum(totals[group][:number]) if merged else 0
                sent = outgoing[0 if merged else number]
                sums[index] = [values[index][0], sent[low : low + rows]]
        inbox[group] = [
            send(value, orders[index][at + 1]) for index, value in zip(group, outgoing)
        ]
        if group == groups[1] and at + 2 == steps:
            parts_own = lax.all_to_all(
                share_of(sums, values[0][1], done), ("fsdp", "tp"), split_axis=0, concat_axis=0
            )
        if at == 1 and group == groups[0]:
            queries, new_key, lengths, outgoing[0] = lax.optimization_barrier(
                (queries, new_key, lengths, outgoing[0])
            )
    own_value = jnp.sum(parts_own.astype(jnp.float32), axis=0)
    w_next = jnp.concatenate(
        [master_w[:, low:high] - coef * values[at][0] for at, (low, high) in enumerate(spans)],
        axis=1,
    )

    share = jnp.repeat(residual_mix, HD)[None, :]
    new_value = (share * own_value + (1.0 - share) * first_value.astype(jnp.float32)).astype(
        jnp.bfloat16
    )
    rows = queries.shape[0]
    heads_kv = residual_mix.shape[0]
    group = HEADS // KV
    context = cache_keys.shape[1]
    scale = 1.0 / math.sqrt(HD)
    query_b = queries.reshape(rows, heads_kv, group, HD)
    keys_b = cache_keys.reshape(rows, context, heads_kv, HD)
    vals_b = cache_values.reshape(rows, context, heads_kv, HD)
    newk_b = new_key.reshape(rows, heads_kv, HD)
    newv_b = new_value.reshape(rows, heads_kv, HD)
    scores = (
        jnp.einsum("rkgd,rckd->rkgc", query_b, keys_b, preferred_element_type=jnp.float32) * scale
    )
    fresh = jnp.einsum("rkgd,rkd->rkg", query_b, newk_b, preferred_element_type=jnp.float32) * scale
    valid = jnp.arange(context, dtype=jnp.int32)[None, :] < lengths[:, None]
    scores = jnp.where(valid[:, None, None, :], scores, -1e30)
    peak = jnp.maximum(jnp.max(scores, axis=-1), fresh)
    expo = jnp.exp(scores - peak[..., None])
    expo_new = jnp.exp(fresh - peak)
    total = jnp.sum(expo, axis=-1) + expo_new
    probs = (expo / total[..., None]).astype(jnp.bfloat16)
    probs_new = (expo_new / total).astype(jnp.bfloat16)
    mixed = lax.optimization_barrier(
        jnp.einsum("rkgc,rckd->rkgd", probs, vals_b, preferred_element_type=jnp.float32)
    )
    mixed = (
        mixed + probs_new.astype(jnp.float32)[..., None] * newv_b.astype(jnp.float32)[:, :, None, :]
    )
    attended = mixed.reshape(rows, group * heads_kv * HD).astype(jnp.bfloat16)
    return (w_next, new_value, attended)


def solution(mesh):
    return jax.shard_map(
        per_device,
        mesh=mesh,
        in_specs=(
            P(("fsdp", "tp"), None),
            P(("fsdp", "tp"), None),
            P(("fsdp", "tp"), None),
            P(("fsdp", "tp"), None),
            P(),
            P("fsdp", "tp"),
            P("fsdp", None, "tp"),
            P("fsdp", None, "tp"),
            P("fsdp", "tp"),
            P("fsdp", "tp"),
            P("tp"),
            P("fsdp"),
        ),
        out_specs=(P(("fsdp", "tp"), None), P("fsdp", "tp"), P("fsdp", "tp")),
        check_vma=False,
    )
```

```python
import functools
import math

import jax
import jax.numpy as jnp
from jax import lax
from jax.experimental import pallas as pl
from jax.experimental.pallas import tpu as pltpu
from jax.sharding import PartitionSpec as P

HEADS = 64
KV = 8
HD = 128
LANES = 128
SLAB = 16
VMEM = 56 << 20
TOKEN = (8, 128)


def exchange(value, axis, mask):
    return lax.ppermute(value, axis, [(i, i ^ mask) for i in range(lax.axis_size(axis))])


def own_place():
    f = lax.axis_index("fsdp")
    return f & 1, f >> 1, lax.axis_index("tp")


def transpose_blocks(arranged, mine, units, source, out, wide, tall, arrived, left):
    core, upper, t = own_place()
    width = wide.shape[2]
    rows = width // units
    side = core if mine else 1 - core
    taken, given = [], []
    for j, r in enumerate(arranged):
        start = pl.multiple_of((((r ^ upper) << 1) | side) * width, LANES)
        copy = pltpu.make_async_copy(source.at[:, pl.ds(start, width)], wide.at[j], arrived.at[j])
        copy.start()
        taken.append(copy)
    for j in range(len(arranged)):
        taken[j].wait()
        for low in range(0, width, LANES):
            tall[j, low : low + LANES, :] = wide[j, :, low : low + LANES].T
        for unit in range(units):
            place = pl.multiple_of(j * width + (unit ^ t) * rows, 32)
            copy = pltpu.make_async_copy(
                tall.at[j, pl.ds(unit * rows, rows)],
                out.at[pl.ds(place, rows)],
                left.at[j * units + unit],
            )
            copy.start()
            given.append(copy)
    for copy in given:
        copy.wait()


def pack(activations, arranged, mine, units, width):
    tokens = activations.shape[0]
    count = len(arranged)
    rows = width // units
    if width % LANES or rows % 32:
        core, upper, t = own_place()
        side = core if mine else 1 - core
        flipped = activations.T
        return jnp.concatenate(
            [
                lax.dynamic_slice_in_dim(
                    flipped, (((r ^ upper) << 1) | side) * width + (unit ^ t) * rows, rows, 0
                )
                for r in arranged
                for unit in range(units)
            ]
        )
    kind = activations.dtype
    return pl.pallas_call(
        functools.partial(transpose_blocks, arranged, mine, units),
        in_specs=[pl.BlockSpec(memory_space=pltpu.HBM)],
        out_specs=pl.BlockSpec(memory_space=pltpu.HBM),
        out_shape=jax.ShapeDtypeStruct((count * width, tokens), kind),
        scratch_shapes=[
            pltpu.VMEM((count, tokens, width), kind),
            pltpu.VMEM((count, width, tokens), kind),
            pltpu.SemaphoreType.DMA((count,)),
            pltpu.SemaphoreType.DMA((count * units,)),
        ],
        compiler_params=pltpu.CompilerParams(vmem_limit_bytes=VMEM),
        cost_estimate=pl.CostEstimate(
            flops=0, bytes_accessed=4 * count * width * tokens, transcendentals=0
        ),
    )(activations)


def runs_of(units):
    runs = []
    for unit in units:
        if runs and runs[-1][1] == unit:
            runs[-1][1] = unit + 1
        else:
            runs.append([unit, unit + 1])
    return runs


def multiply(wanted, rows, blocks, base, tail, *refs):
    count = len(wanted)
    sources = refs[:4]
    if tail:
        appended, refs = refs[4:6], refs[:4] + refs[6:]
    outs = refs[4 : 4 + count]
    left, right, sems = refs[4 + count : 7 + count]
    tokens = left.shape[1] // 2
    per_block = left.shape[0] // blocks
    units_block = per_block // rows
    needed = [
        block
        for block in range(blocks)
        if any(unit // units_block == block for item in wanted for unit in item[0])
    ]
    columns = pl.ds(base, right.shape[1])
    halves = [pl.ds(0, tokens), pl.ds(tokens, tokens)]
    grads, lefts = [], {}
    for at, half in enumerate(halves):
        grads.append(
            pltpu.make_async_copy(sources[2 + at].at[:, columns], right.at[half], sems.at[at])
        )
        grads[at].start()
    for block in needed:
        span = pl.ds(block * per_block, per_block)
        for at, half in enumerate(halves):
            lefts[block, at] = pltpu.make_async_copy(
                sources[at].at[span], left.at[span, half], sems.at[2 + 2 * block + at]
            )
            lefts[block, at].start()
    if tail:
        addends, addend_sems = refs[-2:]
        for at in range(2):
            pltpu.make_async_copy(
                appended[at].at[pl.ds(tail, tail)], addends.at[at], addend_sems.at[at]
            ).start()
    if tail:
        for at in range(2):
            pltpu.make_async_copy(
                appended[at].at[pl.ds(tail, tail)], addends.at[at], addend_sems.at[at]
            ).wait()
        low = len(wanted[0][0]) * rows
        outs[0][low : low + tail, :] = addends[0] + addends[1]
    for copy in grads:
        copy.wait()
    for block in needed:
        for at in range(2):
            lefts[block, at].wait()
        for at, (units, first, last, _) in enumerate(wanted):
            here = [unit for unit in units if unit // units_block == block]
            for low, high in runs_of(here):
                place = units.index(low) * rows
                product = dot32(
                    left[low * rows : high * rows, :], right[:, first - base : last - base]
                )
                outs[at][place : place + (high - low) * rows, :] = product.astype(outs[at].dtype)


def products(lefts, grads, wanted, rows, blocks, appended=None):
    total, tokens = lefts[0].shape
    base = min(first for _, first, _, _ in wanted)
    columns = max(last for _, _, last, _ in wanted) - base
    if rows % 32 or any((first | last) % LANES for _, first, last, _ in wanted):
        results = [
            jnp.concatenate(
                [
                    sum(
                        dot32(left[low * rows : high * rows], grad[:, first:last])
                        for left, grad in zip(lefts, grads)
                    )
                    for low, high in runs_of(units)
                ]
            ).astype(kind)
            for units, first, last, kind in wanted
        ]
        if appended is not None:
            both = appended[0] + appended[1]
            results[0] = jnp.concatenate([results[0], both[both.shape[0] // 2 :]])
        return results
    tail = 0 if appended is None else appended[0].shape[0] // 2
    shapes = [
        jax.ShapeDtypeStruct((len(units) * rows, last - first), kind)
        for units, first, last, kind in wanted
    ]
    if tail:
        grown = (shapes[0].shape[0] + tail, shapes[0].shape[1])
        shapes[0] = jax.ShapeDtypeStruct(grown, shapes[0].dtype)
    staging = []
    if tail:
        staging.append(pltpu.VMEM((2, tail, shapes[0].shape[1]), shapes[0].dtype))
        staging.append(pltpu.SemaphoreType.DMA((2,)))
    return pl.pallas_call(
        functools.partial(multiply, wanted, rows, blocks, base, tail),
        out_shape=shapes,
        in_specs=[pl.BlockSpec(memory_space=pltpu.HBM)] * (6 if tail else 4),
        out_specs=[pl.BlockSpec(memory_space=pltpu.VMEM)] * len(shapes),
        scratch_shapes=[
            pltpu.VMEM((total, 2 * tokens), lefts[0].dtype),
            pltpu.VMEM((2 * tokens, columns), grads[0].dtype),
            pltpu.SemaphoreType.DMA((2 + 2 * blocks,)),
        ]
        + staging,
        compiler_params=pltpu.CompilerParams(vmem_limit_bytes=VMEM // 2),
        cost_estimate=pl.CostEstimate(flops=1, bytes_accessed=1, transcendentals=0),
    )(*lefts, *grads, *(appended or []))


def pick_rows(arranged, units, place, table, tail, *refs):
    outs, (slabs, found, flipped, sems) = refs[:2], refs[2:]
    whole = (table.shape[0] - 1) // SLAB * SLAB
    tokens, width_all = found.shape
    width = flipped.shape[0]
    rows = width // units
    lanes = outs[0].shape[1]
    lanes = lanes // 2
    folds = lanes // tokens
    lines = rows // folds

    def slab_copy(k):
        start = pl.multiple_of(lax.div(place[k], SLAB) * SLAB, SLAB)
        return pltpu.make_async_copy(table.at[pl.ds(start, SLAB)], slabs.at[k], sems.at[k])

    def add_row(k, held):
        at = lax.broadcasted_iota(jnp.int32, held.shape, 0)
        chosen = jnp.where(at == lax.rem(place[k], SLAB), held.astype(jnp.float32), 0.0)
        found[k : k + 1, :] = jnp.sum(chosen, axis=0, keepdims=True)

    for k in range(tokens):

        @pl.when((place[k] >= 0) & (place[k] < whole))
        def _():
            slab_copy(k).start()

    found[...] = jnp.zeros_like(found)
    for k in range(tokens):

        @pl.when(place[k] >= 0)
        def _():
            @pl.when(place[k] < whole)
            def _():
                slab_copy(k).wait()
                add_row(k, slabs[k])

            @pl.when(place[k] >= whole)
            def _():
                add_row(k, tail[...])

    core, upper, t = own_place()
    for side, out in zip((1 - core, core), outs):
        for j, r in enumerate(arranged):
            start = pl.multiple_of((((r ^ upper) << 1) | side) * width, LANES)
            flipped[...] = found[:, pl.ds(start, width)].T
            for unit in range(units):
                from_row = (unit ^ t) * rows
                pieces = [
                    flipped[pl.ds(pl.multiple_of(from_row + fold * lines, 8), lines), :]
                    for fold in range(folds)
                ]
                put = ((unit & 1) * len(arranged) + j) * lines
                side_lanes = slice((unit >> 1) * lanes, ((unit >> 1) + 1) * lanes)
                out[put : put + lines, side_lanes] = jnp.concatenate(pieces, axis=1).astype(
                    out.dtype
                )


def add_and_split(plans, arrays, merged, _, *refs):
    refs, done = list(refs[:-1]), refs[-1]
    done[...] = jnp.zeros_like(done)
    takes = [[refs.pop(0) for _ in plan] for plan in plans]
    inbox = [refs.pop(0) for _ in range(arrays)]
    gives = [[refs.pop(0) for _ in plan] for plan in plans]
    start = put = 0
    for at_plan, (plan, inputs, outputs) in enumerate(zip(plans, takes, gives)):
        got, sent = inbox[min(at_plan, arrays - 1)], refs[0 if merged else at_plan]
        if arrays > 1:
            start = 0
        if not merged:
            put = 0
        for (size, order, go, keep, have), value, kept in zip(plan, inputs, outputs):

            def sum_of(low, high):
                pieces = []
                for at in range(low, high):
                    place, lies = order[at]
                    pieces.append(
                        value[place * size : (place + 1) * size, :]
                        + got[start + lies * size : start + (lies + 1) * size, :].astype(
                            jnp.float32
                        )
                    )
                return pieces

            for at, piece in enumerate(sum_of(0, go)):
                sent[put + at * size : put + (at + 1) * size, :] = piece.astype(sent.dtype)
            for at, piece in enumerate(sum_of(go, go + keep)):
                kept[at * size : (at + 1) * size, :] = piece
            start += have * size
            put += go * size


def combine(plans, values, got, merged, after):
    columns = [parts[0].shape[1] for parts in values]
    totals = [sum(size * go for size, _, go, _, _ in plan) for plan in plans]
    outs = [
        jax.ShapeDtypeStruct((keep * size, width), jnp.float32)
        for plan, width in zip(plans, columns)
        for size, _, _, keep, _ in plan
    ]
    if merged:
        outs.append(jax.ShapeDtypeStruct((sum(totals), columns[0]), jnp.bfloat16))
    else:
        for total, width in zip(totals, columns):
            outs.append(jax.ShapeDtypeStruct((total, width), jnp.bfloat16))
    outs.append(jax.ShapeDtypeStruct(TOKEN, jnp.float32))
    arrays = [array for parts in values for array in parts] + list(got)
    results = pl.pallas_call(
        functools.partial(add_and_split, plans, len(got), merged),
        in_specs=[pl.BlockSpec(memory_space=pl.ANY)]
        + [pl.BlockSpec(memory_space=pltpu.VMEM)] * len(arrays),
        out_specs=[pl.BlockSpec(memory_space=pltpu.VMEM)] * len(outs),
        out_shape=outs,
        compiler_params=pltpu.CompilerParams(vmem_limit_bytes=VMEM // 4),
        cost_estimate=pl.CostEstimate(flops=1, bytes_accessed=1, transcendentals=0),
    )(after, *arrays)
    *results, done = results
    kept = [[results.pop(0) for _ in plan] for plan in plans]
    return kept, results, totals, done


def own_share(coef, spans, plans, rows, tokens, blocks, _, *refs):
    emb, master, out = refs[0], refs[1], refs[-1]
    arrays = refs[2:-1]
    lanes = emb.shape[1] // blocks
    count_fsdp = tokens // out.shape[1]
    col_width = out.shape[2]
    folded = emb[...].astype(jnp.bfloat16)
    lefts = [
        jnp.concatenate(
            [
                folded[:, unit * lanes + at : unit * lanes + at + tokens]
                for at in range(0, lanes, tokens)
            ]
        )
        for unit in range(blocks)
    ]

    def both(left, right):
        high = right.astype(jnp.bfloat16)
        total = across(left, high)
        if right.dtype == jnp.float32:
            total += across(left, (right - high.astype(jnp.float32)).astype(jnp.bfloat16))
        return total

    pieces = []
    for (first, last), plan in zip(spans, plans):
        moved = jnp.zeros((tokens, last - first), jnp.float32)
        for array, units in plan:
            for at, unit in enumerate(units):
                moved += both(lefts[unit], arrays[array][at * rows : (at + 1) * rows, :])
        pieces.append(both(lefts[0], master[:, first:last]) - coef * moved)
    share = jnp.concatenate(pieces, axis=1)
    for f in range(count_fsdp):
        for t in range(out.shape[0] // count_fsdp):
            out[f * (out.shape[0] // count_fsdp) + t] = share[
                f * out.shape[1] : (f + 1) * out.shape[1], t * col_width : (t + 1) * col_width
            ]


def across(left, right):
    return lax.dot_general(
        left, right, (((0,), (0,)), ((), ())), preferred_element_type=jnp.float32
    )


def fold_unit(part, lanes):
    rows, tokens = part.shape
    if tokens >= lanes:
        return jnp.concatenate([part[:, at : at + lanes] for at in range(0, tokens, lanes)])
    lines = rows * tokens // lanes
    return jnp.concatenate([part[at : at + lines] for at in range(0, rows, lines)], axis=1)


def unfold_unit(folded, rows):
    lines, lanes = folded.shape
    tokens = lines * lanes // rows
    if tokens >= lanes:
        return jnp.concatenate([folded[at : at + rows] for at in range(0, lines, rows)], axis=1)
    return jnp.concatenate([folded[:, at : at + tokens] for at in range(0, lanes, tokens)])


def lookup(embed_table, token_ids, arranged, units, width, lanes):
    here, width_all = embed_table.shape
    tokens = token_ids.shape[0]
    rows = width // units
    core, upper, t = own_place()
    inside = token_ids - (lax.axis_index("fsdp") * units + t) * here
    place = jnp.where((inside >= 0) & (inside < here), inside, -1).astype(jnp.int32)
    kind = embed_table.dtype
    if width % LANES or lanes % tokens or (rows * tokens // lanes) % 16:
        found = jnp.where(
            (place >= 0)[:, None], embed_table[jnp.maximum(place, 0)], jnp.zeros((), kind)
        )
        flipped = found.T

        def folded(r, side, unit):
            start = (((r ^ upper) << 1) | side) * width + (unit ^ t) * rows
            return fold_unit(lax.dynamic_slice_in_dim(flipped, start, rows, 0), lanes)

        return [
            jnp.concatenate(
                [
                    jnp.concatenate(
                        [folded(r, side, unit) for unit in range(low, units, 2)], axis=1
                    )
                    for low in range(2)
                    for r in arranged
                ]
            )
            for side in (1 - core, core)
        ]
    shape = jax.ShapeDtypeStruct((len(arranged) * width * tokens // lanes // 2, 2 * lanes), kind)
    return pl.pallas_call(
        functools.partial(pick_rows, arranged, units),
        grid=(1,),
        in_specs=[
            pl.BlockSpec(memory_space=pltpu.SMEM),
            pl.BlockSpec(memory_space=pltpu.HBM),
            pl.BlockSpec((SLAB, width_all), lambda i: ((here - 1) // SLAB, 0)),
        ],
        out_specs=[pl.BlockSpec(memory_space=pltpu.VMEM)] * 2,
        out_shape=[shape, shape],
        scratch_shapes=[
            pltpu.VMEM((tokens, SLAB, width_all), kind),
            pltpu.VMEM((tokens, width_all), jnp.float32),
            pltpu.VMEM((width, tokens), jnp.float32),
            pltpu.SemaphoreType.DMA((tokens,)),
        ],
        compiler_params=pltpu.CompilerParams(vmem_limit_bytes=VMEM // 2),
        cost_estimate=pl.CostEstimate(flops=1, bytes_accessed=1, transcendentals=0),
    )(place, embed_table, embed_table)


def dot32(left, right):
    return jnp.dot(left, right, preferred_element_type=jnp.float32)


def per_device(
    activations,
    grad_out,
    master_w,
    embed_table,
    token_ids,
    queries,
    cache_keys,
    cache_values,
    new_key,
    first_value,
    residual_mix,
    lengths,
):
    count_fsdp = lax.axis_size("fsdp")
    count_tp = lax.axis_size("tp")
    devices_all = count_fsdp * count_tp
    width = activations.shape[1]
    tokens_total = activations.shape[0] * devices_all
    coef = 1.0 / math.sqrt(tokens_total * width)
    upper_bits = count_fsdp.bit_length() - 2
    uppers = 1 << upper_bits

    block = width // count_fsdp
    rows = master_w.shape[0]
    columns = master_w.shape[1]
    arranged = [r ^ (r >> 1) for r in range(uppers)][::-1]
    grads = [grad_out, exchange(grad_out, "fsdp", 1)]
    incoming = exchange(pack(activations, arranged, False, count_tp, block), "fsdp", 1)
    staying = pack(activations, arranged, True, count_tp, block)
    lefts = [staying, incoming]
    tokens_new = token_ids.shape[0]
    quarter = columns // 4
    eighth = columns // 8
    lines = rows * tokens_new // eighth

    places = [(r, unit) for r in arranged for unit in range(count_tp)]
    steps_upper = [("fsdp", bit) for bit in range(upper_bits)]
    steps_tp = [("tp", bit) for bit in range(count_tp.bit_length() - 1)]
    one, two, three = (
        steps_upper + steps_tp,
        steps_upper[::-1] + steps_tp,
        steps_tp[:1] + steps_upper + steps_tp[1:],
    )
    edges = [0, quarter, 2 * quarter, 3 * quarter, 3 * quarter + eighth, columns]
    spans = list(zip(edges[:-1], edges[1:]))
    orders = [one, two, three, one, two]

    def has(place, step):
        return (place[step[0] == "tp"] >> step[1]) & 1

    def flip(place, step):
        mask = 1 << step[1]
        return (place[0], place[1] ^ mask) if step[0] == "tp" else (place[0] ^ mask, place[1])

    def split(held, step):
        return [p for p in held if has(p, step)], [p for p in held if not has(p, step)]

    def take(value, held, chosen, size):
        runs = runs_of([held.index(p) for p in chosen])
        return jnp.concatenate([value[low * size : high * size] for low, high in runs])

    def send(value, step):
        mask = 1 << step[1]
        return exchange(value, step[0], 2 * mask if step[0] == "fsdp" else mask)

    def compute(which, sent, appended=None):
        wanted = []
        for index in which:
            chosen = split(places, orders[index][0])[0 if sent else 1]
            units = [places.index(p) for p in chosen]
            kind = jnp.bfloat16 if sent else jnp.float32
            wanted.append((units, *spans[index], kind))
        return dict(zip(which, products(lefts, grads, wanted, rows, uppers, appended)))

    theirs, ours = lookup(embed_table, token_ids, arranged, count_tp, block, eighth)
    asked = [ours, exchange(theirs, "fsdp", 1)]
    pairs = [(r, low) for low in range(2) for r in arranged]
    going = compute([0, 1], True)
    got = {index: send(value, orders[index][0]) for index, value in going.items()}
    going |= compute([2, 3, 4], True, asked)
    got |= {index: send(going[index], orders[index][0]) for index in (3, 4, 2)}
    values = compute([0, 1, 2], False)
    values |= compute([3, 4], False)
    values = {index: [value] for index, value in values.items()}
    halves = [array[: array.shape[0] // 2].astype(jnp.float32) for array in asked]
    values[2].append(halves[0] + halves[1])
    sizes = {index: [rows] for index in range(5)}
    sizes[2].append(lines)
    held = {index: [split(places, orders[index][0])[1]] for index in range(5)}
    held[2].append(split(pairs, orders[2][0])[1])
    gone = {index: [split(places, orders[index][0])[0]] for index in range(5)}
    gone[2].append(split(pairs, orders[2][0])[0])

    def receive(index, step, arrived):
        start = 0
        for part, (value, size) in enumerate(zip(values[index], sizes[index])):
            landed = [flip(p, step) for p in gone[index][part]]
            piece = arrived[start : start + len(landed) * size]
            start += len(landed) * size
            if part and step == last_tp:
                piece = jnp.roll(piece, piece.shape[1] // 2, axis=1)
            else:
                piece = take(piece, landed, held[index][part], size)
            values[index][part] = value + piece.astype(jnp.float32)

    def onward(index, step):
        return [
            (places_now, places_now) if part and step == last_tp else split(places_now, step)
            for part, places_now in enumerate(held[index])
        ]

    def forward(index, step, following):
        plan = []
        for part, (go, keep) in enumerate(onward(index, following)):
            landed = [flip(p, step) for p in gone[index][part]]
            order = [(held[index][part].index(p), landed.index(p)) for p in go + keep]
            plan.append((sizes[index][part], order, len(go), len(keep), len(landed)))
        return plan

    last_tp = steps_tp[-1]
    rows_f = tokens_new // count_fsdp
    col_width = columns // count_tp

    def share_of(sums, emb, after):
        if plain:
            lefts_own = [
                unfold_unit(emb[:, at * eighth : (at + 1) * eighth], rows) for at in range(2)
            ]

            def exact(left, right):
                return lax.dot_general(
                    left.astype(jnp.float32),
                    right.astype(jnp.float32),
                    (((0,), (0,)), ((), ())),
                    precision=lax.Precision.HIGHEST,
                )

            pieces = []
            for index, (first, last) in enumerate(spans):
                moved = sum(exact(left, array) for left, array in zip(lefts_own, sums[index]))
                pieces.append(exact(lefts_own[0], master_w[:, first:last]) - coef * moved)
            out = jnp.concatenate(pieces, axis=1)
            out = out.reshape(count_fsdp, rows_f, count_tp, col_width)
            out = out.transpose(0, 2, 1, 3).reshape(devices_all, rows_f, col_width)
            return out.astype(jnp.bfloat16)
        arrays = [array for index in range(5) for array in sums[index]]
        plans = [[(2 * index, [0]), (2 * index + 1, [1])] for index in range(5)]
        return pl.pallas_call(
            functools.partial(own_share, coef, spans, plans, rows, tokens_new, 2),
            in_specs=[pl.BlockSpec(memory_space=pl.ANY)]
            + [pl.BlockSpec(memory_space=pltpu.VMEM)] * (2 + len(arrays)),
            out_specs=pl.BlockSpec(memory_space=pltpu.VMEM),
            out_shape=jax.ShapeDtypeStruct((devices_all, rows_f, col_width), jnp.float32),
            compiler_params=pltpu.CompilerParams(vmem_limit_bytes=VMEM // 4),
            cost_estimate=pl.CostEstimate(flops=1, bytes_accessed=1, transcendentals=0),
        )(after, emb, master_w, *arrays).astype(jnp.bfloat16)

    plain = rows % 32 or lines % 16 or block % LANES or eighth % tokens_new
    groups = ((0, 1), (2,), (3, 4))
    inbox = {group: [got[index] for index in group] for group in groups}
    totals = {}
    sums = {}
    steps = len(one)
    events = [(group, at) for at in range(steps) for group in groups]
    if steps == 4:
        first, second, third = groups
        events = [(first, 0), (second, 0), (third, 0), (first, 1), (second, 1), (first, 2)]
        events += [(third, 1), (second, 2), (third, 2), (second, 3), (first, 3), (third, 3)]
    done = jnp.zeros(TOKEN, jnp.float32)
    for group, at in events:
        last = at + 1 == steps
        if plain or last:
            if len(inbox[group]) < len(group):
                whole = inbox[group][0]
                cuts = [sum(totals[group][:place]) for place in range(len(group) + 1)]
                inbox[group] = [whole[low:high] for low, high in zip(cuts[:-1], cuts[1:])]
            for index, arrived in zip(group, inbox[group]):
                receive(index, orders[index][at], arrived)
        if last:
            if group == (2,):
                parts_own = lax.all_to_all(
                    share_of(sums, values[2][1], done),
                    ("fsdp", "tp"),
                    split_axis=0,
                    concat_axis=0,
                )
            continue
        if plain:
            outgoing = []
            for index in group:
                pieces = []
                for part, (go, keep) in enumerate(onward(index, orders[index][at + 1])):
                    value, size = values[index][part], sizes[index][part]
                    pieces.append(take(value, held[index][part], go, size))
                    values[index][part] = take(value, held[index][part], keep, size)
                outgoing.append(jnp.concatenate(pieces).astype(jnp.bfloat16))
            totals[group] = [value.shape[0] for value in outgoing]
            merged = False
        else:
            plans = [forward(i, orders[i][at], orders[i][at + 1]) for i in group]
            merged = len({orders[i][at + 1] for i in group}) == 1
            kept, outgoing, totals[group], done = combine(
                plans, [values[i] for i in group], inbox[group], merged, done
            )
            values |= dict(zip(group, kept))
        for number, index in enumerate(group):
            now = onward(index, orders[index][at + 1])
            gone[index], held[index] = [list(parts) for parts in zip(*now)]
            if at + 2 == steps:
                low = sum(totals[group][:number]) if merged else 0
                sent = outgoing[0 if merged else number]
                sums[index] = [values[index][0], sent[low : low + rows]]
        inbox[group] = [
            send(value, orders[index][at + 1]) for index, value in zip(group, outgoing)
        ]
        if at == 1 and group == groups[0]:
            queries, new_key, lengths, outgoing[0] = lax.optimization_barrier(
                (queries, new_key, lengths, outgoing[0])
            )
    own_value = jnp.sum(parts_own.astype(jnp.float32), axis=0)
    w_next = jnp.concatenate(
        [master_w[:, low:high] - coef * values[at][0] for at, (low, high) in enumerate(spans)],
        axis=1,
    )

    share = jnp.repeat(residual_mix, HD)[None, :]
    new_value = (share * own_value + (1.0 - share) * first_value.astype(jnp.float32)).astype(
        jnp.bfloat16
    )
    rows = queries.shape[0]
    heads_kv = residual_mix.shape[0]
    group = HEADS // KV
    context = cache_keys.shape[1]
    scale = 1.0 / math.sqrt(HD)
    query_b = queries.reshape(rows, heads_kv, group, HD)
    keys_b = cache_keys.reshape(rows, context, heads_kv, HD)
    vals_b = cache_values.reshape(rows, context, heads_kv, HD)
    newk_b = new_key.reshape(rows, heads_kv, HD)
    newv_b = new_value.reshape(rows, heads_kv, HD)
    scores = (
        jnp.einsum("rkgd,rckd->rkgc", query_b, keys_b, preferred_element_type=jnp.float32) * scale
    )
    fresh = jnp.einsum("rkgd,rkd->rkg", query_b, newk_b, preferred_element_type=jnp.float32) * scale
    valid = jnp.arange(context, dtype=jnp.int32)[None, :] < lengths[:, None]
    scores = jnp.where(valid[:, None, None, :], scores, -1e30)
    peak = jnp.maximum(jnp.max(scores, axis=-1), fresh)
    expo = jnp.exp(scores - peak[..., None])
    expo_new = jnp.exp(fresh - peak)
    total = jnp.sum(expo, axis=-1) + expo_new
    probs = (expo / total[..., None]).astype(jnp.bfloat16)
    probs_new = (expo_new / total).astype(jnp.bfloat16)
    mixed = lax.optimization_barrier(
        jnp.einsum("rkgc,rckd->rkgd", probs, vals_b, preferred_element_type=jnp.float32)
    )
    mixed = (
        mixed + probs_new.astype(jnp.float32)[..., None] * newv_b.astype(jnp.float32)[:, :, None, :]
    )
    attended = mixed.reshape(rows, group * heads_kv * HD).astype(jnp.bfloat16)
    return (w_next, new_value, attended)


def solution(mesh):
    return jax.shard_map(
        per_device,
        mesh=mesh,
        in_specs=(
            P(("fsdp", "tp"), None),
            P(("fsdp", "tp"), None),
            P(("fsdp", "tp"), None),
            P(("fsdp", "tp"), None),
            P(),
            P("fsdp", "tp"),
            P("fsdp", None, "tp"),
            P("fsdp", None, "tp"),
            P("fsdp", "tp"),
            P("fsdp", "tp"),
            P("tp"),
            P("fsdp"),
        ),
        out_specs=(P(("fsdp", "tp"), None), P("fsdp", "tp"), P("fsdp", "tp")),
        check_vma=False,
    )
```

```python
import functools
import math

import jax
import jax.numpy as jnp
from jax import lax
from jax.experimental import pallas as pl
from jax.experimental.pallas import tpu as pltpu
from jax.sharding import PartitionSpec as P

HEADS = 64
KV = 8
HD = 128
LANES = 128
SLAB = 16
VMEM = 56 << 20
TOKEN = (8, 128)


def exchange(value, axis, mask):
    return lax.ppermute(value, axis, [(i, i ^ mask) for i in range(lax.axis_size(axis))])


def own_place():
    f = lax.axis_index("fsdp")
    return f & 1, f >> 1, lax.axis_index("tp")


def transpose_blocks(arranged, mine, units, source, out, wide, tall, arrived, left):
    core, upper, t = own_place()
    width = wide.shape[2]
    rows = width // units
    side = core if mine else 1 - core
    taken, given = [], []
    for j, r in enumerate(arranged):
        start = pl.multiple_of((((r ^ upper) << 1) | side) * width, LANES)
        copy = pltpu.make_async_copy(source.at[:, pl.ds(start, width)], wide.at[j], arrived.at[j])
        copy.start()
        taken.append(copy)
    for j in range(len(arranged)):
        taken[j].wait()
        for low in range(0, width, LANES):
            tall[j, low : low + LANES, :] = wide[j, :, low : low + LANES].T
        for unit in range(units):
            place = pl.multiple_of(j * width + (unit ^ t) * rows, 32)
            copy = pltpu.make_async_copy(
                tall.at[j, pl.ds(unit * rows, rows)],
                out.at[pl.ds(place, rows)],
                left.at[j * units + unit],
            )
            copy.start()
            given.append(copy)
    for copy in given:
        copy.wait()


def pack(activations, arranged, mine, units, width):
    tokens = activations.shape[0]
    count = len(arranged)
    rows = width // units
    if width % LANES or rows % 32:
        core, upper, t = own_place()
        side = core if mine else 1 - core
        flipped = activations.T
        return jnp.concatenate(
            [
                lax.dynamic_slice_in_dim(
                    flipped, (((r ^ upper) << 1) | side) * width + (unit ^ t) * rows, rows, 0
                )
                for r in arranged
                for unit in range(units)
            ]
        )
    kind = activations.dtype
    return pl.pallas_call(
        functools.partial(transpose_blocks, arranged, mine, units),
        in_specs=[pl.BlockSpec(memory_space=pltpu.HBM)],
        out_specs=pl.BlockSpec(memory_space=pltpu.HBM),
        out_shape=jax.ShapeDtypeStruct((count * width, tokens), kind),
        scratch_shapes=[
            pltpu.VMEM((count, tokens, width), kind),
            pltpu.VMEM((count, width, tokens), kind),
            pltpu.SemaphoreType.DMA((count,)),
            pltpu.SemaphoreType.DMA((count * units,)),
        ],
        compiler_params=pltpu.CompilerParams(vmem_limit_bytes=VMEM),
        cost_estimate=pl.CostEstimate(
            flops=0, bytes_accessed=4 * count * width * tokens, transcendentals=0
        ),
    )(activations)


def runs_of(units):
    runs = []
    for unit in units:
        if runs and runs[-1][1] == unit:
            runs[-1][1] = unit + 1
        else:
            runs.append([unit, unit + 1])
    return runs


def multiply(wanted, rows, blocks, base, tail, *refs):
    count = len(wanted)
    sources = refs[:4]
    if tail:
        appended, refs = refs[4:6], refs[:4] + refs[6:]
    outs = refs[4 : 4 + count]
    left, right, sems = refs[4 + count : 7 + count]
    tokens = left.shape[1] // 2
    per_block = left.shape[0] // blocks
    units_block = per_block // rows
    needed = [
        block
        for block in range(blocks)
        if any(unit // units_block == block for item in wanted for unit in item[0])
    ]
    columns = pl.ds(base, right.shape[1])
    halves = [pl.ds(0, tokens), pl.ds(tokens, tokens)]
    grads, lefts = [], {}
    for at, half in enumerate(halves):
        grads.append(
            pltpu.make_async_copy(sources[2 + at].at[:, columns], right.at[half], sems.at[at])
        )
        grads[at].start()
    for block in needed:
        span = pl.ds(block * per_block, per_block)
        for at, half in enumerate(halves):
            lefts[block, at] = pltpu.make_async_copy(
                sources[at].at[span], left.at[span, half], sems.at[2 + 2 * block + at]
            )
            lefts[block, at].start()
    if tail:
        addends, addend_sems = refs[-2:]
        for at in range(2):
            pltpu.make_async_copy(
                appended[at].at[pl.ds(tail, tail)], addends.at[at], addend_sems.at[at]
            ).start()
    if tail:
        for at in range(2):
            pltpu.make_async_copy(
                appended[at].at[pl.ds(tail, tail)], addends.at[at], addend_sems.at[at]
            ).wait()
        low = len(wanted[0][0]) * rows
        outs[0][low : low + tail, :] = addends[0] + addends[1]
    for copy in grads:
        copy.wait()
    for block in needed:
        for at in range(2):
            lefts[block, at].wait()
        for at, (units, first, last, _) in enumerate(wanted):
            here = [unit for unit in units if unit // units_block == block]
            for low, high in runs_of(here):
                place = units.index(low) * rows
                product = dot32(
                    left[low * rows : high * rows, :], right[:, first - base : last - base]
                )
                outs[at][place : place + (high - low) * rows, :] = product.astype(outs[at].dtype)


def products(lefts, grads, wanted, rows, blocks, appended=None):
    total, tokens = lefts[0].shape
    base = min(first for _, first, _, _ in wanted)
    columns = max(last for _, _, last, _ in wanted) - base
    if rows % 32 or any((first | last) % LANES for _, first, last, _ in wanted):
        results = [
            jnp.concatenate(
                [
                    sum(
                        dot32(left[low * rows : high * rows], grad[:, first:last])
                        for left, grad in zip(lefts, grads)
                    )
                    for low, high in runs_of(units)
                ]
            ).astype(kind)
            for units, first, last, kind in wanted
        ]
        if appended is not None:
            both = appended[0] + appended[1]
            results[0] = jnp.concatenate([results[0], both[both.shape[0] // 2 :]])
        return results
    tail = 0 if appended is None else appended[0].shape[0] // 2
    shapes = [
        jax.ShapeDtypeStruct((len(units) * rows, last - first), kind)
        for units, first, last, kind in wanted
    ]
    if tail:
        grown = (shapes[0].shape[0] + tail, shapes[0].shape[1])
        shapes[0] = jax.ShapeDtypeStruct(grown, shapes[0].dtype)
    staging = []
    if tail:
        staging.append(pltpu.VMEM((2, tail, shapes[0].shape[1]), shapes[0].dtype))
        staging.append(pltpu.SemaphoreType.DMA((2,)))
    return pl.pallas_call(
        functools.partial(multiply, wanted, rows, blocks, base, tail),
        out_shape=shapes,
        in_specs=[pl.BlockSpec(memory_space=pltpu.HBM)] * (6 if tail else 4),
        out_specs=[pl.BlockSpec(memory_space=pltpu.VMEM)] * len(shapes),
        scratch_shapes=[
            pltpu.VMEM((total, 2 * tokens), lefts[0].dtype),
            pltpu.VMEM((2 * tokens, columns), grads[0].dtype),
            pltpu.SemaphoreType.DMA((2 + 2 * blocks,)),
        ]
        + staging,
        compiler_params=pltpu.CompilerParams(vmem_limit_bytes=VMEM // 2),
        cost_estimate=pl.CostEstimate(flops=1, bytes_accessed=1, transcendentals=0),
    )(*lefts, *grads, *(appended or []))


def pick_rows(arranged, units, place, table, tail, *refs):
    outs, (slabs, found, flipped, sems) = refs[:2], refs[2:]
    whole = (table.shape[0] - 1) // SLAB * SLAB
    tokens, width_all = found.shape
    width = flipped.shape[0]
    rows = width // units
    lanes = outs[0].shape[1]
    lanes = lanes // 2
    folds = lanes // tokens
    lines = rows // folds

    def slab_copy(k):
        start = pl.multiple_of(lax.div(place[k], SLAB) * SLAB, SLAB)
        return pltpu.make_async_copy(table.at[pl.ds(start, SLAB)], slabs.at[k], sems.at[k])

    def add_row(k, held):
        at = lax.broadcasted_iota(jnp.int32, held.shape, 0)
        chosen = jnp.where(at == lax.rem(place[k], SLAB), held.astype(jnp.float32), 0.0)
        found[k : k + 1, :] = jnp.sum(chosen, axis=0, keepdims=True)

    for k in range(tokens):

        @pl.when((place[k] >= 0) & (place[k] < whole))
        def _():
            slab_copy(k).start()

    found[...] = jnp.zeros_like(found)
    for k in range(tokens):

        @pl.when(place[k] >= 0)
        def _():
            @pl.when(place[k] < whole)
            def _():
                slab_copy(k).wait()
                add_row(k, slabs[k])

            @pl.when(place[k] >= whole)
            def _():
                add_row(k, tail[...])

    core, upper, t = own_place()
    for side, out in zip((1 - core, core), outs):
        for j, r in enumerate(arranged):
            start = pl.multiple_of((((r ^ upper) << 1) | side) * width, LANES)
            flipped[...] = found[:, pl.ds(start, width)].T
            for unit in range(units):
                from_row = (unit ^ t) * rows
                pieces = [
                    flipped[pl.ds(pl.multiple_of(from_row + fold * lines, 8), lines), :]
                    for fold in range(folds)
                ]
                put = ((unit & 1) * len(arranged) + j) * lines
                side_lanes = slice((unit >> 1) * lanes, ((unit >> 1) + 1) * lanes)
                out[put : put + lines, side_lanes] = jnp.concatenate(pieces, axis=1).astype(
                    out.dtype
                )


def add_and_split(plans, arrays, merged, _, *refs):
    refs, done = list(refs[:-1]), refs[-1]
    done[...] = jnp.zeros_like(done)
    takes = [[refs.pop(0) for _ in plan] for plan in plans]
    inbox = [refs.pop(0) for _ in range(arrays)]
    gives = [[refs.pop(0) for _ in plan] for plan in plans]
    start = put = 0
    for at_plan, (plan, inputs, outputs) in enumerate(zip(plans, takes, gives)):
        got, sent = inbox[min(at_plan, arrays - 1)], refs[0 if merged else at_plan]
        if arrays > 1:
            start = 0
        if not merged:
            put = 0
        for (size, order, go, keep, have), value, kept in zip(plan, inputs, outputs):

            def sum_of(low, high):
                pieces = []
                for at in range(low, high):
                    place, lies = order[at]
                    pieces.append(
                        value[place * size : (place + 1) * size, :]
                        + got[start + lies * size : start + (lies + 1) * size, :].astype(
                            jnp.float32
                        )
                    )
                return pieces

            for at, piece in enumerate(sum_of(0, go)):
                sent[put + at * size : put + (at + 1) * size, :] = piece.astype(sent.dtype)
            for at, piece in enumerate(sum_of(go, go + keep)):
                kept[at * size : (at + 1) * size, :] = piece
            start += have * size
            put += go * size


def combine(plans, values, got, merged, after):
    columns = [parts[0].shape[1] for parts in values]
    totals = [sum(size * go for size, _, go, _, _ in plan) for plan in plans]
    outs = [
        jax.ShapeDtypeStruct((keep * size, width), jnp.float32)
        for plan, width in zip(plans, columns)
        for size, _, _, keep, _ in plan
    ]
    if merged:
        outs.append(jax.ShapeDtypeStruct((sum(totals), columns[0]), jnp.bfloat16))
    else:
        for total, width in zip(totals, columns):
            outs.append(jax.ShapeDtypeStruct((total, width), jnp.bfloat16))
    outs.append(jax.ShapeDtypeStruct(TOKEN, jnp.float32))
    arrays = [array for parts in values for array in parts] + list(got)
    results = pl.pallas_call(
        functools.partial(add_and_split, plans, len(got), merged),
        in_specs=[pl.BlockSpec(memory_space=pl.ANY)]
        + [pl.BlockSpec(memory_space=pltpu.VMEM)] * len(arrays),
        out_specs=[pl.BlockSpec(memory_space=pltpu.VMEM)] * len(outs),
        out_shape=outs,
        compiler_params=pltpu.CompilerParams(vmem_limit_bytes=VMEM // 4),
        cost_estimate=pl.CostEstimate(flops=1, bytes_accessed=1, transcendentals=0),
    )(after, *arrays)
    *results, done = results
    kept = [[results.pop(0) for _ in plan] for plan in plans]
    return kept, results, totals, done


def end_chunk(coef, spans, _, arrived, master, *refs):
    rows = master.shape[0]
    for at, (first, last) in enumerate(spans):
        value, out = refs[at], refs[len(spans) + at]
        grad = value[...] + arrived[at * rows : (at + 1) * rows, :].astype(jnp.float32)
        out[...] = master[:, first:last] - coef * grad


def finish(coef, spans, values, arrived, master_w, after):
    return pl.pallas_call(
        functools.partial(end_chunk, coef, spans),
        in_specs=[pl.BlockSpec(memory_space=pl.ANY)]
        + [pl.BlockSpec(memory_space=pltpu.VMEM)] * (2 + len(values)),
        out_specs=[pl.BlockSpec(memory_space=pltpu.VMEM)] * len(values),
        out_shape=[jax.ShapeDtypeStruct(value.shape, jnp.float32) for value in values],
        compiler_params=pltpu.CompilerParams(vmem_limit_bytes=VMEM // 4),
        cost_estimate=pl.CostEstimate(flops=1, bytes_accessed=1, transcendentals=0),
    )(after, arrived, master_w, *values)


def own_share(coef, spans, plans, rows, tokens, blocks, _, *refs):
    emb, master, out = refs[0], refs[1], refs[-1]
    arrays = refs[2:-1]
    lanes = emb.shape[1] // blocks
    count_fsdp = tokens // out.shape[1]
    col_width = out.shape[2]
    folded = emb[...].astype(jnp.bfloat16)
    lefts = [
        jnp.concatenate(
            [
                folded[:, unit * lanes + at : unit * lanes + at + tokens]
                for at in range(0, lanes, tokens)
            ]
        )
        for unit in range(blocks)
    ]

    def both(left, right):
        high = right.astype(jnp.bfloat16)
        total = across(left, high)
        if right.dtype == jnp.float32:
            total += across(left, (right - high.astype(jnp.float32)).astype(jnp.bfloat16))
        return total

    pieces = []
    for (first, last), plan in zip(spans, plans):
        moved = jnp.zeros((tokens, last - first), jnp.float32)
        for array, units in plan:
            for at, unit in enumerate(units):
                moved += both(lefts[unit], arrays[array][at * rows : (at + 1) * rows, :])
        pieces.append(both(lefts[0], master[:, first:last]) - coef * moved)
    share = jnp.concatenate(pieces, axis=1)
    for f in range(count_fsdp):
        for t in range(out.shape[0] // count_fsdp):
            out[f * (out.shape[0] // count_fsdp) + t] = share[
                f * out.shape[1] : (f + 1) * out.shape[1], t * col_width : (t + 1) * col_width
            ]


def across(left, right):
    return lax.dot_general(
        left, right, (((0,), (0,)), ((), ())), preferred_element_type=jnp.float32
    )


def fold_unit(part, lanes):
    rows, tokens = part.shape
    if tokens >= lanes:
        return jnp.concatenate([part[:, at : at + lanes] for at in range(0, tokens, lanes)])
    lines = rows * tokens // lanes
    return jnp.concatenate([part[at : at + lines] for at in range(0, rows, lines)], axis=1)


def unfold_unit(folded, rows):
    lines, lanes = folded.shape
    tokens = lines * lanes // rows
    if tokens >= lanes:
        return jnp.concatenate([folded[at : at + rows] for at in range(0, lines, rows)], axis=1)
    return jnp.concatenate([folded[:, at : at + tokens] for at in range(0, lanes, tokens)])


def lookup(embed_table, token_ids, arranged, units, width, lanes):
    here, width_all = embed_table.shape
    tokens = token_ids.shape[0]
    rows = width // units
    core, upper, t = own_place()
    inside = token_ids - (lax.axis_index("fsdp") * units + t) * here
    place = jnp.where((inside >= 0) & (inside < here), inside, -1).astype(jnp.int32)
    kind = embed_table.dtype
    if width % LANES or lanes % tokens or (rows * tokens // lanes) % 16:
        found = jnp.where(
            (place >= 0)[:, None], embed_table[jnp.maximum(place, 0)], jnp.zeros((), kind)
        )
        flipped = found.T

        def folded(r, side, unit):
            start = (((r ^ upper) << 1) | side) * width + (unit ^ t) * rows
            return fold_unit(lax.dynamic_slice_in_dim(flipped, start, rows, 0), lanes)

        return [
            jnp.concatenate(
                [
                    jnp.concatenate(
                        [folded(r, side, unit) for unit in range(low, units, 2)], axis=1
                    )
                    for low in range(2)
                    for r in arranged
                ]
            )
            for side in (1 - core, core)
        ]
    shape = jax.ShapeDtypeStruct((len(arranged) * width * tokens // lanes // 2, 2 * lanes), kind)
    return pl.pallas_call(
        functools.partial(pick_rows, arranged, units),
        grid=(1,),
        in_specs=[
            pl.BlockSpec(memory_space=pltpu.SMEM),
            pl.BlockSpec(memory_space=pltpu.HBM),
            pl.BlockSpec((SLAB, width_all), lambda i: ((here - 1) // SLAB, 0)),
        ],
        out_specs=[pl.BlockSpec(memory_space=pltpu.VMEM)] * 2,
        out_shape=[shape, shape],
        scratch_shapes=[
            pltpu.VMEM((tokens, SLAB, width_all), kind),
            pltpu.VMEM((tokens, width_all), jnp.float32),
            pltpu.VMEM((width, tokens), jnp.float32),
            pltpu.SemaphoreType.DMA((tokens,)),
        ],
        compiler_params=pltpu.CompilerParams(vmem_limit_bytes=VMEM // 2),
        cost_estimate=pl.CostEstimate(flops=1, bytes_accessed=1, transcendentals=0),
    )(place, embed_table, embed_table)


def dot32(left, right):
    return jnp.dot(left, right, preferred_element_type=jnp.float32)


def per_device(
    activations,
    grad_out,
    master_w,
    embed_table,
    token_ids,
    queries,
    cache_keys,
    cache_values,
    new_key,
    first_value,
    residual_mix,
    lengths,
):
    count_fsdp = lax.axis_size("fsdp")
    count_tp = lax.axis_size("tp")
    devices_all = count_fsdp * count_tp
    width = activations.shape[1]
    tokens_total = activations.shape[0] * devices_all
    coef = 1.0 / math.sqrt(tokens_total * width)
    upper_bits = count_fsdp.bit_length() - 2
    uppers = 1 << upper_bits

    block = width // count_fsdp
    rows = master_w.shape[0]
    columns = master_w.shape[1]
    arranged = [r ^ (r >> 1) for r in range(uppers)][::-1]
    grads = [grad_out, exchange(grad_out, "fsdp", 1)]
    incoming = exchange(pack(activations, arranged, False, count_tp, block), "fsdp", 1)
    staying = pack(activations, arranged, True, count_tp, block)
    lefts = [staying, incoming]
    tokens_new = token_ids.shape[0]
    quarter = columns // 4
    eighth = columns // 8
    lines = rows * tokens_new // eighth

    places = [(r, unit) for r in arranged for unit in range(count_tp)]
    steps_upper = [("fsdp", bit) for bit in range(upper_bits)]
    steps_tp = [("tp", bit) for bit in range(count_tp.bit_length() - 1)]
    one, two, three = (
        steps_upper + steps_tp,
        steps_upper[::-1] + steps_tp,
        steps_tp[:1] + steps_upper + steps_tp[1:],
    )
    edges = [0, quarter, 2 * quarter, 3 * quarter, 3 * quarter + eighth, columns]
    spans = list(zip(edges[:-1], edges[1:]))
    orders = [one, two, three, one, two]

    def has(place, step):
        return (place[step[0] == "tp"] >> step[1]) & 1

    def flip(place, step):
        mask = 1 << step[1]
        return (place[0], place[1] ^ mask) if step[0] == "tp" else (place[0] ^ mask, place[1])

    def split(held, step):
        return [p for p in held if has(p, step)], [p for p in held if not has(p, step)]

    def take(value, held, chosen, size):
        runs = runs_of([held.index(p) for p in chosen])
        return jnp.concatenate([value[low * size : high * size] for low, high in runs])

    def send(value, step):
        mask = 1 << step[1]
        return exchange(value, step[0], 2 * mask if step[0] == "fsdp" else mask)

    def compute(which, sent, appended=None):
        wanted = []
        for index in which:
            chosen = split(places, orders[index][0])[0 if sent else 1]
            units = [places.index(p) for p in chosen]
            kind = jnp.bfloat16 if sent else jnp.float32
            wanted.append((units, *spans[index], kind))
        return dict(zip(which, products(lefts, grads, wanted, rows, uppers, appended)))

    theirs, ours = lookup(embed_table, token_ids, arranged, count_tp, block, eighth)
    asked = [ours, exchange(theirs, "fsdp", 1)]
    pairs = [(r, low) for low in range(2) for r in arranged]
    going = compute([0, 1], True)
    got = {index: send(value, orders[index][0]) for index, value in going.items()}
    going |= compute([2, 3, 4], True, asked)
    got |= {index: send(going[index], orders[index][0]) for index in (3, 4, 2)}
    values = compute([0, 1, 2], False)
    values |= compute([3, 4], False)
    values = {index: [value] for index, value in values.items()}
    halves = [array[: array.shape[0] // 2].astype(jnp.float32) for array in asked]
    values[2].append(halves[0] + halves[1])
    sizes = {index: [rows] for index in range(5)}
    sizes[2].append(lines)
    held = {index: [split(places, orders[index][0])[1]] for index in range(5)}
    held[2].append(split(pairs, orders[2][0])[1])
    gone = {index: [split(places, orders[index][0])[0]] for index in range(5)}
    gone[2].append(split(pairs, orders[2][0])[0])

    def receive(index, step, arrived):
        start = 0
        for part, (value, size) in enumerate(zip(values[index], sizes[index])):
            landed = [flip(p, step) for p in gone[index][part]]
            piece = arrived[start : start + len(landed) * size]
            start += len(landed) * size
            if part and step == last_tp:
                piece = jnp.roll(piece, piece.shape[1] // 2, axis=1)
            else:
                piece = take(piece, landed, held[index][part], size)
            values[index][part] = value + piece.astype(jnp.float32)

    def onward(index, step):
        return [
            (places_now, places_now) if part and step == last_tp else split(places_now, step)
            for part, places_now in enumerate(held[index])
        ]

    def forward(index, step, following):
        plan = []
        for part, (go, keep) in enumerate(onward(index, following)):
            landed = [flip(p, step) for p in gone[index][part]]
            order = [(held[index][part].index(p), landed.index(p)) for p in go + keep]
            plan.append((sizes[index][part], order, len(go), len(keep), len(landed)))
        return plan

    last_tp = steps_tp[-1]
    rows_f = tokens_new // count_fsdp
    col_width = columns // count_tp

    def share_of(sums, emb, after):
        if plain:
            lefts_own = [
                unfold_unit(emb[:, at * eighth : (at + 1) * eighth], rows) for at in range(2)
            ]

            def exact(left, right):
                return lax.dot_general(
                    left.astype(jnp.float32),
                    right.astype(jnp.float32),
                    (((0,), (0,)), ((), ())),
                    precision=lax.Precision.HIGHEST,
                )

            pieces = []
            for index, (first, last) in enumerate(spans):
                moved = sum(exact(left, array) for left, array in zip(lefts_own, sums[index]))
                pieces.append(exact(lefts_own[0], master_w[:, first:last]) - coef * moved)
            out = jnp.concatenate(pieces, axis=1)
            out = out.reshape(count_fsdp, rows_f, count_tp, col_width)
            out = out.transpose(0, 2, 1, 3).reshape(devices_all, rows_f, col_width)
            return out.astype(jnp.bfloat16)
        arrays = [array for index in range(5) for array in sums[index]]
        plans = [[(2 * index, [0]), (2 * index + 1, [1])] for index in range(5)]
        return pl.pallas_call(
            functools.partial(own_share, coef, spans, plans, rows, tokens_new, 2),
            in_specs=[pl.BlockSpec(memory_space=pl.ANY)]
            + [pl.BlockSpec(memory_space=pltpu.VMEM)] * (2 + len(arrays)),
            out_specs=pl.BlockSpec(memory_space=pltpu.VMEM),
            out_shape=jax.ShapeDtypeStruct((devices_all, rows_f, col_width), jnp.float32),
            compiler_params=pltpu.CompilerParams(vmem_limit_bytes=VMEM // 4),
            cost_estimate=pl.CostEstimate(flops=1, bytes_accessed=1, transcendentals=0),
        )(after, emb, master_w, *arrays).astype(jnp.bfloat16)

    plain = rows % 32 or lines % 16 or block % LANES or eighth % tokens_new
    groups = ((0, 1), (2,), (3, 4))
    inbox = {group: [got[index] for index in group] for group in groups}
    totals = {}
    sums = {}
    steps = len(one)
    events = [(group, at) for at in range(steps) for group in groups]
    if steps == 4:
        first, second, third = groups
        events = [(first, 0), (second, 0), (third, 0), (first, 1), (second, 1), (third, 1)]
        events += [(second, 2), (first, 2), (third, 2), (second, 3), (first, 3), (third, 3)]
    ended = {}
    done = jnp.zeros(TOKEN, jnp.float32)
    for group, at in events:
        last = at + 1 == steps
        if last and not plain and group != (2,):
            ended |= dict(
                zip(
                    group,
                    finish(
                        coef,
                        [spans[index] for index in group],
                        [values[index][0] for index in group],
                        inbox[group][0],
                        master_w,
                        own_blocks,
                    ),
                )
            )
            continue
        if plain or last:
            if len(inbox[group]) < len(group):
                whole = inbox[group][0]
                cuts = [sum(totals[group][:place]) for place in range(len(group) + 1)]
                inbox[group] = [whole[low:high] for low, high in zip(cuts[:-1], cuts[1:])]
            for index, arrived in zip(group, inbox[group]):
                receive(index, orders[index][at], arrived)
        if last:
            if group == (2,):
                own_blocks = share_of(sums, values[2][1], done)
                parts_own = lax.all_to_all(
                    own_blocks, ("fsdp", "tp"), split_axis=0, concat_axis=0
                )
            continue
        if plain:
            outgoing = []
            for index in group:
                pieces = []
                for part, (go, keep) in enumerate(onward(index, orders[index][at + 1])):
                    value, size = values[index][part], sizes[index][part]
                    pieces.append(take(value, held[index][part], go, size))
                    values[index][part] = take(value, held[index][part], keep, size)
                outgoing.append(jnp.concatenate(pieces).astype(jnp.bfloat16))
            totals[group] = [value.shape[0] for value in outgoing]
            merged = False
        else:
            plans = [forward(i, orders[i][at], orders[i][at + 1]) for i in group]
            merged = len({orders[i][at + 1] for i in group}) == 1
            kept, outgoing, totals[group], done = combine(
                plans, [values[i] for i in group], inbox[group], merged, done
            )
            values |= dict(zip(group, kept))
        for number, index in enumerate(group):
            now = onward(index, orders[index][at + 1])
            gone[index], held[index] = [list(parts) for parts in zip(*now)]
            if at + 2 == steps:
                low = sum(totals[group][:number]) if merged else 0
                sent = outgoing[0 if merged else number]
                sums[index] = [values[index][0], sent[low : low + rows]]
        inbox[group] = [
            send(value, orders[index][at + 1]) for index, value in zip(group, outgoing)
        ]
        if at == 1 and group == groups[0]:
            queries, new_key, lengths, outgoing[0] = lax.optimization_barrier(
                (queries, new_key, lengths, outgoing[0])
            )
    own_value = jnp.sum(parts_own.astype(jnp.float32), axis=0)
    w_next = jnp.concatenate(
        [
            ended[at] if at in ended else master_w[:, low:high] - coef * values[at][0]
            for at, (low, high) in enumerate(spans)
        ],
        axis=1,
    )

    share = jnp.repeat(residual_mix, HD)[None, :]
    new_value = (share * own_value + (1.0 - share) * first_value.astype(jnp.float32)).astype(
        jnp.bfloat16
    )
    rows = queries.shape[0]
    heads_kv = residual_mix.shape[0]
    group = HEADS // KV
    context = cache_keys.shape[1]
    scale = 1.0 / math.sqrt(HD)
    query_b = queries.reshape(rows, heads_kv, group, HD)
    keys_b = cache_keys.reshape(rows, context, heads_kv, HD)
    vals_b = cache_values.reshape(rows, context, heads_kv, HD)
    newk_b = new_key.reshape(rows, heads_kv, HD)
    newv_b = new_value.reshape(rows, heads_kv, HD)
    scores = (
        jnp.einsum("rkgd,rckd->rkgc", query_b, keys_b, preferred_element_type=jnp.float32) * scale
    )
    fresh = jnp.einsum("rkgd,rkd->rkg", query_b, newk_b, preferred_element_type=jnp.float32) * scale
    valid = jnp.arange(context, dtype=jnp.int32)[None, :] < lengths[:, None]
    scores = jnp.where(valid[:, None, None, :], scores, -1e30)
    peak = jnp.maximum(jnp.max(scores, axis=-1), fresh)
    expo = jnp.exp(scores - peak[..., None])
    expo_new = jnp.exp(fresh - peak)
    total = jnp.sum(expo, axis=-1) + expo_new
    probs = (expo / total[..., None]).astype(jnp.bfloat16)
    probs_new = (expo_new / total).astype(jnp.bfloat16)
    mixed = lax.optimization_barrier(
        jnp.einsum("rkgc,rckd->rkgd", probs, vals_b, preferred_element_type=jnp.float32)
    )
    mixed = (
        mixed + probs_new.astype(jnp.float32)[..., None] * newv_b.astype(jnp.float32)[:, :, None, :]
    )
    attended = mixed.reshape(rows, group * heads_kv * HD).astype(jnp.bfloat16)
    return (w_next, new_value, attended)


def solution(mesh):
    return jax.shard_map(
        per_device,
        mesh=mesh,
        in_specs=(
            P(("fsdp", "tp"), None),
            P(("fsdp", "tp"), None),
            P(("fsdp", "tp"), None),
            P(("fsdp", "tp"), None),
            P(),
            P("fsdp", "tp"),
            P("fsdp", None, "tp"),
            P("fsdp", None, "tp"),
            P("fsdp", "tp"),
            P("fsdp", "tp"),
            P("tp"),
            P("fsdp"),
        ),
        out_specs=(P(("fsdp", "tp"), None), P("fsdp", "tp"), P("fsdp", "tp")),
        check_vma=False,
    )
```
